128 devices in a mesh: wide: 8 (over y, core), narrow: 16 (over z, x).
Axes of the slice: x: 4, y: 4, z: 4, core: 2. Of those that a mesh axis runs over, the one named last changes fastest.
Arguments:
- positions: float32 [3, 1048576], P(None, ('wide', 'narrow')), may hold values from 0 to 1
- masses: float32 [1048576], P(('wide', 'narrow')), may hold values from 0.001 to 0.01
- node_mass: float32 [32768], P(('wide', 'narrow')), may hold values from 0.01 to 0.1
- node_centre: float32 [3, 32768], P(None, ('wide', 'narrow')), may hold values from 0 to 1
- node_quad: float32 [6, 32768], P(None, ('wide', 'narrow')), may hold values from -0.018 to 0.018
- local_leaves: int32 [8192, 8], P(('wide', 'narrow')), may hold values from 0 to 63
- node_lists: int32 [8192, 64], P(('wide', 'narrow')), may hold values from 0 to 32767
- export_block: int32 [16384], P(('wide', 'narrow')), may hold values from 0 to 63
- export_dest: int32 [16384, 1], P(('wide', 'narrow')), may hold values from 0 to 127; in each aligned block of 128 rows (0 to 127, 128 to 255, ...) at most 2 rows name the same one
- export_leaves: int32 [16384, 8], P(('wide', 'narrow')), may hold values from 0 to 63
Outputs:
- accel: float32 [3, 1048576], P(None, ('wide', 'narrow'))
The draws below stay inside these ranges and needn't reach their ends.
Inputs may be any that keep to these rules, and one draw needn't show every extreme that they name: `export_dest`: in the exports of one device no destination appears more than 2 times, and some destination appears exactly 2 times.
All inputs are finite; a program needn't handle non-finite values.
Results may differ from the reference program's by a relative error of at most 0.00014.
Values sent between devices are 32-bit elements; how exact they have to be, the bound alone decides.
No kernel may reach another device: no remote copies, remote signals or barrier semaphores. Data moves between devices by JAX's collectives and lax.ppermute only.
A program may use at most 128 MiB of HBM per device.

```python
import math
import jax
import jax.numpy as jnp
import numpy as np
from jax import lax

ROWS = 128
BLK_DEV = 64
LEAF_N = 8
LIST_N = 64
CAP = 2
EXP_BLK = 128
NPART = 1048576
NBLOCKS = 8192
NODES = 32768
EXPORTS = 16384
DEVICES = 128


def set_ends(array, rng, least, largest):
    longest = array.shape.index(max(array.shape))
    spots = []
    for shift in (0, 1):
        where = [jax.random.randint(jax.random.fold_in(rng, axis), (), 0, length) for axis, length in enumerate(array.shape)]
        where[longest] = (where[longest] + shift) % array.shape[longest]
        spots.append(tuple(where))
    return array.at[spots[0]].set(least).at[spots[1]].set(largest)


def level_of(stream_key, dims, cuts, least, top_value):
    def one(position, shards_of):
        heights = jax.random.uniform(jax.random.fold_in(jax.random.fold_in(stream_key, 6), position), (shards_of,), jnp.float32, least / len(cuts), top_value / len(cuts))
        return jnp.repeat(jnp.exp(heights), dims[position] // shards_of).reshape((-1,) + (1,) * (len(dims) - position - 1))

    gain = one(*cuts[0])
    for cut in cuts[1:]:
        gain = gain * one(*cut)
    return gain


def deal_out(key, own, number, rows, amount, top, limit, slope):
    sequence = jax.random.permutation(key, amount)
    crowded, common = portions_of(amount, rows * top, limit, slope, True), portions_of(amount, rows * top, limit, slope, False)
    places = jnp.arange(amount)

    def named(lengths, offset_by):
        used = int((lengths > 0).sum())
        fixed = max(1, used // 4)
        shifted = fixed + (places - fixed + offset_by * (used - fixed)) % max(1, amount - fixed)
        return jnp.zeros((amount,), jnp.int32).at[sequence[jnp.where(places < fixed, places, shifted)]].set(jnp.asarray(lengths, jnp.int32))

    lengths = jnp.where(number % 4 == 0, named(crowded, number // 4), named(common, number - number // 4 - 1))
    mixed = jax.random.permutation(jax.random.fold_in(own, 3), amount)
    giver, receiver = mixed[0:amount // 2 * 2:2], mixed[1:amount // 2 * 2:2]
    margin = jnp.minimum(lengths[giver] - 1, limit - lengths[receiver]) // 2
    margin = jnp.where((giver == sequence[0]) | (receiver == sequence[0]) | (lengths[receiver] == 0), 0, jnp.maximum(margin, 0))
    shifted = jax.random.randint(jax.random.fold_in(own, 4), (amount // 2,), 0, 1 << 20) % (margin + 1)
    lengths = lengths.at[giver].add(-shifted).at[receiver].add(shifted)
    members = jnp.searchsorted(jnp.cumsum(lengths), jnp.arange(rows * top), side="right").astype(jnp.int32)
    table = members.reshape(top, rows).T
    table = table[jax.random.permutation(jax.random.fold_in(own, 1), rows)]
    offset_by = jax.random.randint(jax.random.fold_in(own, 2), (rows, 1), 0, top)
    return jnp.take_along_axis(table, (jnp.arange(top)[None, :] + offset_by) % top, axis=1)


def portions_of(number_of, total, limit, lean, full):
    portions = [(1 << 20) // math.isqrt(rank ** lean) + 1 for rank in range(1, number_of + 1)]
    largest = limit if full else min(limit, max(-(-total // number_of), total * portions[0] // sum(portions)))
    least = 1 if total - largest >= number_of - 1 else 0
    given, spare = [largest] + [least] * (number_of - 1), total - largest - least * (number_of - 1)
    while spare > 0:
        movable = [i for i in range(1, number_of) if given[i] < largest] or [i for i in range(1, number_of) if given[i] < limit]
        mass, left = sum([portions[i] for i in movable]), spare
        for i in movable:
            more = min(limit - given[i], max(1, left * portions[i] // mass), spare)
            given[i] = given[i] + more
            spare = spare - more
    return np.array(given)


def normal_values(key, extent, deviation, limit, pieces=(), held_as=jnp.bfloat16):
    result = jax.random.normal(key, extent, jnp.float32) * deviation
    if len(pieces) > 0:
        result = level_of(key, extent, pieces, -0.22, 0.18) * result
    return jnp.clip(result, min=-limit, max=limit).astype(held_as)


def setup_inputs(seed: int = 0) -> dict:
    splits = jax.random.split(jax.random.key(seed), 11)
    positions = jnp.clip(1.0 * jax.random.uniform(splits[0], (3, NPART), jnp.float32) ** level_of(splits[0], (3, NPART), ((1, 128),), -0.2, 0.2), 0.0, 1.0)
    masses = jnp.clip(jnp.exp(math.log(0.01) - 2.30258502 * jax.random.uniform(splits[1], (NPART,), jnp.float32) ** level_of(splits[1], (NPART,), ((0, 128),), -0.2, 0.2)), 0.001, 0.01)
    node_mass = jnp.clip(jnp.exp(math.log(0.1) - 2.3025851 * jax.random.uniform(splits[2], (NODES,), jnp.float32) ** level_of(splits[2], (NODES,), ((0, 128),), -0.2, 0.2)), 0.01, 0.1)
    node_centre = jnp.clip(1.0 * jax.random.uniform(splits[3], (3, NODES), jnp.float32) ** level_of(splits[3], (3, NODES), ((1, 128),), -0.2, 0.2), 0.0, 1.0)
    node_quad = normal_values(splits[4], (6, NODES), 0.003, 0.018, ((1, 128),), jnp.float32)
    local_leaves = set_ends(jax.random.randint(splits[5], (NBLOCKS, LEAF_N), 0, BLK_DEV), jax.random.fold_in(splits[5], 1), 0, BLK_DEV - 1).astype(jnp.int32)
    node_lists = set_ends(jax.random.randint(splits[6], (NBLOCKS, LIST_N), 0, NODES), jax.random.fold_in(splits[6], 1), 0, NODES - 1).astype(jnp.int32)
    export_block = set_ends(jax.random.randint(splits[7], (EXPORTS,), 0, BLK_DEV), jax.random.fold_in(splits[7], 1), 0, BLK_DEV - 1).astype(jnp.int32)
    export_dest_keys = jax.random.split(jax.random.fold_in(splits[8], 1), EXPORTS // EXP_BLK)
    export_dest_turns = jax.random.permutation(jax.random.fold_in(splits[8], 3), EXPORTS // EXP_BLK)
    export_dest = jax.vmap(lambda own, number: deal_out(jax.random.fold_in(splits[8], 2), own, number, EXP_BLK, DEVICES, 1, CAP, 2))(export_dest_keys, export_dest_turns).reshape((EXPORTS, 1))
    export_leaves = set_ends(jax.random.randint(splits[9], (EXPORTS, LEAF_N), 0, BLK_DEV), jax.random.fold_in(splits[9], 1), 0, BLK_DEV - 1).astype(jnp.int32)
    return dict(positions=positions, masses=masses, node_mass=node_mass, node_centre=node_centre, node_quad=node_quad, local_leaves=local_leaves, node_lists=node_lists, export_block=export_block, export_dest=export_dest, export_leaves=export_leaves)


soften_sq = 0.01

def pair_pull(target, sources, source_mass):
    delta = sources[:, :, None, :] - target[None, :, :, None]
    spread = lax.optimization_barrier(jnp.sum(delta * delta, axis=1)) + soften_sq
    factor = source_mass[:, None, :] / (spread * jnp.sqrt(spread))
    return lax.optimization_barrier(jnp.sum(delta * factor[:, None, :, :], axis=(0, 3)))

def node_pull(target, mass_list, centre_list, quad_list):
    relative = target[:, None, :] - centre_list[:, :, None]
    along_x = relative[0]
    along_y = relative[1]
    along_z = relative[2]
    spread = along_x * along_x + along_y * along_y + along_z * along_z + soften_sq
    quads = quad_list[:, :, None]
    quad_x = quads[0] * along_x + quads[3] * along_y + quads[4] * along_z
    quad_y = quads[3] * along_x + quads[1] * along_y + quads[5] * along_z
    quad_z = quads[4] * along_x + quads[5] * along_y + quads[2] * along_z
    inverse = 1.0 / spread
    cubed = inverse * jnp.sqrt(inverse)
    scalar = along_x * quad_x + along_y * quad_y + along_z * quad_z
    radial = -mass_list[:, None] * cubed - 2.5 * scalar * cubed * inverse * inverse
    quad_vec = jnp.stack([quad_x, quad_y, quad_z])
    total = radial[None] * relative + quad_vec * (cubed * inverse)[None]
    return lax.optimization_barrier(jnp.sum(total, axis=1))

def reference(positions, masses, node_mass, node_centre, node_quad, local_leaves, node_lists, export_block, export_dest, export_leaves):
    block_count = masses.shape[0] // ROWS
    blocks = positions.reshape(3, block_count, ROWS).transpose(1, 0, 2)
    block_mass = masses.reshape(block_count, ROWS)
    owner = jnp.arange(block_count, dtype=jnp.int32) // BLK_DEV
    leaf_global = (owner[:, None] * BLK_DEV + local_leaves).astype(jnp.int32)

    def local_term(packed):
        places, leaf_ids, node_ids = packed
        direct = pair_pull(places, blocks[leaf_ids], block_mass[leaf_ids])
        return direct + node_pull(places, node_mass[node_ids], node_centre[:, node_ids], node_quad[:, node_ids])
    local = lax.map(local_term, (blocks, leaf_global, node_lists), batch_size=64)
    export_count = export_block.shape[0]
    source_ids = (jnp.arange(export_count, dtype=jnp.int32) // EXP_BLK * BLK_DEV + export_block).astype(jnp.int32)
    remote_ids = (export_dest[:, 0][:, None] * BLK_DEV + export_leaves).astype(jnp.int32)

    def remote_term(packed):
        source_id, leaf_ids = packed
        return pair_pull(blocks[source_id], blocks[leaf_ids], block_mass[leaf_ids])
    remote = lax.map(remote_term, (source_ids, remote_ids), batch_size=64)
    total = local + jax.ops.segment_sum(remote, source_ids, num_segments=block_count)
    return total.transpose(1, 0, 2).reshape(3, block_count * ROWS)
```

```python
import functools

import jax
import jax.numpy as jnp
from jax import lax
from jax.experimental import pallas as pl
from jax.experimental.pallas import tpu as pltpu
from jax.sharding import PartitionSpec as P

ROWS = 128
LEAF_N = 8
LIST_N = 64
CAP = 2
BLK_DEV = 64
EXP_BLK = 128
AXES = ("wide", "narrow")
GROUP = 4
STEP = 8
NODE_FIELDS = 10
NODES_ROW = 12
SOFTEN = 0.01

f32 = jnp.float32
bf16 = jnp.bfloat16
VMEM = pl.BlockSpec(memory_space=pltpu.VMEM)
SMEM = pl.BlockSpec(memory_space=pltpu.SMEM)
ANY = pl.BlockSpec(memory_space=pl.ANY)


def params(mib):
    return pltpu.CompilerParams(vmem_limit_bytes=mib * 2**20)


def split3(value):
    high = value.astype(bf16)
    rest = value - high.astype(f32)
    middle = rest.astype(bf16)
    low = (rest - middle.astype(f32)).astype(bf16)
    return high, middle, low


def dot(left, right):
    return jnp.dot(left, right, preferred_element_type=f32)


def send_kernel(place_ref, block_ref, dest_ref, pos_ref, leaf_ref, out_ref, slot_ref, count_ref):
    devices = out_ref.shape[0]
    members = place_ref[0]
    out_ref[:, :, 3:4, :] = jnp.full((devices, CAP, 1, ROWS), -1.0, f32)

    def clear(index, carry):
        count_ref[index] = 0
        return carry

    lax.fori_loop(0, devices, clear, 0)

    def one(export, carry):
        dest = dest_ref[export]
        owner = ((dest // members) % 2) * 2 + dest % 2
        base = dest - ((dest // members) % 2) * members - dest % 2
        seen = count_ref[base]
        count_ref[base] = seen + 1
        member = (seen + place_ref[1]) % GROUP
        slot = seen // GROUP
        target = base + (member // 2) * members + member % 2
        distance = owner ^ member
        slot_ref[export] = target * CAP + slot
        start = pl.multiple_of(block_ref[export] * ROWS, ROWS)
        out_ref[target, slot, 0:3, :] = pos_ref[:, pl.ds(start, ROWS)]
        ids = leaf_ref[pl.ds(export, 1), :] + distance * BLK_DEV
        out_ref[target, slot, 3:4, 0:LEAF_N] = ids.astype(f32)
        return carry

    lax.fori_loop(0, EXP_BLK, one, 0)


def send_blocks(place, export_block, export_dest, positions, export_leaves, devices):
    return pl.pallas_call(
        send_kernel,
        out_shape=(
            jax.ShapeDtypeStruct((devices, CAP, 4, ROWS), f32),
            jax.ShapeDtypeStruct((EXP_BLK,), jnp.int32),
        ),
        in_specs=[SMEM, SMEM, SMEM, VMEM, VMEM],
        out_specs=(VMEM, SMEM),
        scratch_shapes=[pltpu.SMEM((devices,), jnp.int32)],
        compiler_params=params(16),
        name="send_blocks",
    )(place, export_block, export_dest, positions, export_leaves)


def centred_rows(position, centre):
    moved = position - centre
    square = jnp.sum(moved * moved, axis=0, keepdims=True)
    one = jnp.ones_like(square)
    return moved, square, one, jnp.zeros((3,) + square.shape[1:], f32)


def source_kernel(centre_ref, pm_ref, table_ref, weight_ref):
    count = table_ref.shape[0]
    for leaf in range(count):
        window = pm_ref[0, :, leaf * ROWS : (leaf + 1) * ROWS]
        moved, square, one, zero = centred_rows(window[0:3], centre_ref[...])
        row = jnp.concatenate([-2.0 * moved, one, square, zero], axis=0)
        high, middle, low = [part.astype(f32) for part in split3(row)]
        blank = jnp.zeros((16, ROWS), f32)
        half = [high, high, middle, middle, high, low, blank]
        table_ref[leaf] = jnp.concatenate(half + half, axis=0).T.astype(bf16)
        pulled = jnp.concatenate([moved, one, zero, zero[0:1]], axis=0) * window[3:4]
        high, middle, _ = split3(pulled)
        weight_ref[leaf] = jnp.concatenate([high, middle], axis=0)


def source_tables(centre, pm):
    groups = pm.shape[0]
    chunk = 8
    steps = BLK_DEV // chunk
    return pl.pallas_call(
        source_kernel,
        grid=(groups, steps),
        out_shape=(
            jax.ShapeDtypeStruct((groups * BLK_DEV, ROWS, 128), bf16),
            jax.ShapeDtypeStruct((groups * BLK_DEV, 16, ROWS), bf16),
        ),
        in_specs=[
            pl.BlockSpec((3, 1), lambda g, i: (0, 0)),
            pl.BlockSpec((1, 4, chunk * ROWS), lambda g, i: (g, 0, i)),
        ],
        out_specs=(
            pl.BlockSpec((chunk, ROWS, 128), lambda g, i: (g * steps + i, 0, 0)),
            pl.BlockSpec((chunk, 16, ROWS), lambda g, i: (g * steps + i, 0, 0)),
        ),
        compiler_params=params(16),
        name="source_tables",
    )(centre, pm)


def pull_block(position, centre, leaves, table_ref, weight_ref, left):
    moved, square, one, zero = centred_rows(position, centre)
    row = jnp.concatenate([moved, square + SOFTEN, one, zero], axis=0)
    high, middle, low = split3(row)
    blank = jnp.zeros((16, ROWS), bf16)
    half = jnp.concatenate([high, middle, high, middle, low, high, blank], axis=0)
    none = jnp.zeros_like(half)
    right = jnp.concatenate(
        [jnp.concatenate([half, none], axis=1), jnp.concatenate([none, half], axis=1)], axis=0
    )
    total = jnp.zeros((16, ROWS), f32)
    for pair in range(LEAF_N // 2):
        first, second = leaves[2 * pair], leaves[2 * pair + 1]
        spread = dot(jnp.where(left, table_ref[first], table_ref[second]), right)
        root = lax.rsqrt(spread)
        cubed = root * root * root
        high = cubed.astype(bf16)
        low = (cubed - high.astype(f32)).astype(bf16)
        for place, leaf in enumerate((first, second)):
            lanes = slice(place * ROWS, (place + 1) * ROWS)
            weight = weight_ref[leaf]
            total += dot(
                jnp.concatenate([weight, weight], axis=1),
                jnp.concatenate([high[:, lanes], low[:, lanes]], axis=0),
            )
    total = total[0:8] + total[8:16]
    return total[0:3] - moved * total[3:4]


def left_lanes():
    return lax.broadcasted_iota(jnp.int32, (ROWS, 128), 1) < 64


def local_kernel(leaf_ref, centre_ref, pos_ref, table_ref, weight_ref, out_ref):
    left = left_lanes()

    def step(index, carry):
        results = []
        for place in range(STEP):
            block = index * STEP + place
            start = pl.multiple_of(block * ROWS, ROWS)
            leaves = [leaf_ref[block * LEAF_N + k] for k in range(LEAF_N)]
            results.append(
                pull_block(
                    pos_ref[:, pl.ds(start, ROWS)], centre_ref[...], leaves, table_ref, weight_ref, left
                )
            )
        for place in range(STEP):
            out_ref[index * STEP + place, 0:3] = results[place]
        return carry

    lax.fori_loop(0, BLK_DEV // STEP, step, 0)


def local_pull(local_leaves, centre, positions, table, weight):
    return pl.pallas_call(
        local_kernel,
        out_shape=jax.ShapeDtypeStruct((BLK_DEV, 4, ROWS), f32),
        in_specs=[SMEM, VMEM, VMEM, VMEM, VMEM],
        out_specs=VMEM,
        compiler_params=params(24),
        cost_estimate=pl.CostEstimate(flops=16 * 10**9, bytes_accessed=10**6, transcendentals=8 * 10**6),
        name="local_pull",
    )(local_leaves, centre, positions, table, weight)


def remote_kernel(
    leaf_ref, centre_ref, pos_ref, own_ref, own_weight_ref, other_ref, other_weight_ref,
    out_ref, table_ref, weight_ref, list_ref, sems,
):
    copies = [
        pltpu.make_async_copy(own_ref, table_ref.at[pl.ds(0, BLK_DEV)], sems.at[0]),
        pltpu.make_async_copy(own_weight_ref, weight_ref.at[pl.ds(0, BLK_DEV)], sems.at[1]),
        pltpu.make_async_copy(other_ref, table_ref.at[pl.ds(BLK_DEV, (GROUP - 1) * BLK_DEV)], sems.at[2]),
        pltpu.make_async_copy(
            other_weight_ref, weight_ref.at[pl.ds(BLK_DEV, (GROUP - 1) * BLK_DEV)], sems.at[3]
        ),
    ]
    for copy in copies:
        copy.start()
    slots = pos_ref.shape[0]

    def note(slot, found):
        list_ref[found] = slot
        return found + (leaf_ref[slot * LEAF_N] >= 0).astype(jnp.int32)

    found = lax.fori_loop(0, slots, note, 0)
    last = list_ref[jnp.maximum(found - 1, 0)]
    for place in range(STEP):
        list_ref[found + place] = last
    for copy in copies:
        copy.wait()
    left = left_lanes()

    def step(index, carry):
        results = []
        for place in range(STEP):
            slot = list_ref[index * STEP + place]
            leaves = [leaf_ref[slot * LEAF_N + k] for k in range(LEAF_N)]
            results.append(
                (slot, pull_block(pos_ref[slot][0:3], centre_ref[...], leaves, table_ref, weight_ref, left))
            )
        for slot, result in results:
            out_ref[slot, 0:3] = result
        return carry

    lax.fori_loop(0, (found + STEP - 1) // STEP, step, 0)


def remote_pull(leaves, centre, visitors, own, own_weight, other, other_weight):
    slots = visitors.shape[0]
    return pl.pallas_call(
        remote_kernel,
        out_shape=jax.ShapeDtypeStruct((slots, 4, ROWS), f32),
        in_specs=[SMEM, VMEM, VMEM, ANY, ANY, ANY, ANY],
        out_specs=VMEM,
        scratch_shapes=[
            pltpu.VMEM((GROUP * BLK_DEV, ROWS, 128), bf16),
            pltpu.VMEM((GROUP * BLK_DEV, 16, ROWS), bf16),
            pltpu.SMEM((slots + STEP,), jnp.int32),
            pltpu.SemaphoreType.DMA((4,)),
        ],
        compiler_params=params(32),
        cost_estimate=pl.CostEstimate(flops=32 * 10**9, bytes_accessed=10**7, transcendentals=16 * 10**6),
        name="remote_pull",
    )(leaves, centre, visitors, own, own_weight, other, other_weight)


def node_kernel(row_ref, pos_ref, field_ref, table_ref, local_ref, out_ref, picked_ref):
    def step(block, carry):
        start = pl.multiple_of(block * ROWS, ROWS)
        place = pos_ref[:, pl.ds(start, ROWS)]
        for node in range(LIST_N):
            picked_ref[pl.ds(node, 1), :] = table_ref[pl.ds(row_ref[block * LIST_N + node], 1), :]
        column = jnp.full((LIST_N, 128), block, jnp.int32)
        base = jnp.take_along_axis(field_ref[...], column, axis=1, mode="promise_in_bounds")
        picked = picked_ref[...]

        def field(number):
            return jnp.take_along_axis(picked, base + number, axis=1, mode="promise_in_bounds")

        mass, cx, cy, cz = field(0), field(1), field(2), field(3)
        qxx, qyy, qzz, qxy, qxz, qyz = [field(number) for number in range(4, 10)]
        x, y, z = place[0:1] - cx, place[1:2] - cy, place[2:3] - cz
        spread = x * x + y * y + z * z + SOFTEN
        quad_x = qxx * x + qxy * y + qxz * z
        quad_y = qxy * x + qyy * y + qyz * z
        quad_z = qxz * x + qyz * y + qzz * z
        root = lax.rsqrt(spread)
        inverse = root * root
        cubed = inverse * root
        fifth = cubed * inverse
        scalar = x * quad_x + y * quad_y + z * quad_z
        radial = -mass * cubed - 2.5 * scalar * (fifth * inverse)
        total = [
            jnp.sum(radial * x + quad_x * fifth, axis=0, keepdims=True),
            jnp.sum(radial * y + quad_y * fifth, axis=0, keepdims=True),
            jnp.sum(radial * z + quad_z * fifth, axis=0, keepdims=True),
        ]
        out_ref[block, 0:3] = local_ref[block, 0:3] + jnp.concatenate(total, axis=0)
        return carry

    lax.fori_loop(0, BLK_DEV, step, 0)


def node_pull(rows, positions, fields, table, local):
    return pl.pallas_call(
        node_kernel,
        out_shape=jax.ShapeDtypeStruct(local.shape, f32),
        in_specs=[SMEM, VMEM, VMEM, VMEM, VMEM],
        out_specs=VMEM,
        scratch_shapes=[pltpu.VMEM((LIST_N, 128), f32)],
        compiler_params=params(24),
        cost_estimate=pl.CostEstimate(flops=4 * 10**9, bytes_accessed=2 * 10**6, transcendentals=10**6),
        name="node_pull",
    )(rows, positions, fields, table, local)


def add_kernel(slot_ref, block_ref, local_ref, back_ref, out_ref):
    for block in range(BLK_DEV):
        out_ref[:, block * ROWS : (block + 1) * ROWS] = local_ref[block, 0:3]

    def one(export, carry):
        start = pl.multiple_of(block_ref[export] * ROWS, ROWS)
        out_ref[:, pl.ds(start, ROWS)] += back_ref[slot_ref[export]][0:3]
        return carry

    lax.fori_loop(0, EXP_BLK, one, 0)


def add_returned(slots, export_block, local, back):
    return pl.pallas_call(
        add_kernel,
        out_shape=jax.ShapeDtypeStruct((3, BLK_DEV * ROWS), f32),
        in_specs=[SMEM, SMEM, VMEM, VMEM],
        out_specs=VMEM,
        compiler_params=params(16),
        name="add_returned",
    )(slots, export_block, local, back)


def swap(values):
    return lax.all_to_all(values, AXES, split_axis=0, concat_axis=0, tiled=True)


def node_table(node_mass, node_centre, node_quad, devices):
    count = node_mass.shape[0]
    rows = -(-count // NODES_ROW)
    padded = -(-rows // 8) * 8
    fields = jnp.concatenate([node_mass[None], node_centre, node_quad], axis=0).T
    fields = jnp.pad(fields, ((0, rows * NODES_ROW - count), (0, 0)))
    fields = fields.reshape(rows, NODES_ROW * NODE_FIELDS)
    fields = jnp.pad(fields, ((0, padded - rows), (0, 128 - NODES_ROW * NODE_FIELDS)))
    return swap(jnp.broadcast_to(fields[None], (devices, padded, 128))).reshape(devices * padded, 128)


def per_device(
    positions,
    masses,
    node_mass,
    node_centre,
    node_quad,
    local_leaves,
    node_lists,
    export_block,
    export_dest,
    export_leaves,
):
    groups = lax.axis_size("wide")
    members = lax.axis_size("narrow")
    devices = groups * members
    wide = lax.axis_index("wide")
    narrow = lax.axis_index("narrow")
    count = node_mass.shape[0]

    place = jnp.stack([jnp.int32(members), (wide // 2 + narrow // 2 + narrow).astype(jnp.int32)])
    outgoing, slots = send_blocks(
        place, export_block, export_dest[:, 0], positions, export_leaves, devices
    )
    arrived = swap(outgoing)

    pm = jnp.concatenate([positions, masses[None]], axis=0)
    centre = jnp.mean(positions, axis=1, keepdims=True)
    near = [(i, i ^ 1) for i in range(members)]
    pair = [(i, i ^ 1) for i in range(groups)]
    by_narrow = lax.ppermute(pm, "narrow", near)
    by_wide = lax.ppermute(pm, "wide", pair)
    by_both = lax.ppermute(by_narrow, "wide", pair)
    own, own_weight = source_tables(centre, pm[None])
    local = local_pull(local_leaves.reshape(-1), centre, positions, own, own_weight)
    other, other_weight = source_tables(centre, jnp.stack([by_narrow, by_wide, by_both]))
    table = node_table(node_mass, node_centre, node_quad, devices)

    visitors = arrived.reshape(devices * CAP, 4, ROWS)
    visitor_leaves = visitors[:, 3, 0:LEAF_N].astype(jnp.int32).reshape(-1)
    pulls = remote_pull(visitor_leaves, centre, visitors, own, own_weight, other, other_weight)
    back = swap(pulls.reshape(devices, CAP, 4, ROWS))

    inner = node_lists % count
    table_rows = table.shape[0] // devices
    rows = (node_lists // count) * table_rows + inner // NODES_ROW
    fields = jnp.pad((inner % NODES_ROW * NODE_FIELDS).T, ((0, 0), (0, 128 - BLK_DEV)))
    local = node_pull(rows.reshape(-1), positions, fields, table, local)
    return add_returned(slots, export_block, local, back.reshape(devices * CAP, 4, ROWS))


def solution(mesh):
    both = P(AXES)
    lanes = P(None, AXES)
    rows = P(AXES, None)
    return jax.shard_map(
        per_device,
        mesh=mesh,
        in_specs=(lanes, both, both, lanes, lanes, rows, rows, both, rows, rows),
        out_specs=lanes,
        check_vma=False,
    )
```

```python
import functools

import jax
import jax.numpy as jnp
from jax import lax
from jax.experimental import pallas as pl
from jax.experimental.pallas import tpu as pltpu
from jax.sharding import PartitionSpec as P

ROWS = 128
LEAF_N = 8
LIST_N = 64
CAP = 2
BLK_DEV = 64
EXP_BLK = 128
AXES = ("wide", "narrow")
GROUP = 4
STEP = 8
NODE_FIELDS = 10
SOFTEN = 0.01

f32 = jnp.float32
bf16 = jnp.bfloat16
VMEM = pl.BlockSpec(memory_space=pltpu.VMEM)
SMEM = pl.BlockSpec(memory_space=pltpu.SMEM)


def params(mib):
    return pltpu.CompilerParams(vmem_limit_bytes=mib * 2**20)


def split3(value):
    high = value.astype(bf16)
    rest = value - high.astype(f32)
    middle = rest.astype(bf16)
    low = (rest - middle.astype(f32)).astype(bf16)
    return high, middle, low


def dot(left, right):
    return jnp.dot(left, right, preferred_element_type=f32)


def send_kernel(place_ref, block_ref, dest_ref, leaf_ref, pos_ref, mass_ref, out_ref, slot_ref, pm_ref, count_ref, ids_ref):
    devices = out_ref.shape[0]
    members, shift, turn = place_ref[0], place_ref[1], place_ref[2]
    pm_ref[0:3] = pos_ref[...]
    pm_ref[3:4] = mass_ref[...]
    out_ref[:, :, 3:4, :] = jnp.full((devices, CAP, 1, ROWS), -1.0, f32)
    ids_ref[...] = jnp.concatenate([leaf_ref[...].astype(f32)] * (ROWS // LEAF_N), axis=0).T

    def clear(index, carry):
        for part in range(8):
            count_ref[index * 8 + part] = 0
        return carry

    lax.fori_loop(0, devices // 8, clear, 0)

    def one(step, carry):
        for part in range(8):
            export = step * 8 + part
            dest = dest_ref[export]
            side, across = dest & 1, (dest >> shift) & 1
            base = dest - side - across * members
            seen = count_ref[base]
            count_ref[base] = seen + 1
            member = (seen + turn) & (GROUP - 1)
            slot = seen >> 2
            target = base + (member >> 1) * members + (member & 1)
            distance = (across * 2 + side) ^ member
            slot_ref[export] = target * CAP + slot
            start = pl.multiple_of(block_ref[export] * ROWS, ROWS)
            out_ref[target, slot, 0:3, :] = pos_ref[:, pl.ds(start, ROWS)]
            ids = ids_ref[pl.ds(export, 1), 0:LEAF_N]
            out_ref[target, slot, 3:4, 0:LEAF_N] = ids + (distance * BLK_DEV).astype(f32)
        return carry

    lax.fori_loop(0, EXP_BLK // 8, one, 0)


def send_blocks(place, export_block, export_dest, export_leaves, positions, masses, devices):
    return pl.pallas_call(
        send_kernel,
        out_shape=(
            jax.ShapeDtypeStruct((devices, CAP, 4, ROWS), f32),
            jax.ShapeDtypeStruct((EXP_BLK,), jnp.int32),
            jax.ShapeDtypeStruct((4, BLK_DEV * ROWS), f32),
        ),
        in_specs=[SMEM, SMEM, SMEM, VMEM, VMEM, VMEM],
        out_specs=(VMEM, SMEM, VMEM),
        scratch_shapes=[pltpu.SMEM((devices,), jnp.int32), pltpu.VMEM((EXP_BLK, 128), f32)],
        compiler_params=params(16),
        name="send_blocks",
    )(place, export_block, export_dest, export_leaves, positions, masses)


def node_rows_kernel(mass_ref, centre_ref, quad_ref, list_ref, out_ref, row_ref, lane_ref):
    devices, rows = out_ref.shape[0], out_ref.shape[1]
    count = mass_ref.shape[1]
    fields = jnp.concatenate(
        [mass_ref[...], centre_ref[...], quad_ref[...], jnp.zeros((16 - NODE_FIELDS, count), f32)], axis=0
    )
    parts = [fields[:, part * rows : (part + 1) * rows] for part in range(8)]
    table = jnp.concatenate(parts, axis=0).T
    out_ref[...] = jnp.broadcast_to(table[None], out_ref.shape)
    nodes = list_ref[...]
    bits = rows.bit_length() - 1
    row_ref[...] = ((nodes >> (bits + 3)) << bits) + (nodes & (rows - 1))
    lanes = ((nodes >> bits) & 7) * 16
    wide = jnp.concatenate([lanes, jnp.zeros_like(lanes)], axis=1)
    wide = jnp.concatenate([wide, jnp.zeros_like(wide)], axis=0)
    lane_ref[...] = wide.T[0:LIST_N]


def node_rows(node_mass, node_centre, node_quad, node_lists, devices):
    count = node_mass.shape[1]
    return pl.pallas_call(
        node_rows_kernel,
        out_shape=(
            jax.ShapeDtypeStruct((devices, count // 8, 128), f32),
            jax.ShapeDtypeStruct((BLK_DEV, LIST_N), jnp.int32),
            jax.ShapeDtypeStruct((LIST_N, 128), jnp.int32),
        ),
        in_specs=[VMEM] * 4,
        out_specs=(VMEM,) * 3,
        compiler_params=params(16),
        name="node_rows",
    )(node_mass, node_centre, node_quad, node_lists)


def centred_rows(position, centre):
    moved = position - centre
    square = jnp.sum(moved * moved, axis=0, keepdims=True)
    one = jnp.ones_like(square)
    return moved, square, one, jnp.zeros((3,) + square.shape[1:], f32)


def source_kernel(pm0_ref, pm1_ref, pm2_ref, pm3_ref, table_ref, weight_ref, centre_ref):
    size = BLK_DEV * ROWS
    centre = jnp.sum(pm0_ref[0:3], axis=1, keepdims=True) * (1.0 / size)
    centre_ref[...] = jnp.broadcast_to(centre, (3, ROWS))
    chunk = 8

    def step(index, carry):
        start = pl.multiple_of(index * (chunk * ROWS), chunk * ROWS)
        for group, pm_ref in enumerate((pm0_ref, pm1_ref, pm2_ref, pm3_ref)):
            rows = pm_ref[:, pl.ds(start, chunk * ROWS)]
            for part in range(chunk):
                window = rows[:, part * ROWS : (part + 1) * ROWS]
                leaf = group * BLK_DEV + index * chunk + part
                moved, square, one, zero = centred_rows(window[0:3], centre)
                row = jnp.concatenate([-2.0 * moved, one, square, zero], axis=0)
                high, middle, low = [piece.astype(f32) for piece in split3(row)]
                blank = jnp.zeros((16, ROWS), f32)
                half = [high, high, middle, middle, high, low, blank]
                table_ref[leaf] = jnp.concatenate(half + half, axis=0).T.astype(bf16)
                pulled = jnp.concatenate([moved, one, zero, zero[0:1]], axis=0) * window[3:4]
                high, middle, _ = split3(pulled)
                weight_ref[leaf] = jnp.concatenate([high, middle], axis=0)
        return carry

    lax.fori_loop(0, BLK_DEV // chunk, step, 0)


def source_tables(pms):
    return pl.pallas_call(
        source_kernel,
        out_shape=(
            jax.ShapeDtypeStruct((GROUP * BLK_DEV, ROWS, 128), bf16),
            jax.ShapeDtypeStruct((GROUP * BLK_DEV, 16, ROWS), bf16),
            jax.ShapeDtypeStruct((3, ROWS), f32),
        ),
        in_specs=[VMEM] * 4,
        out_specs=(VMEM,) * 3,
        compiler_params=params(32),
        name="source_tables",
    )(*pms)


def pull_block(position, centre, leaves, table_ref, weight_ref, left):
    moved, square, one, zero = centred_rows(position, centre)
    row = jnp.concatenate([moved, square + SOFTEN, one, zero], axis=0)
    high, middle, low = split3(row)
    blank = jnp.zeros((16, ROWS), bf16)
    half = jnp.concatenate([high, middle, high, middle, low, high, blank], axis=0)
    none = jnp.zeros_like(half)
    right = jnp.concatenate(
        [jnp.concatenate([half, none], axis=1), jnp.concatenate([none, half], axis=1)], axis=0
    )
    total = jnp.zeros((16, ROWS), f32)
    for pair in range(LEAF_N // 2):
        first, second = leaves[2 * pair], leaves[2 * pair + 1]
        spread = dot(jnp.where(left, table_ref[first], table_ref[second]), right)
        root = lax.rsqrt(spread)
        cubed = root * root * root
        high = cubed.astype(bf16)
        low = (cubed - high.astype(f32)).astype(bf16)
        for place, leaf in enumerate((first, second)):
            lanes = slice(place * ROWS, (place + 1) * ROWS)
            weight = weight_ref[leaf]
            total += dot(
                jnp.concatenate([weight, weight], axis=1),
                jnp.concatenate([high[:, lanes], low[:, lanes]], axis=0),
            )
    total = total[0:8] + total[8:16]
    return total[0:3] - moved * total[3:4]


def left_lanes():
    return lax.broadcasted_iota(jnp.int32, (ROWS, 128), 1) < 64


def local_kernel(leaf_ref, centre_ref, pos_ref, table_ref, weight_ref, out_ref):
    left = left_lanes()

    def step(index, carry):
        results = []
        for place in range(STEP):
            block = index * STEP + place
            start = pl.multiple_of(block * ROWS, ROWS)
            leaves = [leaf_ref[k, block] for k in range(LEAF_N)]
            results.append(
                pull_block(
                    pos_ref[:, pl.ds(start, ROWS)], centre_ref[...], leaves, table_ref, weight_ref, left
                )
            )
        for place in range(STEP):
            out_ref[index * STEP + place, 0:3] = results[place]
        return carry

    lax.fori_loop(0, BLK_DEV // STEP, step, 0)


def local_pull(local_leaves, centre, positions, table, weight):
    return pl.pallas_call(
        local_kernel,
        out_shape=jax.ShapeDtypeStruct((BLK_DEV, 4, ROWS), f32),
        in_specs=[SMEM, VMEM, VMEM, VMEM, VMEM],
        out_specs=VMEM,
        compiler_params=params(32),
        cost_estimate=pl.CostEstimate(flops=16 * 10**9, bytes_accessed=10**6, transcendentals=8 * 10**6),
        name="local_pull",
    )(local_leaves, centre, positions, table, weight)


def remote_kernel(leaf_ref, centre_ref, pos_ref, table_ref, weight_ref, out_ref, list_ref):
    slots = pos_ref.shape[0]

    def note(slot, found):
        list_ref[found] = slot
        return found + (leaf_ref[slot * LEAF_N] >= 0).astype(jnp.int32)

    found = lax.fori_loop(0, slots, note, 0)
    last = list_ref[jnp.maximum(found - 1, 0)]
    for place in range(STEP):
        list_ref[found + place] = last
    left = left_lanes()

    def step(index, carry):
        results = []
        for place in range(STEP):
            slot = list_ref[index * STEP + place]
            leaves = [leaf_ref[slot * LEAF_N + k] for k in range(LEAF_N)]
            results.append(
                (slot, pull_block(pos_ref[slot][0:3], centre_ref[...], leaves, table_ref, weight_ref, left))
            )
        for slot, result in results:
            out_ref[slot, 0:3] = result
        return carry

    lax.fori_loop(0, (found + STEP - 1) // STEP, step, 0)


def remote_pull(leaves, centre, visitors, table, weight):
    slots = visitors.shape[0]
    return pl.pallas_call(
        remote_kernel,
        out_shape=jax.ShapeDtypeStruct((slots, 4, ROWS), f32),
        in_specs=[SMEM, VMEM, VMEM, VMEM, VMEM],
        out_specs=VMEM,
        scratch_shapes=[pltpu.SMEM((slots + STEP,), jnp.int32)],
        compiler_params=params(32),
        cost_estimate=pl.CostEstimate(flops=32 * 10**9, bytes_accessed=10**7, transcendentals=16 * 10**6),
        name="remote_pull",
    )(leaves, centre, visitors, table, weight)


def pick_lanes(values, lanes):
    numbers = lax.GatherDimensionNumbers(
        offset_dims=(),
        collapsed_slice_dims=(1,),
        start_index_map=(1,),
        operand_batching_dims=(0,),
        start_indices_batching_dims=(0,),
    )
    return lax.gather(
        values, lanes[..., None], numbers, (1, 1), mode=lax.GatherScatterMode.PROMISE_IN_BOUNDS
    )


def node_sum(place, fields):
    mass, cx, cy, cz, qxx, qyy, qzz, qxy, qxz, qyz = fields
    x, y, z = place[0:1] - cx, place[1:2] - cy, place[2:3] - cz
    spread = x * x + y * y + z * z + SOFTEN
    quad_x = qxx * x + qxy * y + qxz * z
    quad_y = qxy * x + qyy * y + qyz * z
    quad_z = qxz * x + qyz * y + qzz * z
    root = lax.rsqrt(spread)
    inverse = root * root
    cubed = inverse * root
    fifth = cubed * inverse
    scalar = x * quad_x + y * quad_y + z * quad_z
    radial = -mass * cubed - 2.5 * scalar * (fifth * inverse)
    total = [
        jnp.sum(radial * along + quad * fifth, axis=0, keepdims=True)
        for along, quad in ((x, quad_x), (y, quad_y), (z, quad_z))
    ]
    return jnp.concatenate(total, axis=0)


NODE_STEP = 4


def node_kernel(row_ref, pos_ref, lane_ref, table_ref, out_ref, *picked_refs):
    shape = (LIST_N, 128)
    along = lax.broadcasted_iota(jnp.int32, shape, 1)

    def step(index, carry):
        for part in range(NODE_STEP):
            for node in range(LIST_N):
                row = row_ref[index * NODE_STEP + part, node]
                picked_refs[part][pl.ds(node, 1), :] = table_ref[pl.ds(row, 1), :]
        results = []
        for part in range(NODE_STEP):
            block = index * NODE_STEP + part
            start = pl.multiple_of(block * ROWS, ROWS)
            first = pick_lanes(lane_ref[...], jnp.full(shape, block, jnp.int32))
            picked = pick_lanes(picked_refs[part][...], (first + along) & 127)
            fields = [jnp.broadcast_to(picked[:, k : k + 1], shape) for k in range(NODE_FIELDS)]
            results.append(node_sum(pos_ref[:, pl.ds(start, ROWS)], fields))
        for part in range(NODE_STEP):
            out_ref[index * NODE_STEP + part, 0:3] = results[part]
        return carry

    lax.fori_loop(0, BLK_DEV // NODE_STEP, step, 0)


def node_pull(rows, positions, lanes, table):
    return pl.pallas_call(
        node_kernel,
        out_shape=jax.ShapeDtypeStruct((BLK_DEV, 4, ROWS), f32),
        in_specs=[SMEM, VMEM, VMEM, VMEM],
        out_specs=VMEM,
        scratch_shapes=[pltpu.VMEM((LIST_N, 128), f32)] * NODE_STEP,
        compiler_params=params(24),
        cost_estimate=pl.CostEstimate(flops=4 * 10**9, bytes_accessed=2 * 10**6, transcendentals=10**6),
        name="node_pull",
    )(rows, positions, lanes, table)


def add_kernel(slot_ref, block_ref, local_ref, node_ref, back_ref, out_ref, *sum_refs):
    parts = len(sum_refs)
    for part in range(1, parts):
        sum_refs[part][...] = jnp.zeros_like(sum_refs[part])
    sum_refs[0][...] = local_ref[...] + node_ref[...]

    def one(step, carry):
        for part in range(parts):
            export = step * parts + part
            block = block_ref[export]
            sum_refs[part][block] += back_ref[slot_ref[export]]
        return carry

    lax.fori_loop(0, EXP_BLK // parts, one, 0)
    for block in range(BLK_DEV):
        total = sum_refs[0][block]
        for part in range(1, parts):
            total = total + sum_refs[part][block]
        out_ref[:, block * ROWS : (block + 1) * ROWS] = total[0:3]


def add_returned(slots, export_block, local, node, back):
    return pl.pallas_call(
        add_kernel,
        out_shape=jax.ShapeDtypeStruct((3, BLK_DEV * ROWS), f32),
        in_specs=[SMEM, SMEM, VMEM, VMEM, VMEM],
        out_specs=VMEM,
        scratch_shapes=[pltpu.VMEM((BLK_DEV, 4, ROWS), f32)] * 4,
        compiler_params=params(16),
        name="add_returned",
    )(slots, export_block, local, node, back)


def swap(values):
    return lax.all_to_all(values, AXES, split_axis=0, concat_axis=0, tiled=True)


def per_device(
    positions,
    masses,
    node_mass,
    node_centre,
    node_quad,
    local_leaves,
    node_lists,
    export_block,
    export_dest,
    export_leaves,
):
    groups = lax.axis_size("wide")
    members = lax.axis_size("narrow")
    devices = groups * members
    wide = lax.axis_index("wide")
    narrow = lax.axis_index("narrow")

    place = jnp.stack(
        [
            jnp.int32(members),
            jnp.int32(members.bit_length() - 1),
            (wide + narrow + (narrow >> 1)).astype(jnp.int32),
        ]
    )
    outgoing, slots, pm = send_blocks(
        place, export_block, export_dest[:, 0], export_leaves.T, positions, masses[None], devices
    )
    arrived = swap(outgoing)

    near = [(i, i ^ 1) for i in range(members)]
    pair = [(i, i ^ 1) for i in range(groups)]
    by_narrow = lax.ppermute(pm, "narrow", near)
    by_wide = lax.ppermute(pm, "wide", pair)
    by_both = lax.ppermute(by_narrow, "wide", pair)
    fields, rows, lanes = node_rows(node_mass[None], node_centre, node_quad, node_lists, devices)
    table = swap(fields).reshape(-1, 128)

    sources, weights, centre = source_tables((pm, by_narrow, by_wide, by_both))
    visitors = arrived.reshape(devices * CAP, 4, ROWS)
    visitor_leaves = visitors[:, 3, 0:LEAF_N].astype(jnp.int32).reshape(-1)
    pulls = remote_pull(visitor_leaves, centre, visitors, sources, weights)
    pulls, leaves = lax.optimization_barrier((pulls, local_leaves.T))
    back = swap(pulls.reshape(devices, CAP, 4, ROWS))
    local = local_pull(leaves, centre, positions, sources, weights)
    node = node_pull(rows, positions, lanes, table)
    return add_returned(slots, export_block, local, node, back.reshape(devices * CAP, 4, ROWS))


def solution(mesh):
    both = P(AXES)
    lanes = P(None, AXES)
    rows = P(AXES, None)
    return jax.shard_map(
        per_device,
        mesh=mesh,
        in_specs=(lanes, both, both, lanes, lanes, rows, rows, both, rows, rows),
        out_specs=lanes,
        check_vma=False,
    )
```

```python
import functools

import jax
import jax.numpy as jnp
from jax import lax
from jax.experimental import pallas as pl
from jax.experimental.pallas import tpu as pltpu
from jax.sharding import PartitionSpec as P

ROWS = 128
LEAF_N = 8
LIST_N = 64
CAP = 2
BLK_DEV = 64
EXP_BLK = 128
AXES = ("wide", "narrow")
GROUP = 4
STEP = 8
NODE_FIELDS = 10
SOFTEN = 0.01

f32 = jnp.float32
bf16 = jnp.bfloat16
VMEM = pl.BlockSpec(memory_space=pltpu.VMEM)
SMEM = pl.BlockSpec(memory_space=pltpu.SMEM)
HBM = pl.BlockSpec(memory_space=pltpu.HBM)


def params(mib):
    return pltpu.CompilerParams(vmem_limit_bytes=mib * 2**20)


def split3(value):
    high = value.astype(bf16)
    rest = value - high.astype(f32)
    middle = rest.astype(bf16)
    low = (rest - middle.astype(f32)).astype(bf16)
    return high, middle, low


def dot(left, right):
    return jnp.dot(left, right, preferred_element_type=f32)


def fetch(sources, targets, sems):
    copies = [
        pltpu.make_async_copy(source, target, sems.at[number])
        for number, (source, target) in enumerate(zip(sources, targets))
    ]
    for copy in copies:
        copy.start()
    return copies


def send_kernel(
    place_ref, block_in, dest_in, leaf_in, pos_in, mass_in, out_ref, slot_ref, pm_ref,
    block_ref, dest_ref, leaf_ref, pos_ref, mass_ref, count_ref, ids_ref, sems,
):
    copies = fetch(
        (block_in, dest_in, leaf_in, pos_in, mass_in),
        (block_ref, dest_ref, leaf_ref, pos_ref, mass_ref),
        sems,
    )
    devices = out_ref.shape[0]
    members, shift, turn = place_ref[0], place_ref[1], place_ref[2]
    out_ref[:, :, 3:4, :] = jnp.full((devices, CAP, 1, ROWS), -1.0, f32)

    def clear(index, carry):
        for part in range(8):
            count_ref[index * 8 + part] = 0
        return carry

    lax.fori_loop(0, devices // 8, clear, 0)
    for copy in copies:
        copy.wait()
    pm_ref[0:3] = pos_ref[...]
    pm_ref[3:4] = mass_ref[...]
    ids_ref[...] = jnp.concatenate([leaf_ref[...].astype(f32)] * (ROWS // LEAF_N), axis=0).T

    def one(step, carry):
        for part in range(8):
            export = step * 8 + part
            dest = dest_ref[export]
            side, across = dest & 1, (dest >> shift) & 1
            base = dest - side - across * members
            seen = count_ref[base]
            count_ref[base] = seen + 1
            member = (seen + turn) & (GROUP - 1)
            slot = seen >> 2
            target = base + (member >> 1) * members + (member & 1)
            distance = (across * 2 + side) ^ member
            slot_ref[export] = target * CAP + slot
            start = pl.multiple_of(block_ref[export] * ROWS, ROWS)
            out_ref[target, slot, 0:3, :] = pos_ref[:, pl.ds(start, ROWS)]
            ids = ids_ref[pl.ds(export, 1), 0:LEAF_N]
            out_ref[target, slot, 3:4, 0:LEAF_N] = ids + (distance * BLK_DEV).astype(f32)
        return carry

    lax.fori_loop(0, EXP_BLK // 8, one, 0)


def send_blocks(place, export_block, export_dest, export_leaves, positions, masses, devices):
    return pl.pallas_call(
        send_kernel,
        out_shape=(
            jax.ShapeDtypeStruct((devices, CAP, 4, ROWS), f32),
            jax.ShapeDtypeStruct((EXP_BLK,), jnp.int32),
            jax.ShapeDtypeStruct((4, BLK_DEV * ROWS), f32),
        ),
        in_specs=[SMEM] + [HBM] * 5,
        out_specs=(VMEM, SMEM, VMEM),
        scratch_shapes=[
            pltpu.SMEM((EXP_BLK,), jnp.int32),
            pltpu.SMEM((EXP_BLK,), jnp.int32),
            pltpu.VMEM((LEAF_N, EXP_BLK), jnp.int32),
            pltpu.VMEM(positions.shape, f32),
            pltpu.VMEM(masses.shape, f32),
            pltpu.SMEM((devices,), jnp.int32),
            pltpu.VMEM((EXP_BLK, 128), f32),
            pltpu.SemaphoreType.DMA((5,)),
        ],
        compiler_params=params(16),
        name="send_blocks",
    )(place, export_block, export_dest, export_leaves, positions, masses)


def node_rows_kernel(
    mass_in, centre_in, quad_in, list_in, out_ref, row_ref, part_ref, mass_ref, centre_ref, quad_ref, list_ref, sems
):
    copies = fetch(
        (mass_in, centre_in, quad_in, list_in), (mass_ref, centre_ref, quad_ref, list_ref), sems
    )
    for copy in copies:
        copy.wait()
    rows = out_ref.shape[1]
    count = mass_ref.shape[1]
    fields = jnp.concatenate(
        [mass_ref[...], centre_ref[...], quad_ref[...], jnp.zeros((16 - NODE_FIELDS, count), f32)], axis=0
    )
    parts = [fields[:, part * rows : (part + 1) * rows] for part in range(8)]
    table = jnp.concatenate(parts, axis=0).T
    out_ref[...] = jnp.broadcast_to(table[None], out_ref.shape)
    half = BLK_DEV // 2
    nodes = list_ref[...]
    nodes = jnp.concatenate([nodes[0:half], nodes[half:]], axis=1)
    bits = rows.bit_length() - 1
    row_ref[...] = ((nodes >> (bits + 3)) << bits) + (nodes & (rows - 1))
    part_ref[...] = (nodes >> bits) & 7


def node_rows(node_mass, node_centre, node_quad, node_lists, devices):
    count = node_mass.shape[1]
    arguments = (node_mass, node_centre, node_quad, node_lists)
    return pl.pallas_call(
        node_rows_kernel,
        out_shape=(
            jax.ShapeDtypeStruct((devices, count // 8, 128), f32),
            jax.ShapeDtypeStruct((BLK_DEV // 2, 2 * LIST_N), jnp.int32),
            jax.ShapeDtypeStruct((BLK_DEV // 2, 2 * LIST_N), jnp.int32),
        ),
        in_specs=[HBM] * 4,
        out_specs=(VMEM,) * 3,
        scratch_shapes=[pltpu.VMEM(value.shape, value.dtype) for value in arguments]
        + [pltpu.SemaphoreType.DMA((4,))],
        compiler_params=params(16),
        name="node_rows",
    )(*arguments)


def centred_rows(position, centre):
    moved = position - centre
    square = jnp.sum(moved * moved, axis=0, keepdims=True)
    one = jnp.ones_like(square)
    return moved, square, one, jnp.zeros((3,) + square.shape[1:], f32)


def mean_position(pm_ref):
    return jnp.sum(pm_ref[0:3], axis=1, keepdims=True) * (1.0 / pm_ref.shape[1])


def fill_tables(pm_refs, centre, table_ref, weight_ref):
    chunk = 8

    def step(index, carry):
        start = pl.multiple_of(index * (chunk * ROWS), chunk * ROWS)
        for group, pm_ref in enumerate(pm_refs):
            rows = pm_ref[:, pl.ds(start, chunk * ROWS)]
            for part in range(chunk):
                window = rows[:, part * ROWS : (part + 1) * ROWS]
                leaf = group * BLK_DEV + index * chunk + part
                moved, square, one, zero = centred_rows(window[0:3], centre)
                row = jnp.concatenate([-2.0 * moved, one, square, zero], axis=0)
                high, middle, low = [piece.astype(f32) for piece in split3(row)]
                blank = jnp.zeros((16, ROWS), f32)
                half = [high, high, middle, middle, high, low, blank]
                table_ref[leaf] = jnp.concatenate(half + half, axis=0).T.astype(bf16)
                pulled = jnp.concatenate([moved, one, zero, zero[0:1]], axis=0) * window[3:4]
                high, middle, _ = split3(pulled)
                weight_ref[leaf] = jnp.concatenate([high, middle], axis=0)
        return carry

    lax.fori_loop(0, BLK_DEV // chunk, step, 0)


def pull_block(position, centre, leaves, table_ref, weight_ref, left):
    moved, square, one, zero = centred_rows(position, centre)
    row = jnp.concatenate([moved, square + SOFTEN, one, zero], axis=0)
    high, middle, low = split3(row)
    blank = jnp.zeros((16, ROWS), bf16)
    half = jnp.concatenate([high, middle, high, middle, low, high, blank], axis=0)
    none = jnp.zeros_like(half)
    right = jnp.concatenate(
        [jnp.concatenate([half, none], axis=1), jnp.concatenate([none, half], axis=1)], axis=0
    )
    total = jnp.zeros((16, ROWS), f32)
    for pair in range(LEAF_N // 2):
        first, second = leaves[2 * pair], leaves[2 * pair + 1]
        spread = dot(jnp.where(left, table_ref[first], table_ref[second]), right)
        root = lax.rsqrt(spread)
        cubed = root * root * root
        high = cubed.astype(bf16)
        low = (cubed - high.astype(f32)).astype(bf16)
        for place, leaf in enumerate((first, second)):
            lanes = slice(place * ROWS, (place + 1) * ROWS)
            weight = weight_ref[leaf]
            total += dot(
                jnp.concatenate([weight, weight], axis=1),
                jnp.concatenate([high[:, lanes], low[:, lanes]], axis=0),
            )
    total = total[0:8] + total[8:16]
    return total[0:3] - moved * total[3:4]


def left_lanes():
    return lax.broadcasted_iota(jnp.int32, (ROWS, 128), 1) < 64


def remote_kernel(
    leaf_ref, pos_ref, pm0_ref, pm1_ref, pm2_ref, pm3_ref, out_ref, list_ref, table_ref, weight_ref
):
    slots = pos_ref.shape[0]

    def note(slot, found):
        list_ref[found] = slot
        return found + (leaf_ref[slot * LEAF_N] >= 0).astype(jnp.int32)

    found = lax.fori_loop(0, slots, note, 0)
    last = list_ref[jnp.maximum(found - 1, 0)]
    for place in range(STEP):
        list_ref[found + place] = last
    centre = mean_position(pm0_ref)
    fill_tables((pm0_ref, pm1_ref, pm2_ref, pm3_ref), centre, table_ref, weight_ref)
    left = left_lanes()

    def step(index, carry):
        results = []
        for place in range(STEP):
            slot = list_ref[index * STEP + place]
            leaves = [leaf_ref[slot * LEAF_N + k] for k in range(LEAF_N)]
            results.append((slot, pull_block(pos_ref[slot][0:3], centre, leaves, table_ref, weight_ref, left)))
        for slot, result in results:
            out_ref[slot, 0:3] = result
        return carry

    lax.fori_loop(0, (found + STEP - 1) // STEP, step, 0)


def remote_pull(leaves, visitors, pms):
    slots = visitors.shape[0]
    return pl.pallas_call(
        remote_kernel,
        out_shape=jax.ShapeDtypeStruct((slots, 4, ROWS), f32),
        in_specs=[SMEM] + [VMEM] * 5,
        out_specs=VMEM,
        scratch_shapes=[
            pltpu.SMEM((slots + STEP,), jnp.int32),
            pltpu.VMEM((GROUP * BLK_DEV, ROWS, 128), bf16),
            pltpu.VMEM((GROUP * BLK_DEV, 16, ROWS), bf16),
        ],
        compiler_params=params(32),
        cost_estimate=pl.CostEstimate(flops=32 * 10**9, bytes_accessed=10**7, transcendentals=16 * 10**6),
        name="remote_pull",
    )(leaves, visitors, *pms)


def node_sum(place, fields):
    mass, cx, cy, cz, qxx, qyy, qzz, qxy, qxz, qyz = fields
    x, y, z = place[0] - cx, place[1] - cy, place[2] - cz
    spread = x * x + y * y + z * z + SOFTEN
    quad_x = qxx * x + qxy * y + qxz * z
    quad_y = qxy * x + qyy * y + qyz * z
    quad_z = qxz * x + qyz * y + qzz * z
    root = lax.rsqrt(spread)
    inverse = root * root
    cubed = inverse * root
    fifth = cubed * inverse
    scalar = x * quad_x + y * quad_y + z * quad_z
    radial = -mass * cubed - 2.5 * scalar * (fifth * inverse)
    return radial * x + quad_x * fifth, radial * y + quad_y * fifth, radial * z + quad_z * fifth


def node_pair(block, centre, table_ref, part_ref, picked, left, spread_ref, gather_ref):
    turned = picked.T
    part = part_ref[pl.ds(block, 1), :]
    fields = turned[0:16]
    for number in range(1, 8):
        fields = jnp.where(part == number, turned[16 * number : 16 * number + 16], fields)
    rows = [fields[0:1]] + [fields[k + 1 : k + 2] - centre[k : k + 1] for k in range(3)]
    rows += [fields[k : k + 1] for k in range(4, NODE_FIELDS)]
    both = jnp.where(left, table_ref[block], table_ref[block + BLK_DEV // 2])
    place = dot(both, spread_ref[...])
    pulls = node_sum([place[:, 128 * k : 128 * k + 128] for k in range(3)], rows)
    total = jnp.zeros((16, ROWS), f32)
    for number, pull in enumerate(pulls):
        high = pull.astype(bf16)
        low = (pull - high.astype(f32)).astype(bf16)
        total += lax.dot_general(
            gather_ref[number],
            jnp.concatenate([high, low], axis=1),
            (((1,), (1,)), ((), ())),
            preferred_element_type=f32,
        )
    return total


NODE_STEP = 2


def own_kernel(
    leaf_ref, row_ref, part_ref, pm_ref, nodes_ref, out_ref, table_ref, weight_ref, spread_ref, gather_ref, *picked_refs
):
    half = BLK_DEV // 2
    centre = mean_position(pm_ref)
    fill_tables((pm_ref,), centre, table_ref, weight_ref)
    left = left_lanes()

    def step(index, carry):
        results = []
        for place in range(STEP):
            block = index * STEP + place
            start = pl.multiple_of(block * ROWS, ROWS)
            leaves = [leaf_ref[k, block] for k in range(LEAF_N)]
            results.append(
                pull_block(pm_ref[0:3, pl.ds(start, ROWS)], centre, leaves, table_ref, weight_ref, left)
            )
        for place in range(STEP):
            out_ref[index * STEP + place, 0:3] = results[place]
        return carry

    lax.fori_loop(0, BLK_DEV // STEP, step, 0)

    row = lax.broadcasted_iota(jnp.int32, (ROWS, 128), 0)
    lane = lax.broadcasted_iota(jnp.int32, (ROWS, 128), 1)
    for along in range(3):
        inner = row & 63
        hit = (inner == along) | (inner == 16 + along) | (inner == 40 + along)
        hit = hit & ((row >> 6) == (lane >> 6))
        spread_ref[:, 128 * along : 128 * along + 128] = jnp.where(hit, -0.5, 0.0).astype(bf16)
        row16 = lax.broadcasted_iota(jnp.int32, (16, 256), 0)
        lane16 = lax.broadcasted_iota(jnp.int32, (16, 256), 1) & 127
        mine = row16 == along + 4 * (lane16 >> 6)
        gather_ref[along] = jnp.where(mine, 1.0, 0.0).astype(bf16)

    def gather(refs, first):
        for number, ref in enumerate(refs):
            for node in range(2 * LIST_N):
                ref[pl.ds(node, 1), :] = nodes_ref[pl.ds(row_ref[first + number, node], 1), :]

    def compute(refs, first):
        results = [
            node_pair(first + number, centre, table_ref, part_ref, ref[...], left, spread_ref, gather_ref)
            for number, ref in enumerate(refs)
        ]
        for number, result in enumerate(results):
            out_ref[first + number, 0:3] += result[0:3]
            out_ref[first + number + half, 0:3] += result[4:7]

    before, after = picked_refs[:NODE_STEP], picked_refs[NODE_STEP:]
    gather(before, 0)

    def node_step(index, carry):
        first = index * (2 * NODE_STEP)
        gather(after, first + NODE_STEP)
        compute(before, first)
        gather(before, jnp.minimum(first + 2 * NODE_STEP, half - NODE_STEP))
        compute(after, first + NODE_STEP)
        return carry

    lax.fori_loop(0, half // (2 * NODE_STEP), node_step, 0)


def own_pull(local_leaves, rows, parts, pm, nodes):
    return pl.pallas_call(
        own_kernel,
        out_shape=jax.ShapeDtypeStruct((BLK_DEV, 4, ROWS), f32),
        in_specs=[SMEM, SMEM, VMEM, VMEM, VMEM],
        out_specs=VMEM,
        scratch_shapes=[
            pltpu.VMEM((BLK_DEV, ROWS, 128), bf16),
            pltpu.VMEM((BLK_DEV, 16, ROWS), bf16),
            pltpu.VMEM((ROWS, 3 * 128), bf16),
            pltpu.VMEM((3, 16, 256), bf16),
        ]
        + [pltpu.VMEM((2 * LIST_N, 128), f32)] * (2 * NODE_STEP),
        compiler_params=params(32),
        cost_estimate=pl.CostEstimate(flops=20 * 10**9, bytes_accessed=4 * 10**6, transcendentals=9 * 10**6),
        name="own_pull",
    )(local_leaves, rows, parts, pm, nodes)


def add_kernel(slot_ref, block_ref, own_ref, back_ref, out_ref, *sum_refs):
    parts = len(sum_refs)
    for part in range(1, parts):
        sum_refs[part][...] = jnp.zeros_like(sum_refs[part])
    sum_refs[0][...] = own_ref[...]

    def one(step, carry):
        for part in range(parts):
            export = step * parts + part
            block = block_ref[export]
            sum_refs[part][block] += back_ref[slot_ref[export]]
        return carry

    lax.fori_loop(0, EXP_BLK // parts, one, 0)
    for block in range(BLK_DEV):
        total = sum_refs[0][block]
        for part in range(1, parts):
            total = total + sum_refs[part][block]
        out_ref[:, block * ROWS : (block + 1) * ROWS] = total[0:3]


def add_returned(slots, export_block, own, back):
    return pl.pallas_call(
        add_kernel,
        out_shape=jax.ShapeDtypeStruct((3, BLK_DEV * ROWS), f32),
        in_specs=[SMEM, SMEM, VMEM, VMEM],
        out_specs=VMEM,
        scratch_shapes=[pltpu.VMEM((BLK_DEV, 4, ROWS), f32)] * 4,
        compiler_params=params(16),
        name="add_returned",
    )(slots, export_block, own, back)


def swap(values):
    return lax.all_to_all(values, AXES, split_axis=0, concat_axis=0, tiled=True)


def per_device(
    positions,
    masses,
    node_mass,
    node_centre,
    node_quad,
    local_leaves,
    node_lists,
    export_block,
    export_dest,
    export_leaves,
):
    groups = lax.axis_size("wide")
    members = lax.axis_size("narrow")
    devices = groups * members
    wide = lax.axis_index("wide")
    narrow = lax.axis_index("narrow")

    place = jnp.stack(
        [
            jnp.int32(members),
            jnp.int32(members.bit_length() - 1),
            (wide + narrow + (narrow >> 1)).astype(jnp.int32),
        ]
    )
    outgoing, slots, pm = send_blocks(
        place, export_block, export_dest[:, 0], export_leaves.T, positions, masses[None], devices
    )
    arrived = swap(outgoing)

    pms = [pm] + [
        lax.ppermute(pm, AXES, [(i, i ^ flip) for i in range(devices)])
        for flip in (1, members, members + 1)
    ]
    fields, rows, parts = node_rows(node_mass[None], node_centre, node_quad, node_lists, devices)
    nodes = swap(fields).reshape(-1, 128)

    visitors = arrived.reshape(devices * CAP, 4, ROWS)
    visitor_leaves = visitors[:, 3, 0:LEAF_N].astype(jnp.int32).reshape(-1)
    pulls = remote_pull(visitor_leaves, visitors, pms)
    pulls, leaves = lax.optimization_barrier((pulls, local_leaves.T))
    back = swap(pulls.reshape(devices, CAP, 4, ROWS))
    own = own_pull(leaves, rows, parts, pm, nodes)
    return add_returned(slots, export_block, own, back.reshape(devices * CAP, 4, ROWS))


def solution(mesh):
    both = P(AXES)
    lanes = P(None, AXES)
    rows = P(AXES, None)
    return jax.shard_map(
        per_device,
        mesh=mesh,
        in_specs=(lanes, both, both, lanes, lanes, rows, rows, both, rows, rows),
        out_specs=lanes,
        check_vma=False,
    )
```

```python
import functools

import jax
import jax.numpy as jnp
from jax import lax
from jax.experimental import pallas as pl
from jax.experimental.pallas import tpu as pltpu
from jax.sharding import PartitionSpec as P

ROWS = 128
LEAF_N = 8
LIST_N = 64
CAP = 2
BLK_DEV = 64
EXP_BLK = 128
AXES = ("wide", "narrow")
GROUP = 8
STEP = 8
NODE_FIELDS = 10
SOFTEN = 0.01

f32 = jnp.float32
bf16 = jnp.bfloat16
VMEM = pl.BlockSpec(memory_space=pltpu.VMEM)
SMEM = pl.BlockSpec(memory_space=pltpu.SMEM)
HBM = pl.BlockSpec(memory_space=pltpu.HBM)


def params(mib):
    return pltpu.CompilerParams(vmem_limit_bytes=mib * 2**20)


def split3(value):
    high = value.astype(bf16)
    rest = value - high.astype(f32)
    middle = rest.astype(bf16)
    low = (rest - middle.astype(f32)).astype(bf16)
    return high, middle, low


def dot(left, right):
    return jnp.dot(left, right, preferred_element_type=f32)


def fetch(sources, targets, sems):
    copies = [
        pltpu.make_async_copy(source, target, sems.at[number])
        for number, (source, target) in enumerate(zip(sources, targets))
    ]
    for copy in copies:
        copy.start()
    return copies


def node_rows(mass, centre, quad, nodes):
    count = mass.shape[1]
    rows = count // 8
    fields = jnp.concatenate([mass, centre, quad, jnp.zeros((16 - NODE_FIELDS, count), f32)], axis=0)
    parts = [fields[:, part * rows : (part + 1) * rows] for part in range(8)]
    half = BLK_DEV // 2
    nodes = jnp.concatenate([nodes[0:half], nodes[half:]], axis=1)
    bits = rows.bit_length() - 1
    row = ((nodes >> (bits + 3)) << bits) + (nodes & (rows - 1))
    return jnp.concatenate(parts, axis=0).T, row, (nodes >> bits) & 7


def send_kernel(
    place_ref, block_in, dest_in, leaf_in, pos_in, mass_in, node_mass_in, node_centre_in, node_quad_in, list_in,
    out_ref, slot_ref, pm_ref, table_ref, row_ref, part_ref,
    block_ref, dest_ref, leaf_ref, pos_ref, mass_ref, node_mass_ref, node_centre_ref, node_quad_ref, list_ref,
    count_ref, ids_ref, sems,
):
    copies = fetch(
        (block_in, dest_in, leaf_in, pos_in, mass_in, node_mass_in, node_centre_in, node_quad_in, list_in),
        (
            block_ref, dest_ref, leaf_ref, pos_ref, mass_ref,
            node_mass_ref, node_centre_ref, node_quad_ref, list_ref,
        ),
        sems,
    )
    devices = out_ref.shape[0]
    shift, turn = place_ref[0], place_ref[1]
    out_ref[:, :, 3:4, :] = jnp.full((devices, CAP, 1, ROWS), -1.0, f32)

    def clear(index, carry):
        for part in range(8):
            count_ref[index * 8 + part] = 0
        return carry

    lax.fori_loop(0, devices // 8, clear, 0)
    for copy in copies:
        copy.wait()
    table_ref[...], row_ref[...], part_ref[...] = node_rows(
        node_mass_ref[...], node_centre_ref[...], node_quad_ref[...], list_ref[...]
    )
    pm_ref[0:3] = pos_ref[...]
    pm_ref[3:4] = mass_ref[...]
    ids_ref[...] = jnp.concatenate([leaf_ref[...].astype(f32)] * (ROWS // LEAF_N), axis=0).T

    def one(step, carry):
        for part in range(8):
            export = step * 8 + part
            dest = dest_ref[export]
            side, up, core = dest & 1, (dest >> 2) & 1, (dest >> shift) & 1
            base = dest - side - up * 4 - (core << shift)
            seen = count_ref[base]
            count_ref[base] = seen + 1
            member = (seen + turn) & (GROUP - 1)
            slot = seen >> 3
            target = base + (member & 1) + (member & 2) * 2 + ((member >> 2) << shift)
            distance = (side + up * 2 + core * 4) ^ member
            slot_ref[export] = target * CAP + slot
            start = pl.multiple_of(block_ref[export] * ROWS, ROWS)
            out_ref[target, slot, 0:3, :] = pos_ref[:, pl.ds(start, ROWS)]
            ids = ids_ref[pl.ds(export, 1), 0:LEAF_N]
            out_ref[target, slot, 3:4, 0:LEAF_N] = ids + (distance * BLK_DEV).astype(f32)
        return carry

    lax.fori_loop(0, EXP_BLK // 8, one, 0)


def send_blocks(place, devices, *arguments):
    lists = arguments[-1]
    count = arguments[-4].shape[1]
    half = (lists.shape[0] // 2, lists.shape[1] * 2)
    return pl.pallas_call(
        send_kernel,
        out_shape=(
            jax.ShapeDtypeStruct((devices, CAP, 4, ROWS), f32),
            jax.ShapeDtypeStruct((EXP_BLK,), jnp.int32),
            jax.ShapeDtypeStruct((4, BLK_DEV * ROWS), f32),
            jax.ShapeDtypeStruct((count // 8, 128), f32),
            jax.ShapeDtypeStruct(half, jnp.int32),
            jax.ShapeDtypeStruct(half, jnp.int32),
        ),
        in_specs=[SMEM] + [HBM] * len(arguments),
        out_specs=(VMEM, SMEM, VMEM, VMEM, VMEM, VMEM),
        scratch_shapes=[
            pltpu.SMEM((EXP_BLK,), jnp.int32),
            pltpu.SMEM((EXP_BLK,), jnp.int32),
        ]
        + [pltpu.VMEM(value.shape, value.dtype) for value in arguments[2:]]
        + [
            pltpu.SMEM((devices,), jnp.int32),
            pltpu.VMEM((EXP_BLK, 128), f32),
            pltpu.SemaphoreType.DMA((len(arguments),)),
        ],
        compiler_params=params(56),
        name="send_blocks",
    )(place, *arguments)


def centred_rows(position, centre):
    moved = position - centre
    square = jnp.sum(moved * moved, axis=0, keepdims=True)
    one = jnp.ones_like(square)
    return moved, square, one, jnp.zeros((3,) + square.shape[1:], f32)


def mean_position(pm_ref):
    return jnp.sum(pm_ref[0:3], axis=1, keepdims=True) * (1.0 / pm_ref.shape[1])


def fill_tables(pm_refs, centre, table_ref, weight_ref):
    chunk = 4

    def step(index, carry):
        start = pl.multiple_of(index * (chunk * ROWS), chunk * ROWS)
        for group, pm_ref in enumerate(pm_refs):
            rows = pm_ref[:, pl.ds(start, chunk * ROWS)]
            for part in range(chunk):
                window = rows[:, part * ROWS : (part + 1) * ROWS]
                leaf = group * BLK_DEV + index * chunk + part
                moved, square, one, zero = centred_rows(window[0:3], centre)
                row = jnp.concatenate([-2.0 * moved, one, square, zero], axis=0)
                high, middle, low = [piece.astype(f32) for piece in split3(row)]
                blank = jnp.zeros((16, ROWS), f32)
                half = [high, high, middle, middle, high, low, blank]
                table_ref[leaf] = jnp.concatenate(half + half, axis=0).T.astype(bf16)
                pulled = jnp.concatenate([moved, one, zero, zero[0:1]], axis=0) * window[3:4]
                high, middle, _ = split3(pulled)
                weight_ref[leaf] = jnp.concatenate([high, middle], axis=0)
        return carry

    lax.fori_loop(0, BLK_DEV // chunk, step, 0)


def pull_block(position, centre, leaves, table_ref, weight_ref, left):
    moved, square, one, zero = centred_rows(position, centre)
    row = jnp.concatenate([moved, square + SOFTEN, one, zero], axis=0)
    high, middle, low = split3(row)
    blank = jnp.zeros((16, ROWS), bf16)
    half = jnp.concatenate([high, middle, high, middle, low, high, blank], axis=0)
    none = jnp.zeros_like(half)
    right = jnp.concatenate(
        [jnp.concatenate([half, none], axis=1), jnp.concatenate([none, half], axis=1)], axis=0
    )
    total = jnp.zeros((16, ROWS), f32)
    for pair in range(LEAF_N // 2):
        first, second = leaves[2 * pair], leaves[2 * pair + 1]
        spread = dot(jnp.where(left, table_ref[first], table_ref[second]), right)
        root = lax.rsqrt(spread)
        cubed = root * root * root
        high = cubed.astype(bf16)
        low = (cubed - high.astype(f32)).astype(bf16)
        for place, leaf in enumerate((first, second)):
            lanes = slice(place * ROWS, (place + 1) * ROWS)
            weight = weight_ref[leaf]
            total += dot(
                jnp.concatenate([weight, weight], axis=1),
                jnp.concatenate([high[:, lanes], low[:, lanes]], axis=0),
            )
    total = total[0:8] + total[8:16]
    return total[0:3] - moved * total[3:4]


def left_lanes():
    return lax.broadcasted_iota(jnp.int32, (ROWS, 128), 1) < 64


def remote_kernel(leaf_ref, pos_ref, *refs):
    pm_refs = refs[:GROUP]
    out_ref, list_ref, table_ref, weight_ref = refs[GROUP:]
    slots = pos_ref.shape[0]

    def note(slot, found):
        list_ref[found] = slot
        return found + (leaf_ref[slot * LEAF_N] >= 0).astype(jnp.int32)

    found = lax.fori_loop(0, slots, note, 0)
    last = list_ref[jnp.maximum(found - 1, 0)]
    for place in range(STEP):
        list_ref[found + place] = last
    centre = mean_position(pm_refs[0])
    fill_tables(pm_refs, centre, table_ref, weight_ref)
    left = left_lanes()

    def step(index, carry):
        results = []
        for place in range(STEP):
            slot = list_ref[index * STEP + place]
            leaves = [leaf_ref[slot * LEAF_N + k] for k in range(LEAF_N)]
            results.append((slot, pull_block(pos_ref[slot][0:3], centre, leaves, table_ref, weight_ref, left)))
        for slot, result in results:
            out_ref[slot, 0:3] = result
        return carry

    lax.fori_loop(0, (found + STEP - 1) // STEP, step, 0)


def remote_pull(leaves, visitors, pms):
    slots = visitors.shape[0]
    return pl.pallas_call(
        remote_kernel,
        out_shape=jax.ShapeDtypeStruct((slots, 4, ROWS), f32),
        in_specs=[SMEM] + [VMEM] * (1 + GROUP),
        out_specs=VMEM,
        scratch_shapes=[
            pltpu.SMEM((slots + STEP,), jnp.int32),
            pltpu.VMEM((GROUP * BLK_DEV, ROWS, 128), bf16),
            pltpu.VMEM((GROUP * BLK_DEV, 16, ROWS), bf16),
        ],
        compiler_params=params(40),
        cost_estimate=pl.CostEstimate(flops=32 * 10**9, bytes_accessed=10**7, transcendentals=16 * 10**6),
        name="remote_pull",
    )(leaves, visitors, *pms)


def node_sum(place, fields):
    mass, cx, cy, cz, qxx, qyy, qzz, qxy, qxz, qyz = fields
    x, y, z = place[0] - cx, place[1] - cy, place[2] - cz
    spread = x * x + y * y + z * z + SOFTEN
    quad_x = qxx * x + qxy * y + qxz * z
    quad_y = qxy * x + qyy * y + qyz * z
    quad_z = qxz * x + qyz * y + qzz * z
    root = lax.rsqrt(spread)
    inverse = root * root
    cubed = inverse * root
    fifth = cubed * inverse
    scalar = x * quad_x + y * quad_y + z * quad_z
    radial = -mass * cubed - 2.5 * scalar * (fifth * inverse)
    return radial * x + quad_x * fifth, radial * y + quad_y * fifth, radial * z + quad_z * fifth


def node_pair(block, centre, table_ref, part_ref, picked, left, spread_ref, gather_ref):
    turned = picked.T
    part = part_ref[pl.ds(block, 1), :]
    fields = turned[0:16]
    for number in range(1, 8):
        fields = jnp.where(part == number, turned[16 * number : 16 * number + 16], fields)
    rows = [fields[0:1]] + [fields[k + 1 : k + 2] - centre[k : k + 1] for k in range(3)]
    rows += [fields[k : k + 1] for k in range(4, NODE_FIELDS)]
    both = jnp.where(left, table_ref[block], table_ref[block + BLK_DEV // 2])
    place = dot(both, spread_ref[...])
    pulls = node_sum([place[:, 128 * k : 128 * k + 128] for k in range(3)], rows)
    total = jnp.zeros((16, ROWS), f32)
    for number, pull in enumerate(pulls):
        high = pull.astype(bf16)
        low = (pull - high.astype(f32)).astype(bf16)
        total += lax.dot_general(
            gather_ref[number],
            jnp.concatenate([high, low], axis=1),
            (((1,), (1,)), ((), ())),
            preferred_element_type=f32,
        )
    return total


NODE_STEP = 2


def local_kernel(leaf_ref, pm_ref, out_ref, table_ref, weight_ref):
    centre = mean_position(pm_ref)
    fill_tables((pm_ref,), centre, table_ref, weight_ref)
    left = left_lanes()

    def step(index, carry):
        results = []
        for place in range(STEP):
            block = index * STEP + place
            start = pl.multiple_of(block * ROWS, ROWS)
            leaves = [leaf_ref[k, block] for k in range(LEAF_N)]
            results.append(
                pull_block(pm_ref[0:3, pl.ds(start, ROWS)], centre, leaves, table_ref, weight_ref, left)
            )
        for place in range(STEP):
            out_ref[index * STEP + place, 0:3] = results[place]
        return carry

    lax.fori_loop(0, BLK_DEV // STEP, step, 0)


def local_pull(local_leaves, pm):
    return pl.pallas_call(
        local_kernel,
        out_shape=jax.ShapeDtypeStruct((BLK_DEV, 4, ROWS), f32),
        in_specs=[SMEM, VMEM],
        out_specs=VMEM,
        scratch_shapes=[
            pltpu.VMEM((BLK_DEV, ROWS, 128), bf16),
            pltpu.VMEM((BLK_DEV, 16, ROWS), bf16),
        ],
        compiler_params=params(24),
        cost_estimate=pl.CostEstimate(flops=16 * 10**9, bytes_accessed=10**6, transcendentals=8 * 10**6),
        name="local_pull",
    )(local_leaves, pm)


def node_kernel(
    row_ref, part_ref, pm_ref, nodes_ref, local_ref, out_ref, table_ref, weight_ref, spread_ref, gather_ref, *picked_refs
):
    half = BLK_DEV // 2
    centre = mean_position(pm_ref)
    fill_tables((pm_ref,), centre, table_ref, weight_ref)
    left = left_lanes()

    row = lax.broadcasted_iota(jnp.int32, (ROWS, 128), 0)
    lane = lax.broadcasted_iota(jnp.int32, (ROWS, 128), 1)
    for along in range(3):
        inner = row & 63
        hit = (inner == along) | (inner == 16 + along) | (inner == 40 + along)
        hit = hit & ((row >> 6) == (lane >> 6))
        spread_ref[:, 128 * along : 128 * along + 128] = jnp.where(hit, -0.5, 0.0).astype(bf16)
        row16 = lax.broadcasted_iota(jnp.int32, (16, 256), 0)
        lane16 = lax.broadcasted_iota(jnp.int32, (16, 256), 1) & 127
        mine = row16 == along + 4 * (lane16 >> 6)
        gather_ref[along] = jnp.where(mine, 1.0, 0.0).astype(bf16)

    def gather(refs, first):
        for number, ref in enumerate(refs):
            for node in range(2 * LIST_N):
                ref[pl.ds(node, 1), :] = nodes_ref[pl.ds(row_ref[first + number, node], 1), :]

    def compute(refs, first):
        results = [
            node_pair(first + number, centre, table_ref, part_ref, ref[...], left, spread_ref, gather_ref)
            for number, ref in enumerate(refs)
        ]
        for number, result in enumerate(results):
            out_ref[first + number, 0:3] = local_ref[first + number, 0:3] + result[0:3]
            out_ref[first + number + half, 0:3] = local_ref[first + number + half, 0:3] + result[4:7]

    before, after = picked_refs[:NODE_STEP], picked_refs[NODE_STEP:]
    gather(before, 0)

    def node_step(index, carry):
        first = index * (2 * NODE_STEP)
        gather(after, first + NODE_STEP)
        compute(before, first)
        gather(before, jnp.minimum(first + 2 * NODE_STEP, half - NODE_STEP))
        compute(after, first + NODE_STEP)
        return carry

    lax.fori_loop(0, half // (2 * NODE_STEP), node_step, 0)


def node_pull(rows, parts, pm, nodes, local):
    return pl.pallas_call(
        node_kernel,
        out_shape=jax.ShapeDtypeStruct((BLK_DEV, 4, ROWS), f32),
        in_specs=[SMEM, VMEM, VMEM, VMEM, VMEM],
        out_specs=VMEM,
        scratch_shapes=[
            pltpu.VMEM((BLK_DEV, ROWS, 128), bf16),
            pltpu.VMEM((BLK_DEV, 16, ROWS), bf16),
            pltpu.VMEM((ROWS, 3 * 128), bf16),
            pltpu.VMEM((3, 16, 256), bf16),
        ]
        + [pltpu.VMEM((2 * LIST_N, 128), f32)] * (2 * NODE_STEP),
        compiler_params=params(24),
        cost_estimate=pl.CostEstimate(flops=12 * 10**9, bytes_accessed=4 * 10**6, transcendentals=10**6),
        name="node_pull",
    )(rows, parts, pm, nodes, local)


def add_kernel(slot_ref, block_ref, own_ref, back_ref, out_ref, *sum_refs):
    parts = len(sum_refs)
    for part in range(1, parts):
        sum_refs[part][...] = jnp.zeros_like(sum_refs[part])
    sum_refs[0][...] = own_ref[...]

    def one(step, carry):
        for part in range(parts):
            export = step * parts + part
            block = block_ref[export]
            sum_refs[part][block] += back_ref[slot_ref[export]]
        return carry

    lax.fori_loop(0, EXP_BLK // parts, one, 0)
    for block in range(BLK_DEV):
        total = sum_refs[0][block]
        for part in range(1, parts):
            total = total + sum_refs[part][block]
        out_ref[:, block * ROWS : (block + 1) * ROWS] = total[0:3]


def add_returned(slots, export_block, own, back):
    return pl.pallas_call(
        add_kernel,
        out_shape=jax.ShapeDtypeStruct((3, BLK_DEV * ROWS), f32),
        in_specs=[SMEM, SMEM, VMEM, VMEM],
        out_specs=VMEM,
        scratch_shapes=[pltpu.VMEM((BLK_DEV, 4, ROWS), f32)] * 4,
        compiler_params=params(16),
        name="add_returned",
    )(slots, export_block, own, back)


def swap(values):
    return lax.all_to_all(values, AXES, split_axis=0, concat_axis=0, tiled=True)


def per_device(
    positions,
    masses,
    node_mass,
    node_centre,
    node_quad,
    local_leaves,
    node_lists,
    export_block,
    export_dest,
    export_leaves,
):
    groups = lax.axis_size("wide")
    members = lax.axis_size("narrow")
    devices = groups * members
    narrow = lax.axis_index("narrow")

    place = jnp.stack([jnp.int32(members.bit_length() - 1), narrow.astype(jnp.int32)])
    outgoing, slots, pm, fields, rows, parts = send_blocks(
        place,
        devices,
        export_block,
        export_dest[:, 0],
        export_leaves.T,
        positions,
        masses[None],
        node_mass[None],
        node_centre,
        node_quad,
        node_lists,
    )
    arrived = swap(outgoing)
    nodes = lax.all_gather(fields, AXES, axis=0, tiled=True)

    pms = [pm] + [
        lax.ppermute(pm, "narrow", [(i, i ^ flip) for i in range(members)]) for flip in (1, 4, 5)
    ]
    pms += [lax.ppermute(other, "wide", [(i, i ^ 1) for i in range(groups)]) for other in pms]
    local = local_pull(local_leaves.T, pm)
    arrived, local = lax.optimization_barrier((arrived, local))

    visitors = arrived.reshape(devices * CAP, 4, ROWS)
    visitor_leaves = visitors[:, 3, 0:LEAF_N].astype(jnp.int32).reshape(-1)
    pulls = remote_pull(visitor_leaves, visitors, pms)
    pulls, local = lax.optimization_barrier((pulls, local))
    back = swap(pulls.reshape(devices, CAP, 4, ROWS))
    own = node_pull(rows, parts, pm, nodes, local)
    return add_returned(slots, export_block, own, back.reshape(devices * CAP, 4, ROWS))


def solution(mesh):
    both = P(AXES)
    lanes = P(None, AXES)
    rows = P(AXES, None)
    return jax.shard_map(
        per_device,
        mesh=mesh,
        in_specs=(lanes, both, both, lanes, lanes, rows, rows, both, rows, rows),
        out_specs=lanes,
        check_vma=False,
    )
```

```python
import functools

import jax
import jax.numpy as jnp
from jax import lax
from jax.experimental import pallas as pl
from jax.experimental.pallas import tpu as pltpu
from jax.sharding import PartitionSpec as P

ROWS = 128
LEAF_N = 8
LIST_N = 64
CAP = 2
BLK_DEV = 64
EXP_BLK = 128
AXES = ("wide", "narrow")
GROUP = 8
STEP = 8
NODE_FIELDS = 10
SOFTEN = 0.01

f32 = jnp.float32
bf16 = jnp.bfloat16
VMEM = pl.BlockSpec(memory_space=pltpu.VMEM)
SMEM = pl.BlockSpec(memory_space=pltpu.SMEM)
HBM = pl.BlockSpec(memory_space=pltpu.HBM)


def params(mib):
    return pltpu.CompilerParams(vmem_limit_bytes=mib * 2**20)


def split3(value):
    high = value.astype(bf16)
    rest = value - high.astype(f32)
    middle = rest.astype(bf16)
    low = (rest - middle.astype(f32)).astype(bf16)
    return high, middle, low


def dot(left, right):
    return jnp.dot(left, right, preferred_element_type=f32)


def fetch(sources, targets, sems):
    copies = [
        pltpu.make_async_copy(source, target, sems.at[number])
        for number, (source, target) in enumerate(zip(sources, targets))
    ]
    for copy in copies:
        copy.start()
    return copies


def node_rows(mass, centre, quad, nodes, devices):
    count = mass.shape[1]
    rows = count // 8
    fields = jnp.concatenate([mass, centre, quad, jnp.zeros((16 - NODE_FIELDS, count), f32)], axis=0)
    parts = [fields[:, part * rows : (part + 1) * rows] for part in range(8)]
    half = BLK_DEV // 2
    nodes = jnp.concatenate([nodes[0:half], nodes[half:]], axis=1)
    bits = rows.bit_length() - 1
    each = rows // GROUP
    share = (nodes & (rows - 1)) // each
    row = (share * devices + (nodes >> (bits + 3))) * each + (nodes & (each - 1))
    return jnp.concatenate(parts, axis=0).T, row, (nodes >> bits) & 7


def send_kernel(
    block_in, dest_in, leaf_in, pos_in, mass_in, node_mass_in, node_centre_in, node_quad_in, list_in,
    out_ref, slot_ref, pm_ref, row_ref, part_ref,
    block_ref, dest_ref, leaf_ref, pos_ref, mass_ref, node_mass_ref, node_centre_ref, node_quad_ref, list_ref,
    count_ref, ids_ref, sems,
):
    copies = fetch(
        (block_in, dest_in, leaf_in, pos_in, mass_in, node_mass_in, node_centre_in, node_quad_in, list_in),
        (
            block_ref, dest_ref, leaf_ref, pos_ref, mass_ref,
            node_mass_ref, node_centre_ref, node_quad_ref, list_ref,
        ),
        sems,
    )
    devices = out_ref.shape[0]
    shift = lax.axis_size("narrow").bit_length() - 1
    turn = lax.axis_index("narrow")
    out_ref[:, 0:CAP, 3:4, :] = jnp.full((devices, CAP, 1, ROWS), -1.0, f32)

    def clear(index, carry):
        for part in range(8):
            count_ref[index * 8 + part] = 0
        return carry

    lax.fori_loop(0, devices // 8, clear, 0)
    for copy in copies:
        copy.wait()
    table, row_ref[...], part_ref[...] = node_rows(
        node_mass_ref[...], node_centre_ref[...], node_quad_ref[...], list_ref[...], devices
    )
    each = table.shape[0] // GROUP
    for device in range(devices):
        member = (device & 1) + ((device >> 2) & 1) * 2 + ((device >> shift) & 1) * 4
        out_ref[device, CAP] = table[member * each : (member + 1) * each]
    pm_ref[0:3] = pos_ref[...]
    pm_ref[3:4] = mass_ref[...]
    ids_ref[...] = jnp.concatenate([leaf_ref[...].astype(f32)] * (ROWS // LEAF_N), axis=0).T

    def one(step, carry):
        for part in range(8):
            export = step * 8 + part
            dest = dest_ref[export]
            side, up, core = dest & 1, (dest >> 2) & 1, (dest >> shift) & 1
            base = dest - side - up * 4 - (core << shift)
            seen = count_ref[base]
            count_ref[base] = seen + 1
            member = (seen + turn) & (GROUP - 1)
            slot = seen >> 3
            target = base + (member & 1) + (member & 2) * 2 + ((member >> 2) << shift)
            distance = (side + up * 2 + core * 4) ^ member
            slot_ref[export] = target * CAP + slot
            start = pl.multiple_of(block_ref[export] * ROWS, ROWS)
            out_ref[target, slot, 0:3, :] = pos_ref[:, pl.ds(start, ROWS)]
            ids = ids_ref[pl.ds(export, 1), 0:LEAF_N]
            out_ref[target, slot, 3:4, 0:LEAF_N] = ids + (distance * BLK_DEV).astype(f32)
        return carry

    lax.fori_loop(0, EXP_BLK // 8, one, 0)


def send_blocks(devices, *arguments):
    lists = arguments[-1]
    half = (lists.shape[0] // 2, lists.shape[1] * 2)
    return pl.pallas_call(
        send_kernel,
        out_shape=(
            jax.ShapeDtypeStruct((devices, CAP + 1, 4, ROWS), f32),
            jax.ShapeDtypeStruct((EXP_BLK,), jnp.int32),
            jax.ShapeDtypeStruct((4, BLK_DEV * ROWS), f32),
            jax.ShapeDtypeStruct(half, jnp.int32),
            jax.ShapeDtypeStruct(half, jnp.int32),
        ),
        in_specs=[HBM] * len(arguments),
        out_specs=(VMEM, SMEM, VMEM, VMEM, VMEM),
        scratch_shapes=[
            pltpu.SMEM((EXP_BLK,), jnp.int32),
            pltpu.SMEM((EXP_BLK,), jnp.int32),
        ]
        + [pltpu.VMEM(value.shape, value.dtype) for value in arguments[2:]]
        + [
            pltpu.SMEM((devices,), jnp.int32),
            pltpu.VMEM((EXP_BLK, 128), f32),
            pltpu.SemaphoreType.DMA((len(arguments),)),
        ],
        compiler_params=params(56),
        name="send_blocks",
    )(*arguments)


def centred_rows(position, centre):
    moved = position - centre
    square = jnp.sum(moved * moved, axis=0, keepdims=True)
    one = jnp.ones_like(square)
    return moved, square, one, jnp.zeros((3,) + square.shape[1:], f32)


def mean_position(pm_ref):
    return jnp.sum(pm_ref[0:3], axis=1, keepdims=True) * (1.0 / pm_ref.shape[1])


def fill_tables(pm_refs, centre, table_ref, weight_ref):
    chunk = 4

    def step(index, carry):
        start = pl.multiple_of(index * (chunk * ROWS), chunk * ROWS)
        for group, pm_ref in enumerate(pm_refs):
            rows = pm_ref[:, pl.ds(start, chunk * ROWS)]
            for part in range(chunk):
                window = rows[:, part * ROWS : (part + 1) * ROWS]
                leaf = group * BLK_DEV + index * chunk + part
                moved, square, one, zero = centred_rows(window[0:3], centre)
                row = jnp.concatenate([-2.0 * moved, one, square, zero], axis=0)
                high, middle, low = [piece.astype(f32) for piece in split3(row)]
                blank = jnp.zeros((16, ROWS), f32)
                half = [high, high, middle, middle, high, low, blank]
                table_ref[leaf] = jnp.concatenate(half + half, axis=0).T.astype(bf16)
                pulled = jnp.concatenate([moved, one, zero, zero[0:1]], axis=0) * window[3:4]
                high, middle, _ = split3(pulled)
                weight_ref[leaf] = jnp.concatenate([high, middle], axis=0)
        return carry

    lax.fori_loop(0, BLK_DEV // chunk, step, 0)


def pull_block(position, centre, leaves, table_ref, weight_ref, left):
    moved, square, one, zero = centred_rows(position, centre)
    row = jnp.concatenate([moved, square + SOFTEN, one, zero], axis=0)
    high, middle, low = split3(row)
    blank = jnp.zeros((16, ROWS), bf16)
    half = jnp.concatenate([high, middle, high, middle, low, high, blank], axis=0)
    none = jnp.zeros_like(half)
    right = jnp.concatenate(
        [jnp.concatenate([half, none], axis=1), jnp.concatenate([none, half], axis=1)], axis=0
    )
    total = jnp.zeros((16, ROWS), f32)
    for pair in range(LEAF_N // 2):
        first, second = leaves[2 * pair], leaves[2 * pair + 1]
        spread = dot(jnp.where(left, table_ref[first], table_ref[second]), right)
        root = lax.rsqrt(spread)
        cubed = root * root * root
        high = cubed.astype(bf16)
        low = (cubed - high.astype(f32)).astype(bf16)
        for place, leaf in enumerate((first, second)):
            lanes = slice(place * ROWS, (place + 1) * ROWS)
            weight = weight_ref[leaf]
            total += dot(
                jnp.concatenate([weight, weight], axis=1),
                jnp.concatenate([high[:, lanes], low[:, lanes]], axis=0),
            )
    total = total[0:8] + total[8:16]
    return total[0:3] - moved * total[3:4]


def left_lanes():
    return lax.broadcasted_iota(jnp.int32, (ROWS, 128), 1) < 64


def remote_kernel(leaf_ref, pos_ref, *refs):
    pm_refs = refs[:GROUP]
    out_ref, list_ref, table_ref, weight_ref = refs[GROUP:]
    devices = pos_ref.shape[0] // (CAP + 1)

    def note(index, found):
        for part in range(8):
            for slot in range(CAP):
                slot = (index * 8 + part) * (CAP + 1) + slot
                list_ref[found] = slot
                found = found + jnp.where(leaf_ref[slot * LEAF_N] >= 0, 1, 0)
        return found

    found = lax.fori_loop(0, devices // 8, note, 0)
    last = list_ref[jnp.maximum(found - 1, 0)]
    for place in range(STEP):
        list_ref[found + place] = last
    centre = mean_position(pm_refs[0])
    fill_tables(pm_refs, centre, table_ref, weight_ref)
    left = left_lanes()

    def step(index, carry):
        results = []
        for place in range(STEP):
            slot = list_ref[index * STEP + place]
            leaves = [leaf_ref[slot * LEAF_N + k] for k in range(LEAF_N)]
            results.append((slot, pull_block(pos_ref[slot][0:3], centre, leaves, table_ref, weight_ref, left)))
        for slot, result in results:
            out_ref[slot // (CAP + 1), slot % (CAP + 1), 0:3] = result
        return carry

    lax.fori_loop(0, (found + STEP - 1) // STEP, step, 0)


def remote_pull(leaves, visitors, pms):
    devices = visitors.shape[0] // (CAP + 1)
    return pl.pallas_call(
        remote_kernel,
        out_shape=jax.ShapeDtypeStruct((devices, CAP, 4, ROWS), f32),
        in_specs=[SMEM] + [VMEM] * (1 + GROUP),
        out_specs=VMEM,
        scratch_shapes=[
            pltpu.SMEM((devices * CAP + STEP,), jnp.int32),
            pltpu.VMEM((GROUP * BLK_DEV, ROWS, 128), bf16),
            pltpu.VMEM((GROUP * BLK_DEV, 16, ROWS), bf16),
        ],
        compiler_params=params(40),
        cost_estimate=pl.CostEstimate(flops=32 * 10**9, bytes_accessed=10**7, transcendentals=16 * 10**6),
        name="remote_pull",
    )(leaves, visitors, *pms)


def node_sum(place, fields):
    mass, cx, cy, cz, qxx, qyy, qzz, qxy, qxz, qyz = fields
    x, y, z = place[0] - cx, place[1] - cy, place[2] - cz
    spread = x * x + y * y + (z * z + SOFTEN)
    quad_x = qxx * x + qxy * y + qxz * z
    quad_y = qxy * x + qyy * y + qyz * z
    quad_z = qxz * x + qyz * y + qzz * z
    root = lax.rsqrt(spread)
    inverse = root * root
    cubed = inverse * root
    fifth = cubed * inverse
    scalar = x * quad_x + y * quad_y + z * quad_z
    radial = mass * cubed + scalar * (fifth * (-2.5 * inverse))
    return radial * x + quad_x * fifth, radial * y + quad_y * fifth, radial * z + quad_z * fifth


NODE_PART = 16


def node_kernel(
    row_ref, part_ref, pm_ref, local_ref, *refs,
):
    half = BLK_DEV // 2
    share_refs, (out_ref, table_ref, weight_ref, spread_ref, gather_ref, nodes_ref) = refs[:GROUP], refs[GROUP : GROUP + 6]
    refs = refs[GROUP + 6 :]
    picked_refs, field_refs, place_refs, pull_refs = refs[0:2], refs[2:4], refs[4:6], refs[6:8]
    narrow = lax.axis_index("narrow")
    here = (narrow & 1) + ((narrow >> 2) & 1) * 2 + (lax.axis_index("wide") & 1) * 4
    devices, each = share_refs[0].shape[0], share_refs[0].shape[1]
    for distance, share_ref in enumerate(share_refs):
        first = pl.multiple_of((here ^ distance) * (devices * each), devices * each)
        for device in range(0, devices, 2):
            nodes_ref[pl.ds(first + device * each, 2 * each), :] = jnp.concatenate(
                [share_ref[device], share_ref[device + 1]], axis=0
            )
    centre = mean_position(pm_ref)
    fill_tables((pm_ref,), centre, table_ref, weight_ref)
    left = left_lanes()

    row = lax.broadcasted_iota(jnp.int32, (ROWS, 128), 0)
    lane = lax.broadcasted_iota(jnp.int32, (ROWS, 128), 1)
    for along in range(3):
        inner = row & 63
        hit = (inner == along) | (inner == 16 + along) | (inner == 40 + along)
        hit = hit & ((row >> 6) == (lane >> 6))
        spread_ref[:, 128 * along : 128 * along + 128] = jnp.where(hit, -0.5, 0.0).astype(bf16)
        row16 = lax.broadcasted_iota(jnp.int32, (16, 256), 0)
        lane16 = lax.broadcasted_iota(jnp.int32, (16, 256), 1) & 127
        mine = row16 == along + 4 * (lane16 >> 6)
        gather_ref[along] = jnp.where(mine, 1.0, 0.0).astype(bf16)

    def pick(block, target, first, last):
        for node in range(first, last):
            target[pl.ds(node, 1), :] = nodes_ref[pl.ds(row_ref[block, node], 1), :]

    def lay_out(block, side):
        turned = picked_refs[side][...].T
        part = part_ref[pl.ds(block, 1), :]
        fields = turned[0:16]
        for number in range(1, 8):
            fields = jnp.where(part == number, turned[16 * number : 16 * number + 16], fields)
        rows = [-fields[0:1]] + [fields[k + 1 : k + 2] - centre[k : k + 1] for k in range(3)]
        rows += [fields[k : k + 1] for k in range(4, NODE_FIELDS)]
        for number, value in enumerate(rows):
            field_refs[side][number] = jnp.broadcast_to(value, (8, 128))
        both = jnp.where(left, table_ref[block], table_ref[block + half])
        place_refs[side][...] = dot(both, spread_ref[...])

    def compute(side, start):
        rows = [field_refs[side][number] for number in range(NODE_FIELDS)]
        halves = [
            node_sum([place_refs[side][at : at + 8, 128 * k : 128 * k + 128] for k in range(3)], rows)
            for at in range(start, start + NODE_PART, 8)
        ]
        for number in range(3):
            pull = jnp.concatenate([half_[number] for half_ in halves], axis=0)
            high = pull.astype(bf16)
            pull_refs[side][number, start : start + NODE_PART, 0:128] = high
            pull_refs[side][number, start : start + NODE_PART, 128:256] = (pull - high.astype(f32)).astype(bf16)

    def add_up(block, side):
        total = jnp.zeros((16, ROWS), f32)
        for number in range(3):
            total += lax.dot_general(
                gather_ref[number],
                pull_refs[side][number],
                (((1,), (1,)), ((), ())),
                preferred_element_type=f32,
            )
        out_ref[block, 0:3] = local_ref[block, 0:3] + total[0:3]
        out_ref[block + half, 0:3] = local_ref[block + half, 0:3] + total[4:7]

    pick(0, picked_refs[0], 0, 2 * LIST_N)
    pick(1, picked_refs[1], 0, 2 * LIST_N)
    lay_out(0, 0)

    def step(index, carry):
        for side in range(2):
            block = index * 2 + side
            other = 1 - side
            lay_out(jnp.minimum(block + 1, half - 1), other)
            add_up(jnp.maximum(block - 1, 0), other)
            ahead = jnp.minimum(block + 2, half - 1)
            for start in range(0, ROWS, NODE_PART):
                compute(side, start)
                pick(ahead, picked_refs[side], start, start + NODE_PART)
        return carry

    lax.fori_loop(0, half // 2, step, 0)
    add_up(half - 1, 1)


def node_pull(rows, parts, pm, local, shares):
    devices, each = shares[0].shape[0:2]
    return pl.pallas_call(
        node_kernel,
        out_shape=jax.ShapeDtypeStruct((BLK_DEV, 4, ROWS), f32),
        in_specs=[SMEM] + [VMEM] * (3 + GROUP),
        out_specs=VMEM,
        scratch_shapes=[
            pltpu.VMEM((BLK_DEV, ROWS, 128), bf16),
            pltpu.VMEM((BLK_DEV, 16, ROWS), bf16),
            pltpu.VMEM((ROWS, 3 * 128), bf16),
            pltpu.VMEM((3, 16, 256), bf16),
            pltpu.VMEM((GROUP * devices * each, 128), f32),
        ]
        + [pltpu.VMEM((2 * LIST_N, 128), f32)] * 2
        + [pltpu.VMEM((NODE_FIELDS, 8, 128), f32)] * 2
        + [pltpu.VMEM((ROWS, 3 * 128), f32)] * 2
        + [pltpu.VMEM((3, ROWS, 256), bf16)] * 2,
        compiler_params=params(24),
        cost_estimate=pl.CostEstimate(flops=12 * 10**9, bytes_accessed=4 * 10**6, transcendentals=10**6),
        name="node_pull",
    )(rows, parts, pm, local, *shares)


def local_kernel(leaf_ref, pm_ref, out_ref, table_ref, weight_ref):
    centre = mean_position(pm_ref)
    fill_tables((pm_ref,), centre, table_ref, weight_ref)
    left = left_lanes()

    def step(index, carry):
        results = []
        for place in range(STEP):
            block = index * STEP + place
            start = pl.multiple_of(block * ROWS, ROWS)
            leaves = [leaf_ref[k, block] for k in range(LEAF_N)]
            results.append(
                pull_block(pm_ref[0:3, pl.ds(start, ROWS)], centre, leaves, table_ref, weight_ref, left)
            )
        for place in range(STEP):
            out_ref[index * STEP + place, 0:3] = results[place]
        return carry

    lax.fori_loop(0, BLK_DEV // STEP, step, 0)


def local_pull(local_leaves, pm):
    return pl.pallas_call(
        local_kernel,
        out_shape=jax.ShapeDtypeStruct((BLK_DEV, 4, ROWS), f32),
        in_specs=[SMEM, VMEM],
        out_specs=VMEM,
        scratch_shapes=[
            pltpu.VMEM((BLK_DEV, ROWS, 128), bf16),
            pltpu.VMEM((BLK_DEV, 16, ROWS), bf16),
        ],
        compiler_params=params(24),
        cost_estimate=pl.CostEstimate(flops=16 * 10**9, bytes_accessed=10**6, transcendentals=8 * 10**6),
        name="local_pull",
    )(local_leaves, pm)


def add_kernel(slot_ref, block_ref, own_ref, back_ref, out_ref, *sum_refs):
    parts = len(sum_refs)
    for part in range(1, parts):
        sum_refs[part][...] = jnp.zeros_like(sum_refs[part])
    sum_refs[0][...] = own_ref[...]

    def one(step, carry):
        for part in range(parts):
            export = step * parts + part
            block = block_ref[export]
            sum_refs[part][block] += back_ref[slot_ref[export]]
        return carry

    lax.fori_loop(0, EXP_BLK // parts, one, 0)
    for block in range(BLK_DEV):
        total = sum_refs[0][block]
        for part in range(1, parts):
            total = total + sum_refs[part][block]
        out_ref[:, block * ROWS : (block + 1) * ROWS] = total[0:3]


def add_returned(slots, export_block, own, back):
    return pl.pallas_call(
        add_kernel,
        out_shape=jax.ShapeDtypeStruct((3, BLK_DEV * ROWS), f32),
        in_specs=[SMEM, SMEM, VMEM, VMEM],
        out_specs=VMEM,
        scratch_shapes=[pltpu.VMEM((BLK_DEV, 4, ROWS), f32)] * 4,
        compiler_params=params(16),
        name="add_returned",
    )(slots, export_block, own, back)


def swap(values):
    return lax.all_to_all(values, AXES, split_axis=0, concat_axis=0, tiled=True)


def per_device(
    positions,
    masses,
    node_mass,
    node_centre,
    node_quad,
    local_leaves,
    node_lists,
    export_block,
    export_dest,
    export_leaves,
):
    groups = lax.axis_size("wide")
    members = lax.axis_size("narrow")
    devices = groups * members

    def group_of(value):
        found = [value] + [
            lax.ppermute(value, "narrow", [(i, i ^ flip) for i in range(members)]) for flip in (1, 4, 5)
        ]
        return found + [lax.ppermute(other, "wide", [(i, i ^ 1) for i in range(groups)]) for other in found]

    outgoing, slots, pm, rows, parts = send_blocks(
        devices,
        export_block,
        export_dest[:, 0],
        export_leaves.T,
        positions,
        masses[None],
        node_mass[None],
        node_centre,
        node_quad,
        node_lists,
    )
    arrived = swap(outgoing)
    pms = group_of(pm)
    local = local_pull(local_leaves.T, pm)
    arrived, local = lax.optimization_barrier((arrived, local))

    shares = group_of(arrived[:, CAP])
    visitors = arrived.reshape(devices * (CAP + 1), 4, ROWS)
    visitor_leaves = visitors[:, 3, 0:LEAF_N].astype(jnp.int32).reshape(-1)
    pulls = remote_pull(visitor_leaves, visitors, pms)
    pulls, local = lax.optimization_barrier((pulls, local))
    back = swap(pulls)
    own = node_pull(rows, parts, pm, local, shares)
    return add_returned(slots, export_block, own, back.reshape(devices * CAP, 4, ROWS))


def solution(mesh):
    both = P(AXES)
    lanes = P(None, AXES)
    rows = P(AXES, None)
    return jax.shard_map(
        per_device,
        mesh=mesh,
        in_specs=(lanes, both, both, lanes, lanes, rows, rows, both, rows, rows),
        out_specs=lanes,
        check_vma=False,
    )
```

```python
import functools

import jax
import jax.numpy as jnp
from jax import lax
from jax.experimental import pallas as pl
from jax.experimental.pallas import tpu as pltpu
from jax.sharding import PartitionSpec as P

ROWS = 128
LEAF_N = 8
LIST_N = 64
CAP = 2
BLK_DEV = 64
EXP_BLK = 128
AXES = ("wide", "narrow")
GROUP = 8
STEP = 8
NODE_FIELDS = 10
SOFTEN = 0.01

f32 = jnp.float32
bf16 = jnp.bfloat16
VMEM = pl.BlockSpec(memory_space=pltpu.VMEM)
SMEM = pl.BlockSpec(memory_space=pltpu.SMEM)
HBM = pl.BlockSpec(memory_space=pltpu.HBM)


def params(mib):
    return pltpu.CompilerParams(vmem_limit_bytes=mib * 2**20)


def split3(value):
    high = value.astype(bf16)
    rest = value - high.astype(f32)
    middle = rest.astype(bf16)
    low = (rest - middle.astype(f32)).astype(bf16)
    return high, middle, low


def dot(left, right):
    return jnp.dot(left, right, preferred_element_type=f32)


def fetch(sources, targets, sems):
    copies = [
        pltpu.make_async_copy(source, target, sems.at[number])
        for number, (source, target) in enumerate(zip(sources, targets))
    ]
    for copy in copies:
        copy.start()
    return copies


def node_rows(mass, centre, quad, nodes, devices):
    count = mass.shape[1]
    rows = count // 8
    fields = jnp.concatenate([mass, centre, quad, jnp.zeros((16 - NODE_FIELDS, count), f32)], axis=0)
    parts = [fields[:, part * rows : (part + 1) * rows] for part in range(8)]
    half = BLK_DEV // 2
    nodes = jnp.concatenate([nodes[0:half], nodes[half:]], axis=1)
    bits = rows.bit_length() - 1
    each = rows // GROUP
    share = (nodes & (rows - 1)) // each
    row = (share * devices + (nodes >> (bits + 3))) * each + (nodes & (each - 1))
    return jnp.concatenate(parts, axis=0).T, row, (nodes >> bits) & 7


def send_kernel(
    block_in, dest_in, leaf_in, pos_in, mass_in, node_mass_in, node_centre_in, node_quad_in, list_in,
    out_ref, slot_ref, pm_ref, row_ref, part_ref,
    block_ref, dest_ref, leaf_ref, pos_ref, mass_ref, node_mass_ref, node_centre_ref, node_quad_ref, list_ref,
    count_ref, ids_ref, sems,
):
    copies = fetch(
        (block_in, dest_in, leaf_in, pos_in, mass_in, node_mass_in, node_centre_in, node_quad_in, list_in),
        (
            block_ref, dest_ref, leaf_ref, pos_ref, mass_ref,
            node_mass_ref, node_centre_ref, node_quad_ref, list_ref,
        ),
        sems,
    )
    devices = out_ref.shape[0]
    shift = lax.axis_size("narrow").bit_length() - 1
    turn = lax.axis_index("narrow")
    out_ref[:, 0:CAP, 3:4, :] = jnp.full((devices, CAP, 1, ROWS), -1.0, f32)

    def clear(index, carry):
        for part in range(8):
            count_ref[index * 8 + part] = 0
        return carry

    lax.fori_loop(0, devices // 8, clear, 0)
    for copy in copies:
        copy.wait()
    table, row_ref[...], part_ref[...] = node_rows(
        node_mass_ref[...], node_centre_ref[...], node_quad_ref[...], list_ref[...], devices
    )
    each = table.shape[0] // GROUP
    for device in range(devices):
        member = (device & 1) + ((device >> 2) & 1) * 2 + ((device >> shift) & 1) * 4
        out_ref[device, CAP] = table[member * each : (member + 1) * each]
    size = pos_ref.shape[1]
    centre = jnp.sum(pos_ref[...], axis=1, keepdims=True) * (1.0 / size)
    moved = pos_ref[...] - centre
    square = jnp.sum(moved * moved, axis=0, keepdims=True)
    mass = mass_ref[...]
    pm_ref[:, 0:size] = jnp.concatenate([-2.0 * moved, square, mass * moved, mass], axis=0)
    pm_ref[:, size : size + ROWS] = jnp.broadcast_to(
        jnp.concatenate([centre, jnp.zeros((5, 1), f32)], axis=0), (8, ROWS)
    )
    ids_ref[...] = jnp.concatenate([leaf_ref[...].astype(f32)] * (ROWS // LEAF_N), axis=0).T

    def one(step, carry):
        for part in range(8):
            export = step * 8 + part
            dest = dest_ref[export]
            side, up, core = dest & 1, (dest >> 2) & 1, (dest >> shift) & 1
            base = dest - side - up * 4 - (core << shift)
            seen = count_ref[base]
            count_ref[base] = seen + 1
            member = (seen + turn) & (GROUP - 1)
            slot = seen >> 3
            target = base + (member & 1) + (member & 2) * 2 + ((member >> 2) << shift)
            distance = (side + up * 2 + core * 4) ^ member
            slot_ref[export] = target * CAP + slot
            start = pl.multiple_of(block_ref[export] * ROWS, ROWS)
            out_ref[target, slot, 0:3, :] = pos_ref[:, pl.ds(start, ROWS)]
            ids = ids_ref[pl.ds(export, 1), 0:LEAF_N]
            out_ref[target, slot, 3:4, 0:LEAF_N] = ids + (distance * BLK_DEV).astype(f32)
        return carry

    lax.fori_loop(0, EXP_BLK // 8, one, 0)


def send_blocks(devices, *arguments):
    lists = arguments[-1]
    half = (lists.shape[0] // 2, lists.shape[1] * 2)
    return pl.pallas_call(
        send_kernel,
        out_shape=(
            jax.ShapeDtypeStruct((devices, CAP + 1, 4, ROWS), f32),
            jax.ShapeDtypeStruct((EXP_BLK,), jnp.int32),
            jax.ShapeDtypeStruct((8, BLK_DEV * ROWS + ROWS), f32),
            jax.ShapeDtypeStruct(half, jnp.int32),
            jax.ShapeDtypeStruct(half, jnp.int32),
        ),
        in_specs=[HBM] * len(arguments),
        out_specs=(VMEM, SMEM, VMEM, VMEM, VMEM),
        scratch_shapes=[
            pltpu.SMEM((EXP_BLK,), jnp.int32),
            pltpu.SMEM((EXP_BLK,), jnp.int32),
        ]
        + [pltpu.VMEM(value.shape, value.dtype) for value in arguments[2:]]
        + [
            pltpu.SMEM((devices,), jnp.int32),
            pltpu.VMEM((EXP_BLK, 128), f32),
            pltpu.SemaphoreType.DMA((len(arguments),)),
        ],
        compiler_params=params(56),
        name="send_blocks",
    )(*arguments)


def fill_tables(source_refs, table_ref, weight_ref):
    chunk = 32 if len(source_refs) == 1 else 8
    row = lax.broadcasted_iota(jnp.int32, (16, ROWS), 0)
    ones = jnp.where(row < 3, 1.0, 0.0).astype(bf16)

    def step(index, carry):
        start = pl.multiple_of(index * (chunk * ROWS), chunk * ROWS)
        for group, source_ref in enumerate(source_refs):
            rows = source_ref[:, pl.ds(start, chunk * ROWS)]
            for part in range(chunk):
                leaf = group * BLK_DEV + index * chunk + part
                high, middle, low = split3(rows[:, part * ROWS : (part + 1) * ROWS])
                half = [high, high, middle, middle, high, low, ones]
                table_ref[leaf] = jnp.concatenate(half + half, axis=0).T
                weight_ref[leaf] = jnp.concatenate([high, middle], axis=0)
        return carry

    lax.fori_loop(0, BLK_DEV // chunk, step, 0)


def pull_block(moved, leaves, table_ref, weight_ref, left):
    square = jnp.sum(moved * moved, axis=0, keepdims=True) + SOFTEN
    one = jnp.ones_like(square)
    none = jnp.zeros((4, ROWS), f32)
    high, middle, low = split3(jnp.concatenate([moved, one, none], axis=0))
    pieces = [piece.astype(f32) for piece in split3(square)]
    ends = jnp.concatenate(pieces + [none, none, none, one - one], axis=0).astype(bf16)
    half = jnp.concatenate([high, middle, high, middle, low, high, ends], axis=0)
    none = jnp.zeros_like(half)
    right = jnp.concatenate(
        [jnp.concatenate([half, none], axis=1), jnp.concatenate([none, half], axis=1)], axis=0
    )
    total = jnp.zeros((16, ROWS), f32)
    for pair in range(LEAF_N // 2):
        first, second = leaves[2 * pair], leaves[2 * pair + 1]
        spread = dot(jnp.where(left, table_ref[first], table_ref[second]), right)
        root = lax.rsqrt(spread)
        cubed = root * root * root
        high = cubed.astype(bf16)
        low = (cubed - high.astype(f32)).astype(bf16)
        for place, leaf in enumerate((first, second)):
            lanes = slice(place * ROWS, (place + 1) * ROWS)
            weight = weight_ref[leaf]
            total += dot(
                jnp.concatenate([weight, weight], axis=1),
                jnp.concatenate([high[:, lanes], low[:, lanes]], axis=0),
            )
    total = total[4:8] + total[12:16]
    return total[0:3] - moved * total[3:4]


def left_lanes():
    return lax.broadcasted_iota(jnp.int32, (ROWS, 128), 1) < 64


def remote_kernel(leaf_ref, pos_ref, *refs):
    pm_refs = refs[:GROUP]
    out_ref, list_ref, centre_ref, table_ref, weight_ref = refs[GROUP:]
    devices = pos_ref.shape[0] // (CAP + 1)

    def note(index, found):
        for part in range(8):
            for slot in range(CAP):
                slot = (index * 8 + part) * (CAP + 1) + slot
                list_ref[found] = slot
                found = found + jnp.where(leaf_ref[slot * LEAF_N] >= 0, 1, 0)
        return found

    found = lax.fori_loop(0, devices // 8, note, 0)
    last = list_ref[jnp.maximum(found - 1, 0)]
    for place in range(STEP):
        list_ref[found + place] = last
    size = BLK_DEV * ROWS
    for group, pm_ref in enumerate(pm_refs):
        centre_ref[group] = pm_ref[:, size : size + ROWS]
    fill_tables(pm_refs, table_ref, weight_ref)
    left = left_lanes()

    def step(index, carry):
        results = []
        for place in range(STEP):
            slot = list_ref[index * STEP + place]
            leaves = [leaf_ref[slot * LEAF_N + k] for k in range(LEAF_N)]
            moved = pos_ref[slot][0:3] - centre_ref[leaves[0] // BLK_DEV][0:3]
            results.append((slot, pull_block(moved, leaves, table_ref, weight_ref, left)))
        for slot, result in results:
            out_ref[slot // (CAP + 1), slot % (CAP + 1), 0:3] = result
        return carry

    lax.fori_loop(0, (found + STEP - 1) // STEP, step, 0)


def remote_pull(leaves, visitors, pms):
    devices = visitors.shape[0] // (CAP + 1)
    return pl.pallas_call(
        remote_kernel,
        out_shape=jax.ShapeDtypeStruct((devices, CAP, 4, ROWS), f32),
        in_specs=[SMEM] + [VMEM] * (1 + GROUP),
        out_specs=VMEM,
        scratch_shapes=[
            pltpu.SMEM((devices * CAP + STEP,), jnp.int32),
            pltpu.VMEM((GROUP, 8, ROWS), f32),
            pltpu.VMEM((GROUP * BLK_DEV, ROWS, 128), bf16),
            pltpu.VMEM((GROUP * BLK_DEV, 16, ROWS), bf16),
        ],
        compiler_params=params(28),
        cost_estimate=pl.CostEstimate(flops=32 * 10**9, bytes_accessed=10**7, transcendentals=16 * 10**6),
        name="remote_pull",
    )(leaves, visitors, *pms)


def node_sum(place, fields):
    mass, cx, cy, cz, qxx, qyy, qzz, qxy, qxz, qyz = fields
    x, y, z = place[0] - cx, place[1] - cy, place[2] - cz
    spread = x * x + y * y + (z * z + SOFTEN)
    quad_x = qxx * x + qxy * y + qxz * z
    quad_y = qxy * x + qyy * y + qyz * z
    quad_z = qxz * x + qyz * y + qzz * z
    root = lax.rsqrt(spread)
    inverse = root * root
    cubed = inverse * root
    fifth = cubed * inverse
    scalar = x * quad_x + y * quad_y + z * quad_z
    radial = mass * cubed + scalar * (fifth * (-2.5 * inverse))
    return radial * x + quad_x * fifth, radial * y + quad_y * fifth, radial * z + quad_z * fifth


NODE_PART = 16


def node_kernel(
    row_ref, part_ref, pm_ref, local_ref, *refs,
):
    half = BLK_DEV // 2
    share_refs, (out_ref, table_ref, weight_ref, spread_ref, gather_ref, nodes_ref) = refs[:GROUP], refs[GROUP : GROUP + 6]
    refs = refs[GROUP + 6 :]
    picked_refs, field_refs, place_refs, pull_refs = refs[0:2], refs[2:4], refs[4:6], refs[6:8]
    narrow = lax.axis_index("narrow")
    here = (narrow & 1) + ((narrow >> 2) & 1) * 2 + (lax.axis_index("wide") & 1) * 4
    devices, each = share_refs[0].shape[0], share_refs[0].shape[1]
    for distance, share_ref in enumerate(share_refs):
        first = pl.multiple_of((here ^ distance) * (devices * each), devices * each)
        for device in range(0, devices, 2):
            nodes_ref[pl.ds(first + device * each, 2 * each), :] = jnp.concatenate(
                [share_ref[device], share_ref[device + 1]], axis=0
            )
    fill_tables((pm_ref,), table_ref, weight_ref)
    left = left_lanes()

    row = lax.broadcasted_iota(jnp.int32, (ROWS, 128), 0)
    lane = lax.broadcasted_iota(jnp.int32, (ROWS, 128), 1)
    for along in range(3):
        inner = row & 63
        hit = (inner == along) | (inner == 16 + along) | (inner == 40 + along)
        hit = hit & ((row >> 6) == (lane >> 6))
        spread_ref[:, 128 * along : 128 * along + 128] = jnp.where(hit, -0.5, 0.0).astype(bf16)
        row16 = lax.broadcasted_iota(jnp.int32, (16, 256), 0)
        lane16 = lax.broadcasted_iota(jnp.int32, (16, 256), 1) & 127
        mine = row16 == along + 4 * (lane16 >> 6)
        gather_ref[along] = jnp.where(mine, 1.0, 0.0).astype(bf16)

    def pick(block, target, first, last):
        for node in range(first, last):
            target[pl.ds(node, 1), :] = nodes_ref[pl.ds(row_ref[block, node], 1), :]

    def lay_out(block, side):
        turned = picked_refs[side][...].T
        part = part_ref[pl.ds(block, 1), :]
        fields = turned[0:16]
        for number in range(1, 8):
            fields = jnp.where(part == number, turned[16 * number : 16 * number + 16], fields)
        centre = pm_ref[:, BLK_DEV * ROWS : BLK_DEV * ROWS + ROWS]
        rows = [-fields[0:1]] + [fields[k + 1 : k + 2] - centre[k : k + 1] for k in range(3)]
        rows += [fields[k : k + 1] for k in range(4, NODE_FIELDS)]
        for number, value in enumerate(rows):
            field_refs[side][number] = jnp.broadcast_to(value, (8, 128))
        both = jnp.where(left, table_ref[block], table_ref[block + half])
        place_refs[side][...] = dot(both, spread_ref[...])

    def compute(side, start):
        rows = [field_refs[side][number] for number in range(NODE_FIELDS)]
        halves = [
            node_sum([place_refs[side][at : at + 8, 128 * k : 128 * k + 128] for k in range(3)], rows)
            for at in range(start, start + NODE_PART, 8)
        ]
        for number in range(3):
            pull = jnp.concatenate([half_[number] for half_ in halves], axis=0)
            high = pull.astype(bf16)
            pull_refs[side][number, start : start + NODE_PART, 0:128] = high
            pull_refs[side][number, start : start + NODE_PART, 128:256] = (pull - high.astype(f32)).astype(bf16)

    def add_up(block, side):
        total = jnp.zeros((16, ROWS), f32)
        for number in range(3):
            total += lax.dot_general(
                gather_ref[number],
                pull_refs[side][number],
                (((1,), (1,)), ((), ())),
                preferred_element_type=f32,
            )
        out_ref[block, 0:3] = local_ref[block, 0:3] + total[0:3]
        out_ref[block + half, 0:3] = local_ref[block + half, 0:3] + total[4:7]

    pick(0, picked_refs[0], 0, 2 * LIST_N)
    pick(1, picked_refs[1], 0, 2 * LIST_N)
    lay_out(0, 0)

    def step(index, carry):
        for side in range(2):
            block = index * 2 + side
            other = 1 - side
            lay_out(jnp.minimum(block + 1, half - 1), other)
            add_up(jnp.maximum(block - 1, 0), other)
            ahead = jnp.minimum(block + 2, half - 1)
            for start in range(0, ROWS, NODE_PART):
                compute(side, start)
                pick(ahead, picked_refs[side], start, start + NODE_PART)
        return carry

    lax.fori_loop(0, half // 2, step, 0)
    add_up(half - 1, 1)


def node_pull(rows, parts, pm, local, shares):
    devices, each = shares[0].shape[0:2]
    return pl.pallas_call(
        node_kernel,
        out_shape=jax.ShapeDtypeStruct((BLK_DEV, 4, ROWS), f32),
        in_specs=[SMEM] + [VMEM] * (3 + GROUP),
        out_specs=VMEM,
        scratch_shapes=[
            pltpu.VMEM((BLK_DEV, ROWS, 128), bf16),
            pltpu.VMEM((BLK_DEV, 16, ROWS), bf16),
            pltpu.VMEM((ROWS, 3 * 128), bf16),
            pltpu.VMEM((3, 16, 256), bf16),
            pltpu.VMEM((GROUP * devices * each, 128), f32),
        ]
        + [pltpu.VMEM((2 * LIST_N, 128), f32)] * 2
        + [pltpu.VMEM((NODE_FIELDS, 8, 128), f32)] * 2
        + [pltpu.VMEM((ROWS, 3 * 128), f32)] * 2
        + [pltpu.VMEM((3, ROWS, 256), bf16)] * 2,
        compiler_params=params(14),
        cost_estimate=pl.CostEstimate(flops=12 * 10**9, bytes_accessed=4 * 10**6, transcendentals=10**6),
        name="node_pull",
    )(rows, parts, pm, local, *shares)


def local_kernel(leaf_ref, pm_ref, out_ref, table_ref, weight_ref):
    fill_tables((pm_ref,), table_ref, weight_ref)
    left = left_lanes()

    def step(index, carry):
        results = []
        for place in range(STEP):
            block = index * STEP + place
            start = pl.multiple_of(block * ROWS, ROWS)
            leaves = [leaf_ref[k, block] for k in range(LEAF_N)]
            moved = pm_ref[0:3, pl.ds(start, ROWS)] * -0.5
            results.append(pull_block(moved, leaves, table_ref, weight_ref, left))
        for place in range(STEP):
            out_ref[index * STEP + place, 0:3] = results[place]
        return carry

    lax.fori_loop(0, BLK_DEV // STEP, step, 0)


def local_pull(local_leaves, pm):
    return pl.pallas_call(
        local_kernel,
        out_shape=jax.ShapeDtypeStruct((BLK_DEV, 4, ROWS), f32),
        in_specs=[SMEM, VMEM],
        out_specs=VMEM,
        scratch_shapes=[
            pltpu.VMEM((BLK_DEV, ROWS, 128), bf16),
            pltpu.VMEM((BLK_DEV, 16, ROWS), bf16),
        ],
        compiler_params=params(10),
        cost_estimate=pl.CostEstimate(flops=16 * 10**9, bytes_accessed=10**6, transcendentals=8 * 10**6),
        name="local_pull",
    )(local_leaves, pm)


def add_kernel(slot_ref, block_ref, own_ref, back_ref, out_ref, *sum_refs):
    parts = len(sum_refs)
    for part in range(1, parts):
        sum_refs[part][...] = jnp.zeros_like(sum_refs[part])
    sum_refs[0][...] = own_ref[...]

    def one(step, carry):
        for part in range(parts):
            export = step * parts + part
            block = block_ref[export]
            sum_refs[part][block] += back_ref[slot_ref[export]]
        return carry

    lax.fori_loop(0, EXP_BLK // parts, one, 0)
    for block in range(BLK_DEV):
        total = sum_refs[0][block]
        for part in range(1, parts):
            total = total + sum_refs[part][block]
        out_ref[:, block * ROWS : (block + 1) * ROWS] = total[0:3]


def add_returned(slots, export_block, own, back):
    return pl.pallas_call(
        add_kernel,
        out_shape=jax.ShapeDtypeStruct((3, BLK_DEV * ROWS), f32),
        in_specs=[SMEM, SMEM, VMEM, VMEM],
        out_specs=VMEM,
        scratch_shapes=[pltpu.VMEM((BLK_DEV, 4, ROWS), f32)] * 4,
        compiler_params=params(16),
        name="add_returned",
    )(slots, export_block, own, back)


def swap(values):
    return lax.all_to_all(values, AXES, split_axis=0, concat_axis=0, tiled=True)


def per_device(
    positions,
    masses,
    node_mass,
    node_centre,
    node_quad,
    local_leaves,
    node_lists,
    export_block,
    export_dest,
    export_leaves,
):
    groups = lax.axis_size("wide")
    members = lax.axis_size("narrow")
    devices = groups * members

    def same_core(value):
        flips = [[(i, i ^ flip) for i in range(members)] for flip in (1, 4, 5)]
        return [value] + [lax.ppermute(value, "narrow", flip) for flip in flips]

    def other_core(values):
        return values + [lax.ppermute(value, "wide", [(i, i ^ 1) for i in range(groups)]) for value in values]

    outgoing, slots, pm, rows, parts = send_blocks(
        devices,
        export_block,
        export_dest[:, 0],
        export_leaves.T,
        positions,
        masses[None],
        node_mass[None],
        node_centre,
        node_quad,
        node_lists,
    )
    arrived = swap(outgoing)
    pms = other_core(same_core(pm))
    local = local_pull(local_leaves.T, pm)
    arrived, local = lax.optimization_barrier((arrived, local))

    shares = same_core(arrived[:, CAP])
    visitors = arrived.reshape(devices * (CAP + 1), 4, ROWS)
    visitor_leaves = visitors[:, 3, 0:LEAF_N].astype(jnp.int32).reshape(-1)
    pulls = remote_pull(visitor_leaves, visitors, pms)
    pulls, local, shares = lax.optimization_barrier((pulls, local, shares))
    back = swap(pulls)
    shares = other_core(shares)
    own = node_pull(rows, parts, pm, local, shares)
    return add_returned(slots, export_block, own, back.reshape(devices * CAP, 4, ROWS))


def solution(mesh):
    both = P(AXES)
    lanes = P(None, AXES)
    rows = P(AXES, None)
    return jax.shard_map(
        per_device,
        mesh=mesh,
        in_specs=(lanes, both, both, lanes, lanes, rows, rows, both, rows, rows),
        out_specs=lanes,
        check_vma=False,
    )
```

```python
import functools

import jax
import jax.numpy as jnp
from jax import lax
from jax.experimental import pallas as pl
from jax.experimental.pallas import tpu as pltpu
from jax.sharding import PartitionSpec as P

ROWS = 128
LEAF_N = 8
LIST_N = 64
CAP = 2
BLK_DEV = 64
EXP_BLK = 128
AXES = ("wide", "narrow")
GROUP = 8
STEP = 8
NODE_FIELDS = 10
SOFTEN = 0.01

f32 = jnp.float32
bf16 = jnp.bfloat16
VMEM = pl.BlockSpec(memory_space=pltpu.VMEM)
SMEM = pl.BlockSpec(memory_space=pltpu.SMEM)
HBM = pl.BlockSpec(memory_space=pltpu.HBM)


def params(mib):
    return pltpu.CompilerParams(vmem_limit_bytes=mib * 2**20)


def split3(value):
    high = value.astype(bf16)
    rest = value - high.astype(f32)
    middle = rest.astype(bf16)
    low = (rest - middle.astype(f32)).astype(bf16)
    return high, middle, low


def dot(left, right):
    return jnp.dot(left, right, preferred_element_type=f32)


def fetch(sources, targets, sems):
    copies = [
        pltpu.make_async_copy(source, target, sems.at[number])
        for number, (source, target) in enumerate(zip(sources, targets))
    ]
    for copy in copies:
        copy.start()
    return copies


def node_rows(mass, centre, quad, nodes, devices):
    count = mass.shape[1]
    rows = count // 8
    fields = jnp.concatenate([mass, centre, quad, jnp.zeros((16 - NODE_FIELDS, count), f32)], axis=0)
    parts = [fields[:, part * rows : (part + 1) * rows] for part in range(8)]
    half = BLK_DEV // 2
    nodes = jnp.concatenate([nodes[0:half], nodes[half:]], axis=1)
    bits = rows.bit_length() - 1
    each = rows // GROUP
    share = (nodes & (rows - 1)) // each
    row = (share * devices + (nodes >> (bits + 3))) * each + (nodes & (each - 1))
    return jnp.concatenate(parts, axis=0).T, row, (nodes >> bits) & 7


def send_kernel(
    block_in, dest_in, leaf_in, pos_in, mass_in, node_mass_in, node_centre_in, node_quad_in, list_in,
    out_ref, slot_ref, pm_ref, row_ref, part_ref,
    block_ref, dest_ref, leaf_ref, pos_ref, mass_ref, node_mass_ref, node_centre_ref, node_quad_ref, list_ref,
    count_ref, ids_ref, sems,
):
    copies = fetch(
        (block_in, dest_in, leaf_in, pos_in, mass_in, node_mass_in, node_centre_in, node_quad_in, list_in),
        (
            block_ref, dest_ref, leaf_ref, pos_ref, mass_ref,
            node_mass_ref, node_centre_ref, node_quad_ref, list_ref,
        ),
        sems,
    )
    devices = out_ref.shape[0]
    shift = lax.axis_size("narrow").bit_length() - 1
    turn = lax.axis_index("narrow")
    out_ref[:, 0:CAP, 3:4, :] = jnp.full((devices, CAP, 1, ROWS), -1.0, f32)

    def clear(index, carry):
        for part in range(8):
            count_ref[index * 8 + part] = 0
        return carry

    lax.fori_loop(0, devices // 8, clear, 0)
    for copy in copies:
        copy.wait()
    table, row_ref[...], part_ref[...] = node_rows(
        node_mass_ref[...], node_centre_ref[...], node_quad_ref[...], list_ref[...], devices
    )
    each = table.shape[0] // GROUP
    for device in range(devices):
        member = (device & 1) + ((device >> 2) & 1) * 2 + ((device >> shift) & 1) * 4
        out_ref[device, CAP] = table[member * each : (member + 1) * each]
    size = pos_ref.shape[1]
    centre = jnp.sum(pos_ref[...], axis=1, keepdims=True) * (1.0 / size)
    moved = pos_ref[...] - centre
    square = jnp.sum(moved * moved, axis=0, keepdims=True)
    mass = mass_ref[...]
    pm_ref[:, 0:size] = jnp.concatenate([-2.0 * moved, square, mass * moved, mass], axis=0)
    pm_ref[:, size : size + ROWS] = jnp.broadcast_to(
        jnp.concatenate([centre, jnp.zeros((5, 1), f32)], axis=0), (8, ROWS)
    )
    ids_ref[...] = jnp.concatenate([leaf_ref[...].astype(f32)] * (ROWS // LEAF_N), axis=0).T

    def one(step, carry):
        for part in range(8):
            export = step * 8 + part
            dest = dest_ref[export]
            side, up, core = dest & 1, (dest >> 2) & 1, (dest >> shift) & 1
            base = dest - side - up * 4 - (core << shift)
            seen = count_ref[base]
            count_ref[base] = seen + 1
            member = (seen + turn) & (GROUP - 1)
            slot = seen >> 3
            target = base + (member & 1) + (member & 2) * 2 + ((member >> 2) << shift)
            distance = (side + up * 2 + core * 4) ^ member
            slot_ref[export] = target * CAP + slot
            slot_ref[EXP_BLK + export] = block_ref[export]
            start = pl.multiple_of(block_ref[export] * ROWS, ROWS)
            out_ref[target, slot, 0:3, :] = pos_ref[:, pl.ds(start, ROWS)]
            ids = ids_ref[pl.ds(export, 1), 0:LEAF_N]
            out_ref[target, slot, 3:4, 0:LEAF_N] = ids + (distance * BLK_DEV).astype(f32)
        return carry

    lax.fori_loop(0, EXP_BLK // 8, one, 0)


def send_blocks(devices, *arguments):
    lists = arguments[-1]
    half = (lists.shape[0] // 2, lists.shape[1] * 2)
    return pl.pallas_call(
        send_kernel,
        out_shape=(
            jax.ShapeDtypeStruct((devices, CAP + 1, 4, ROWS), f32),
            jax.ShapeDtypeStruct((2 * EXP_BLK,), jnp.int32),
            jax.ShapeDtypeStruct((8, BLK_DEV * ROWS + ROWS), f32),
            jax.ShapeDtypeStruct(half, jnp.int32),
            jax.ShapeDtypeStruct(half, jnp.int32),
        ),
        in_specs=[HBM] * len(arguments),
        out_specs=(VMEM, SMEM, VMEM, VMEM, VMEM),
        scratch_shapes=[
            pltpu.SMEM((EXP_BLK,), jnp.int32),
            pltpu.SMEM((EXP_BLK,), jnp.int32),
        ]
        + [pltpu.VMEM(value.shape, value.dtype) for value in arguments[2:]]
        + [
            pltpu.SMEM((devices,), jnp.int32),
            pltpu.VMEM((EXP_BLK, 128), f32),
            pltpu.SemaphoreType.DMA((len(arguments),)),
        ],
        compiler_params=params(56),
        name="send_blocks",
    )(*arguments)


def fill_tables(source_refs, table_ref, weight_ref):
    chunk = 32 if len(source_refs) == 1 else 8
    row = lax.broadcasted_iota(jnp.int32, (16, ROWS), 0)
    ones = jnp.where(row < 3, 1.0, 0.0).astype(bf16)

    def step(index, carry):
        start = pl.multiple_of(index * (chunk * ROWS), chunk * ROWS)
        for group, source_ref in enumerate(source_refs):
            rows = source_ref[:, pl.ds(start, chunk * ROWS)]
            for part in range(chunk):
                leaf = group * BLK_DEV + index * chunk + part
                high, middle, low = split3(rows[:, part * ROWS : (part + 1) * ROWS])
                half = [high, high, middle, middle, high, low, ones]
                table_ref[leaf] = jnp.concatenate(half + half, axis=0).T
                weight_ref[leaf] = jnp.concatenate([high, middle], axis=0)
        return carry

    lax.fori_loop(0, BLK_DEV // chunk, step, 0)


def pull_block(moved, leaves, table_ref, weight_ref, left):
    square = jnp.sum(moved * moved, axis=0, keepdims=True) + SOFTEN
    one = jnp.ones_like(square)
    none = jnp.zeros((4, ROWS), f32)
    high, middle, low = split3(jnp.concatenate([moved, one, none], axis=0))
    pieces = [piece.astype(f32) for piece in split3(square)]
    ends = jnp.concatenate(pieces + [none, none, none, one - one], axis=0).astype(bf16)
    half = jnp.concatenate([high, middle, high, middle, low, high, ends], axis=0)
    none = jnp.zeros_like(half)
    right = jnp.concatenate(
        [jnp.concatenate([half, none], axis=1), jnp.concatenate([none, half], axis=1)], axis=0
    )
    total = jnp.zeros((16, ROWS), f32)
    for pair in range(LEAF_N // 2):
        first, second = leaves[2 * pair], leaves[2 * pair + 1]
        spread = dot(jnp.where(left, table_ref[first], table_ref[second]), right)
        root = lax.rsqrt(spread)
        cubed = root * root * root
        high = cubed.astype(bf16)
        low = (cubed - high.astype(f32)).astype(bf16)
        for place, leaf in enumerate((first, second)):
            lanes = slice(place * ROWS, (place + 1) * ROWS)
            weight = weight_ref[leaf]
            total += dot(
                jnp.concatenate([weight, weight], axis=1),
                jnp.concatenate([high[:, lanes], low[:, lanes]], axis=0),
            )
    total = total[4:8] + total[12:16]
    return total[0:3] - moved * total[3:4]


def left_lanes():
    return lax.broadcasted_iota(jnp.int32, (ROWS, 128), 1) < 64


def remote_kernel(pos_ref, *refs):
    pm_refs = refs[:GROUP]
    out_ref, list_ref, leaf_ref, centre_ref, table_ref, weight_ref, sem = refs[GROUP:]
    devices = pos_ref.shape[0] // (CAP + 1)
    copy = pltpu.make_async_copy(pos_ref.at[:, 3], leaf_ref, sem)
    copy.start()
    size = BLK_DEV * ROWS
    for group, pm_ref in enumerate(pm_refs):
        centre_ref[group] = pm_ref[:, size : size + ROWS]
    fill_tables(pm_refs, table_ref, weight_ref)
    copy.wait()

    def note(index, found):
        for part in range(8):
            for slot in range(CAP):
                slot = (index * 8 + part) * (CAP + 1) + slot
                list_ref[found] = slot
                found = found + jnp.where(leaf_ref[slot, 0] >= 0.0, 1, 0)
        return found

    found = lax.fori_loop(0, devices // 8, note, 0)
    last = list_ref[jnp.maximum(found - 1, 0)]
    for place in range(STEP):
        list_ref[found + place] = last
    left = left_lanes()

    def step(index, carry):
        results = []
        for place in range(STEP):
            slot = list_ref[index * STEP + place]
            leaves = [leaf_ref[slot, k].astype(jnp.int32) for k in range(LEAF_N)]
            moved = pos_ref[slot][0:3] - centre_ref[leaves[0] // BLK_DEV][0:3]
            results.append((slot, pull_block(moved, leaves, table_ref, weight_ref, left)))
        for slot, result in results:
            out_ref[slot // (CAP + 1), slot % (CAP + 1), 0:3] = result
        return carry

    lax.fori_loop(0, (found + STEP - 1) // STEP, step, 0)


def remote_pull(visitors, pms):
    devices = visitors.shape[0] // (CAP + 1)
    return pl.pallas_call(
        remote_kernel,
        out_shape=jax.ShapeDtypeStruct((devices, CAP, 4, ROWS), f32),
        in_specs=[VMEM] * (1 + GROUP),
        out_specs=VMEM,
        scratch_shapes=[
            pltpu.SMEM((devices * CAP + STEP,), jnp.int32),
            pltpu.SMEM((visitors.shape[0], ROWS), f32),
            pltpu.VMEM((GROUP, 8, ROWS), f32),
            pltpu.VMEM((GROUP * BLK_DEV, ROWS, 128), bf16),
            pltpu.VMEM((GROUP * BLK_DEV, 16, ROWS), bf16),
            pltpu.SemaphoreType.DMA,
        ],
        compiler_params=params(28),
        cost_estimate=pl.CostEstimate(flops=32 * 10**9, bytes_accessed=10**7, transcendentals=16 * 10**6),
        name="remote_pull",
    )(visitors, *pms)


def node_sum(place, fields):
    mass, cx, cy, cz, qxx, qyy, qzz, qxy, qxz, qyz = fields
    x, y, z = place[0] - cx, place[1] - cy, place[2] - cz
    spread = x * x + y * y + (z * z + SOFTEN)
    quad_x = qxx * x + qxy * y + qxz * z
    quad_y = qxy * x + qyy * y + qyz * z
    quad_z = qxz * x + qyz * y + qzz * z
    root = lax.rsqrt(spread)
    inverse = root * root
    cubed = inverse * root
    fifth = cubed * inverse
    scalar = x * quad_x + y * quad_y + z * quad_z
    radial = mass * cubed + scalar * (fifth * (-2.5 * inverse))
    return radial * x + quad_x * fifth, radial * y + quad_y * fifth, radial * z + quad_z * fifth


NODE_PART = 16


def node_kernel(
    row_ref, part_ref, pm_ref, local_ref, *refs,
):
    half = BLK_DEV // 2
    share_refs, (out_ref, table_ref, weight_ref, spread_ref, gather_ref, nodes_ref) = refs[:GROUP], refs[GROUP : GROUP + 6]
    refs = refs[GROUP + 6 :]
    picked_refs, field_refs, place_refs, pull_refs = refs[0:2], refs[2:4], refs[4:6], refs[6:8]
    narrow = lax.axis_index("narrow")
    here = (narrow & 1) + ((narrow >> 2) & 1) * 2 + (lax.axis_index("wide") & 1) * 4
    devices, each = share_refs[0].shape[0], share_refs[0].shape[1]
    for distance, share_ref in enumerate(share_refs):
        first = pl.multiple_of((here ^ distance) * (devices * each), devices * each)
        for device in range(0, devices, 2):
            nodes_ref[pl.ds(first + device * each, 2 * each), :] = jnp.concatenate(
                [share_ref[device], share_ref[device + 1]], axis=0
            )
    fill_tables((pm_ref,), table_ref, weight_ref)
    left = left_lanes()

    row = lax.broadcasted_iota(jnp.int32, (ROWS, 128), 0)
    lane = lax.broadcasted_iota(jnp.int32, (ROWS, 128), 1)
    for along in range(3):
        inner = row & 63
        hit = (inner == along) | (inner == 16 + along) | (inner == 40 + along)
        hit = hit & ((row >> 6) == (lane >> 6))
        spread_ref[:, 128 * along : 128 * along + 128] = jnp.where(hit, -0.5, 0.0).astype(bf16)
        row16 = lax.broadcasted_iota(jnp.int32, (16, 256), 0)
        lane16 = lax.broadcasted_iota(jnp.int32, (16, 256), 1) & 127
        mine = row16 == along + 4 * (lane16 >> 6)
        gather_ref[along] = jnp.where(mine, 1.0, 0.0).astype(bf16)

    def pick(block, target, first, last):
        for node in range(first, last):
            target[pl.ds(node, 1), :] = nodes_ref[pl.ds(row_ref[block, node], 1), :]

    def lay_out(block, side):
        turned = picked_refs[side][...].T
        part = part_ref[pl.ds(block, 1), :]
        fields = turned[0:16]
        for number in range(1, 8):
            fields = jnp.where(part == number, turned[16 * number : 16 * number + 16], fields)
        centre = pm_ref[:, BLK_DEV * ROWS : BLK_DEV * ROWS + ROWS]
        rows = [-fields[0:1]] + [fields[k + 1 : k + 2] - centre[k : k + 1] for k in range(3)]
        rows += [fields[k : k + 1] for k in range(4, NODE_FIELDS)]
        for number, value in enumerate(rows):
            field_refs[side][number] = jnp.broadcast_to(value, (8, 128))
        both = jnp.where(left, table_ref[block], table_ref[block + half])
        place_refs[side][...] = dot(both, spread_ref[...])

    def compute(side, start):
        rows = [field_refs[side][number] for number in range(NODE_FIELDS)]
        halves = [
            node_sum([place_refs[side][at : at + 8, 128 * k : 128 * k + 128] for k in range(3)], rows)
            for at in range(start, start + NODE_PART, 8)
        ]
        for number in range(3):
            pull = jnp.concatenate([half_[number] for half_ in halves], axis=0)
            high = pull.astype(bf16)
            pull_refs[side][number, start : start + NODE_PART, 0:128] = high
            pull_refs[side][number, start : start + NODE_PART, 128:256] = (pull - high.astype(f32)).astype(bf16)

    def add_up(block, side):
        total = jnp.zeros((16, ROWS), f32)
        for number in range(3):
            total += lax.dot_general(
                gather_ref[number],
                pull_refs[side][number],
                (((1,), (1,)), ((), ())),
                preferred_element_type=f32,
            )
        out_ref[block, 0:3] = local_ref[block, 0:3] + total[0:3]
        out_ref[block + half, 0:3] = local_ref[block + half, 0:3] + total[4:7]

    pick(0, picked_refs[0], 0, 2 * LIST_N)
    pick(1, picked_refs[1], 0, 2 * LIST_N)
    lay_out(0, 0)

    def step(index, carry):
        for side in range(2):
            block = index * 2 + side
            other = 1 - side
            lay_out(jnp.minimum(block + 1, half - 1), other)
            add_up(jnp.maximum(block - 1, 0), other)
            ahead = jnp.minimum(block + 2, half - 1)
            for start in range(0, ROWS, NODE_PART):
                compute(side, start)
                pick(ahead, picked_refs[side], start, start + NODE_PART)
        return carry

    lax.fori_loop(0, half // 2, step, 0)
    add_up(half - 1, 1)


def node_pull(rows, parts, pm, local, shares):
    devices, each = shares[0].shape[0:2]
    return pl.pallas_call(
        node_kernel,
        out_shape=jax.ShapeDtypeStruct((BLK_DEV, 4, ROWS), f32),
        in_specs=[SMEM] + [VMEM] * (3 + GROUP),
        out_specs=VMEM,
        scratch_shapes=[
            pltpu.VMEM((BLK_DEV, ROWS, 128), bf16),
            pltpu.VMEM((BLK_DEV, 16, ROWS), bf16),
            pltpu.VMEM((ROWS, 3 * 128), bf16),
            pltpu.VMEM((3, 16, 256), bf16),
            pltpu.VMEM((GROUP * devices * each, 128), f32),
        ]
        + [pltpu.VMEM((2 * LIST_N, 128), f32)] * 2
        + [pltpu.VMEM((NODE_FIELDS, 8, 128), f32)] * 2
        + [pltpu.VMEM((ROWS, 3 * 128), f32)] * 2
        + [pltpu.VMEM((3, ROWS, 256), bf16)] * 2,
        compiler_params=params(14),
        cost_estimate=pl.CostEstimate(flops=12 * 10**9, bytes_accessed=4 * 10**6, transcendentals=10**6),
        name="node_pull",
    )(rows, parts, pm, local, *shares)


def local_kernel(leaf_ref, pm_ref, out_ref, table_ref, weight_ref):
    fill_tables((pm_ref,), table_ref, weight_ref)
    left = left_lanes()

    def step(index, carry):
        results = []
        for place in range(STEP):
            block = index * STEP + place
            start = pl.multiple_of(block * ROWS, ROWS)
            leaves = [leaf_ref[k, block] for k in range(LEAF_N)]
            moved = pm_ref[0:3, pl.ds(start, ROWS)] * -0.5
            results.append(pull_block(moved, leaves, table_ref, weight_ref, left))
        for place in range(STEP):
            out_ref[index * STEP + place, 0:3] = results[place]
        return carry

    lax.fori_loop(0, BLK_DEV // STEP, step, 0)


def local_pull(local_leaves, pm):
    return pl.pallas_call(
        local_kernel,
        out_shape=jax.ShapeDtypeStruct((BLK_DEV, 4, ROWS), f32),
        in_specs=[SMEM, VMEM],
        out_specs=VMEM,
        scratch_shapes=[
            pltpu.VMEM((BLK_DEV, ROWS, 128), bf16),
            pltpu.VMEM((BLK_DEV, 16, ROWS), bf16),
        ],
        compiler_params=params(10),
        cost_estimate=pl.CostEstimate(flops=16 * 10**9, bytes_accessed=10**6, transcendentals=8 * 10**6),
        name="local_pull",
    )(local_leaves, pm)


def add_kernel(slot_ref, own_ref, back_ref, out_ref, *sum_refs):
    parts = len(sum_refs)
    for part in range(1, parts):
        sum_refs[part][...] = jnp.zeros_like(sum_refs[part])
    sum_refs[0][...] = own_ref[...]

    def one(step, carry):
        for part in range(parts):
            export = step * parts + part
            block = slot_ref[EXP_BLK + export]
            sum_refs[part][block] += back_ref[slot_ref[export]]
        return carry

    lax.fori_loop(0, EXP_BLK // parts, one, 0)
    for block in range(BLK_DEV):
        total = sum_refs[0][block]
        for part in range(1, parts):
            total = total + sum_refs[part][block]
        out_ref[:, block * ROWS : (block + 1) * ROWS] = total[0:3]


def add_returned(slots, own, back):
    return pl.pallas_call(
        add_kernel,
        out_shape=jax.ShapeDtypeStruct((3, BLK_DEV * ROWS), f32),
        in_specs=[SMEM, VMEM, VMEM],
        out_specs=VMEM,
        scratch_shapes=[pltpu.VMEM((BLK_DEV, 4, ROWS), f32)] * 4,
        compiler_params=params(16),
        name="add_returned",
    )(slots, own, back)


def swap(values):
    return lax.all_to_all(values, AXES, split_axis=0, concat_axis=0, tiled=True)


def per_device(
    positions,
    masses,
    node_mass,
    node_centre,
    node_quad,
    local_leaves,
    node_lists,
    export_block,
    export_dest,
    export_leaves,
):
    groups = lax.axis_size("wide")
    members = lax.axis_size("narrow")
    devices = groups * members

    def flipped(value, axis, size, bit):
        return lax.ppermute(value, axis, [(i, i ^ bit) for i in range(size)])

    def along_x(values):
        return values + [flipped(value, "narrow", members, 1) for value in values]

    def along_z(values):
        return values + [flipped(value, "narrow", members, 4) for value in values]

    def other_core(values):
        return values + [flipped(value, "wide", groups, 1) for value in values]

    outgoing, slots, pm, rows, parts = send_blocks(
        devices,
        export_block,
        export_dest[:, 0],
        export_leaves.T,
        positions,
        masses[None],
        node_mass[None],
        node_centre,
        node_quad,
        node_lists,
    )
    arrived = swap(outgoing)
    pms = other_core([pm] + [flipped(pm, "narrow", members, bit) for bit in (1, 4, 5)])
    local = local_pull(local_leaves.T, pm)
    arrived, local = lax.optimization_barrier((arrived, local))

    shares = along_x([arrived[:, CAP]])
    visitors = arrived.reshape(devices * (CAP + 1), 4, ROWS)
    pulls = remote_pull(visitors, pms)
    pulls, local, shares = lax.optimization_barrier((pulls, local, shares))
    back = swap(pulls)
    shares = other_core(along_z(shares))
    own = node_pull(rows, parts, pm, local, shares)
    return add_returned(slots, own, back.reshape(devices * CAP, 4, ROWS))


def solution(mesh):
    both = P(AXES)
    lanes = P(None, AXES)
    rows = P(AXES, None)
    return jax.shard_map(
        per_device,
        mesh=mesh,
        in_specs=(lanes, both, both, lanes, lanes, rows, rows, both, rows, rows),
        out_specs=lanes,
        check_vma=False,
    )
```

```python
import functools

import jax
import jax.numpy as jnp
from jax import lax
from jax.experimental import pallas as pl
from jax.experimental.pallas import tpu as pltpu
from jax.sharding import PartitionSpec as P

ROWS = 128
LEAF_N = 8
LIST_N = 64
CAP = 2
BLK_DEV = 64
EXP_BLK = 128
AXES = ("wide", "narrow")
GROUP = 8
STEP = 8
NODE_FIELDS = 10
SOFTEN = 0.01

f32 = jnp.float32
bf16 = jnp.bfloat16
VMEM = pl.BlockSpec(memory_space=pltpu.VMEM)
SMEM = pl.BlockSpec(memory_space=pltpu.SMEM)
HBM = pl.BlockSpec(memory_space=pltpu.HBM)


def params(mib):
    return pltpu.CompilerParams(vmem_limit_bytes=mib * 2**20)


def split3(value):
    high = value.astype(bf16)
    rest = value - high.astype(f32)
    middle = rest.astype(bf16)
    low = (rest - middle.astype(f32)).astype(bf16)
    return high, middle, low


def dot(left, right):
    return jnp.dot(left, right, preferred_element_type=f32)


def fetch(sources, targets, sems):
    copies = [
        pltpu.make_async_copy(source, target, sems.at[number])
        for number, (source, target) in enumerate(zip(sources, targets))
    ]
    for copy in copies:
        copy.start()
    return copies


def node_rows(mass, centre, quad, nodes, devices):
    count = mass.shape[1]
    rows = count // 8
    fields = jnp.concatenate([mass, centre, quad, jnp.zeros((16 - NODE_FIELDS, count), f32)], axis=0)
    parts = [fields[:, part * rows : (part + 1) * rows] for part in range(8)]
    half = BLK_DEV // 2
    nodes = jnp.concatenate([nodes[0:half], nodes[half:]], axis=1)
    bits = rows.bit_length() - 1
    each = rows // GROUP
    share = (nodes & (rows - 1)) // each
    row = (share * devices + (nodes >> (bits + 3))) * each + (nodes & (each - 1))
    return jnp.concatenate(parts, axis=0).T, row, (nodes >> bits) & 7


def send_kernel(
    block_in, dest_in, leaf_in, pos_in, mass_in, node_mass_in, node_centre_in, node_quad_in, list_in,
    out_ref, slot_ref, pm_ref, row_ref, part_ref,
    block_ref, dest_ref, leaf_ref, pos_ref, mass_ref, node_mass_ref, node_centre_ref, node_quad_ref, list_ref,
    count_ref, ids_ref, sems,
):
    copies = fetch(
        (block_in, dest_in, leaf_in, pos_in, mass_in, node_mass_in, node_centre_in, node_quad_in, list_in),
        (
            block_ref, dest_ref, leaf_ref, pos_ref, mass_ref,
            node_mass_ref, node_centre_ref, node_quad_ref, list_ref,
        ),
        sems,
    )
    devices = out_ref.shape[0]
    shift = lax.axis_size("narrow").bit_length() - 1
    turn = lax.axis_index("narrow")
    out_ref[:, 0:CAP, 3:4, :] = jnp.full((devices, CAP, 1, ROWS), -1.0, f32)

    def clear(index, carry):
        for part in range(8):
            count_ref[index * 8 + part] = 0
        return carry

    lax.fori_loop(0, devices // 8, clear, 0)
    for copy in copies:
        copy.wait()
    table, row_ref[...], part_ref[...] = node_rows(
        node_mass_ref[...], node_centre_ref[...], node_quad_ref[...], list_ref[...], devices
    )
    each = table.shape[0] // GROUP
    for device in range(devices):
        member = (device & 1) + ((device >> 2) & 1) * 2 + ((device >> shift) & 1) * 4
        out_ref[device, CAP] = table[member * each : (member + 1) * each]
    size = pos_ref.shape[1]
    centre = jnp.sum(pos_ref[...], axis=1, keepdims=True) * (1.0 / size)
    moved = pos_ref[...] - centre
    square = jnp.sum(moved * moved, axis=0, keepdims=True)
    mass = mass_ref[...]
    pm_ref[:, 0:size] = jnp.concatenate([-2.0 * moved, square, mass * moved, mass], axis=0)
    pm_ref[:, size : size + ROWS] = jnp.broadcast_to(
        jnp.concatenate([centre, jnp.zeros((5, 1), f32)], axis=0), (8, ROWS)
    )
    ids_ref[...] = jnp.concatenate([leaf_ref[...].astype(f32)] * (ROWS // LEAF_N), axis=0).T

    def one(step, carry):
        for part in range(8):
            export = step * 8 + part
            dest = dest_ref[export]
            side, up, core = dest & 1, (dest >> 2) & 1, (dest >> shift) & 1
            base = dest - side - up * 4 - (core << shift)
            seen = count_ref[base]
            count_ref[base] = seen + 1
            member = (seen + turn) & (GROUP - 1)
            slot = seen >> 3
            target = base + (member & 1) + (member & 2) * 2 + ((member >> 2) << shift)
            distance = (side + up * 2 + core * 4) ^ member
            slot_ref[export] = target * CAP + slot
            slot_ref[EXP_BLK + export] = block_ref[export]
            start = pl.multiple_of(block_ref[export] * ROWS, ROWS)
            out_ref[target, slot, 0:3, :] = pos_ref[:, pl.ds(start, ROWS)]
            ids = ids_ref[pl.ds(export, 1), 0:LEAF_N]
            out_ref[target, slot, 3:4, 0:LEAF_N] = ids + (distance * BLK_DEV).astype(f32)
        return carry

    lax.fori_loop(0, EXP_BLK // 8, one, 0)


def send_blocks(devices, *arguments):
    lists = arguments[-1]
    half = (lists.shape[0] // 2, lists.shape[1] * 2)
    return pl.pallas_call(
        send_kernel,
        out_shape=(
            jax.ShapeDtypeStruct((devices, CAP + 1, 4, ROWS), f32),
            jax.ShapeDtypeStruct((2 * EXP_BLK,), jnp.int32),
            jax.ShapeDtypeStruct((8, BLK_DEV * ROWS + ROWS), f32),
            jax.ShapeDtypeStruct(half, jnp.int32),
            jax.ShapeDtypeStruct(half, jnp.int32),
        ),
        in_specs=[HBM] * len(arguments),
        out_specs=(VMEM, SMEM, VMEM, VMEM, VMEM),
        scratch_shapes=[
            pltpu.SMEM((EXP_BLK,), jnp.int32),
            pltpu.SMEM((EXP_BLK,), jnp.int32),
        ]
        + [pltpu.VMEM(value.shape, value.dtype) for value in arguments[2:]]
        + [
            pltpu.SMEM((devices,), jnp.int32),
            pltpu.VMEM((EXP_BLK, 128), f32),
            pltpu.SemaphoreType.DMA((len(arguments),)),
        ],
        compiler_params=params(56),
        name="send_blocks",
    )(*arguments)


def fill_tables(source_refs, table_ref, weight_ref):
    chunk = 32 if len(source_refs) == 1 else 8
    row = lax.broadcasted_iota(jnp.int32, (16, ROWS), 0)
    ones = jnp.where(row < 3, 1.0, 0.0).astype(bf16)

    def step(index, carry):
        start = pl.multiple_of(index * (chunk * ROWS), chunk * ROWS)
        for group, source_ref in enumerate(source_refs):
            rows = source_ref[:, pl.ds(start, chunk * ROWS)]
            for part in range(chunk):
                leaf = group * BLK_DEV + index * chunk + part
                high, middle, low = split3(rows[:, part * ROWS : (part + 1) * ROWS])
                half = [high, high, middle, middle, high, low, ones]
                table_ref[leaf] = jnp.concatenate(half + half, axis=0).T
                weight_ref[leaf] = jnp.concatenate([high, middle], axis=0)
        return carry

    lax.fori_loop(0, BLK_DEV // chunk, step, 0)


def pull_block(moved, leaves, table_ref, weight_ref, left):
    square = jnp.sum(moved * moved, axis=0, keepdims=True) + SOFTEN
    one = jnp.ones_like(square)
    none = jnp.zeros((4, ROWS), f32)
    high, middle, low = split3(jnp.concatenate([moved, one, none], axis=0))
    pieces = [piece.astype(f32) for piece in split3(square)]
    ends = jnp.concatenate(pieces + [none, none, none, one - one], axis=0).astype(bf16)
    half = jnp.concatenate([high, middle, high, middle, low, high, ends], axis=0)
    none = jnp.zeros_like(half)
    right = jnp.concatenate(
        [jnp.concatenate([half, none], axis=1), jnp.concatenate([none, half], axis=1)], axis=0
    )
    total = jnp.zeros((16, ROWS), f32)
    for pair in range(LEAF_N // 2):
        first, second = leaves[2 * pair], leaves[2 * pair + 1]
        spread = dot(jnp.where(left, table_ref[first], table_ref[second]), right)
        root = lax.rsqrt(spread)
        cubed = root * root * root
        high = cubed.astype(bf16)
        low = (cubed - high.astype(f32)).astype(bf16)
        for place, leaf in enumerate((first, second)):
            lanes = slice(place * ROWS, (place + 1) * ROWS)
            weight = weight_ref[leaf]
            total += dot(
                jnp.concatenate([weight, weight], axis=1),
                jnp.concatenate([high[:, lanes], low[:, lanes]], axis=0),
            )
    total = total[4:8] + total[12:16]
    return total[0:3] - moved * total[3:4]


def left_lanes():
    return lax.broadcasted_iota(jnp.int32, (ROWS, 128), 1) < 64


def remote_kernel(pos_ref, *refs):
    pm_refs = refs[:GROUP]
    out_ref, list_ref, leaf_ref, centre_ref, table_ref, weight_ref, sem = refs[GROUP:]
    devices = pos_ref.shape[0] // (CAP + 1)
    copy = pltpu.make_async_copy(pos_ref.at[:, 3], leaf_ref, sem)
    copy.start()
    size = BLK_DEV * ROWS
    for group, pm_ref in enumerate(pm_refs):
        centre_ref[group] = pm_ref[:, size : size + ROWS]
    fill_tables(pm_refs, table_ref, weight_ref)
    copy.wait()

    def note(index, found):
        for part in range(8):
            for slot in range(CAP):
                slot = (index * 8 + part) * (CAP + 1) + slot
                list_ref[found] = slot
                found = found + jnp.where(leaf_ref[slot, 0] >= 0.0, 1, 0)
        return found

    found = lax.fori_loop(0, devices // 8, note, 0)
    last = list_ref[jnp.maximum(found - 1, 0)]
    for place in range(STEP):
        list_ref[found + place] = last
    left = left_lanes()

    def step(index, carry):
        results = []
        for place in range(STEP):
            slot = list_ref[index * STEP + place]
            leaves = [leaf_ref[slot, k].astype(jnp.int32) for k in range(LEAF_N)]
            moved = pos_ref[slot][0:3] - centre_ref[leaves[0] // BLK_DEV][0:3]
            results.append((slot, pull_block(moved, leaves, table_ref, weight_ref, left)))
        for slot, result in results:
            out_ref[slot // (CAP + 1), slot % (CAP + 1), 0:3] = result
        return carry

    lax.fori_loop(0, (found + STEP - 1) // STEP, step, 0)


def remote_pull(visitors, pms):
    devices = visitors.shape[0] // (CAP + 1)
    return pl.pallas_call(
        remote_kernel,
        out_shape=jax.ShapeDtypeStruct((devices, CAP, 4, ROWS), f32),
        in_specs=[VMEM] * (1 + GROUP),
        out_specs=VMEM,
        scratch_shapes=[
            pltpu.SMEM((devices * CAP + STEP,), jnp.int32),
            pltpu.SMEM((visitors.shape[0], ROWS), f32),
            pltpu.VMEM((GROUP, 8, ROWS), f32),
            pltpu.VMEM((GROUP * BLK_DEV, ROWS, 128), bf16),
            pltpu.VMEM((GROUP * BLK_DEV, 16, ROWS), bf16),
            pltpu.SemaphoreType.DMA,
        ],
        compiler_params=params(28),
        cost_estimate=pl.CostEstimate(flops=32 * 10**9, bytes_accessed=10**7, transcendentals=16 * 10**6),
        name="remote_pull",
    )(visitors, *pms)


def node_sum(place, fields):
    mass, cx, cy, cz, qxx, qyy, qzz, qxy, qxz, qyz = fields
    x, y, z = place[0] - cx, place[1] - cy, place[2] - cz
    spread = x * x + y * y + (z * z + SOFTEN)
    quad_x = qxx * x + qxy * y + qxz * z
    quad_y = qxy * x + qyy * y + qyz * z
    quad_z = qxz * x + qyz * y + qzz * z
    root = lax.rsqrt(spread)
    inverse = root * root
    cubed = inverse * root
    fifth = cubed * inverse
    scalar = x * quad_x + y * quad_y + z * quad_z
    radial = mass * cubed + scalar * (fifth * (-2.5 * inverse))
    return radial * x + quad_x * fifth, radial * y + quad_y * fifth, radial * z + quad_z * fifth


NODE_PART = 16


def node_kernel(
    row_ref, part_ref, pm_ref, local_ref, *refs,
):
    half = BLK_DEV // 2
    share_refs, (out_ref, table_ref, weight_ref, spread_ref, gather_ref, nodes_ref) = refs[:GROUP], refs[GROUP : GROUP + 6]
    refs = refs[GROUP + 6 :]
    picked_refs, field_refs, place_refs, pull_refs = refs[0:2], refs[2:4], refs[4:6], refs[6:8]
    narrow = lax.axis_index("narrow")
    here = (narrow & 1) + ((narrow >> 2) & 1) * 2 + (lax.axis_index("wide") & 1) * 4
    devices, each = share_refs[0].shape[0], share_refs[0].shape[1]
    for distance, share_ref in enumerate(share_refs):
        first = pl.multiple_of((here ^ distance) * (devices * each), devices * each)
        for device in range(0, devices, 2):
            nodes_ref[pl.ds(first + device * each, 2 * each), :] = jnp.concatenate(
                [share_ref[device], share_ref[device + 1]], axis=0
            )
    fill_tables((pm_ref,), table_ref, weight_ref)
    left = left_lanes()

    row = lax.broadcasted_iota(jnp.int32, (ROWS, 128), 0)
    lane = lax.broadcasted_iota(jnp.int32, (ROWS, 128), 1)
    for along in range(3):
        inner = row & 63
        hit = (inner == along) | (inner == 16 + along) | (inner == 40 + along)
        hit = hit & ((row >> 6) == (lane >> 6))
        spread_ref[:, 128 * along : 128 * along + 128] = jnp.where(hit, -0.5, 0.0).astype(bf16)
        row16 = lax.broadcasted_iota(jnp.int32, (16, 256), 0)
        lane16 = lax.broadcasted_iota(jnp.int32, (16, 256), 1) & 127
        mine = row16 == along + 4 * (lane16 >> 6)
        gather_ref[along] = jnp.where(mine, 1.0, 0.0).astype(bf16)

    def pick(block, target, first, last):
        for node in range(first, last):
            target[pl.ds(node, 1), :] = nodes_ref[pl.ds(row_ref[block, node], 1), :]

    def lay_out(block, side):
        turned = picked_refs[side][...].T
        part = part_ref[pl.ds(block, 1), :]
        fields = turned[0:16]
        for number in range(1, 8):
            fields = jnp.where(part == number, turned[16 * number : 16 * number + 16], fields)
        centre = pm_ref[:, BLK_DEV * ROWS : BLK_DEV * ROWS + ROWS]
        rows = [-fields[0:1]] + [fields[k + 1 : k + 2] - centre[k : k + 1] for k in range(3)]
        rows += [fields[k : k + 1] for k in range(4, NODE_FIELDS)]
        for number, value in enumerate(rows):
            field_refs[side][number] = jnp.broadcast_to(value, (8, 128))
        both = jnp.where(left, table_ref[block], table_ref[block + half])
        place_refs[side][...] = dot(both, spread_ref[...])

    def compute(side, start):
        rows = [field_refs[side][number] for number in range(NODE_FIELDS)]
        halves = [
            node_sum([place_refs[side][at : at + 8, 128 * k : 128 * k + 128] for k in range(3)], rows)
            for at in range(start, start + NODE_PART, 8)
        ]
        for number in range(3):
            pull = jnp.concatenate([half_[number] for half_ in halves], axis=0)
            high = pull.astype(bf16)
            pull_refs[side][number, start : start + NODE_PART, 0:128] = high
            pull_refs[side][number, start : start + NODE_PART, 128:256] = (pull - high.astype(f32)).astype(bf16)

    def add_up(block, side):
        total = jnp.zeros((16, ROWS), f32)
        for number in range(3):
            total += lax.dot_general(
                gather_ref[number],
                pull_refs[side][number],
                (((1,), (1,)), ((), ())),
                preferred_element_type=f32,
            )
        out_ref[block, 0:3] = local_ref[block, 0:3] + total[0:3]
        out_ref[block + half, 0:3] = local_ref[block + half, 0:3] + total[4:7]

    pick(0, picked_refs[0], 0, 2 * LIST_N)
    pick(1, picked_refs[1], 0, 2 * LIST_N)
    lay_out(0, 0)

    def step(index, carry):
        for side in range(2):
            block = index * 2 + side
            other = 1 - side
            lay_out(jnp.minimum(block + 1, half - 1), other)
            add_up(jnp.maximum(block - 1, 0), other)
            ahead = jnp.minimum(block + 2, half - 1)
            for start in range(0, ROWS, NODE_PART):
                compute(side, start)
                pick(ahead, picked_refs[side], start, start + NODE_PART)
        return carry

    lax.fori_loop(0, half // 2, step, 0)
    add_up(half - 1, 1)


def node_pull(rows, parts, pm, local, shares):
    devices, each = shares[0].shape[0:2]
    return pl.pallas_call(
        node_kernel,
        out_shape=jax.ShapeDtypeStruct((BLK_DEV, 4, ROWS), f32),
        in_specs=[SMEM] + [VMEM] * (3 + GROUP),
        out_specs=VMEM,
        scratch_shapes=[
            pltpu.VMEM((BLK_DEV, ROWS, 128), bf16),
            pltpu.VMEM((BLK_DEV, 16, ROWS), bf16),
            pltpu.VMEM((ROWS, 3 * 128), bf16),
            pltpu.VMEM((3, 16, 256), bf16),
            pltpu.VMEM((GROUP * devices * each, 128), f32),
        ]
        + [pltpu.VMEM((2 * LIST_N, 128), f32)] * 2
        + [pltpu.VMEM((NODE_FIELDS, 8, 128), f32)] * 2
        + [pltpu.VMEM((ROWS, 3 * 128), f32)] * 2
        + [pltpu.VMEM((3, ROWS, 256), bf16)] * 2,
        compiler_params=params(14),
        cost_estimate=pl.CostEstimate(flops=12 * 10**9, bytes_accessed=4 * 10**6, transcendentals=10**6),
        name="node_pull",
    )(rows, parts, pm, local, *shares)


def local_kernel(leaf_ref, pm_ref, out_ref, table_ref, weight_ref):
    fill_tables((pm_ref,), table_ref, weight_ref)
    left = left_lanes()

    def step(index, carry):
        results = []
        for place in range(STEP):
            block = index * STEP + place
            start = pl.multiple_of(block * ROWS, ROWS)
            leaves = [leaf_ref[k, block] for k in range(LEAF_N)]
            moved = pm_ref[0:3, pl.ds(start, ROWS)] * -0.5
            results.append(pull_block(moved, leaves, table_ref, weight_ref, left))
        for place in range(STEP):
            out_ref[index * STEP + place, 0:3] = results[place]
        return carry

    lax.fori_loop(0, BLK_DEV // STEP, step, 0)


def local_pull(local_leaves, pm):
    return pl.pallas_call(
        local_kernel,
        out_shape=jax.ShapeDtypeStruct((BLK_DEV, 4, ROWS), f32),
        in_specs=[SMEM, VMEM],
        out_specs=VMEM,
        scratch_shapes=[
            pltpu.VMEM((BLK_DEV, ROWS, 128), bf16),
            pltpu.VMEM((BLK_DEV, 16, ROWS), bf16),
        ],
        compiler_params=params(10),
        cost_estimate=pl.CostEstimate(flops=16 * 10**9, bytes_accessed=10**6, transcendentals=8 * 10**6),
        name="local_pull",
    )(local_leaves, pm)


def add_kernel(slot_ref, own_ref, back_ref, out_ref, *sum_refs):
    parts = len(sum_refs)
    for part in range(1, parts):
        sum_refs[part][...] = jnp.zeros_like(sum_refs[part])
    sum_refs[0][...] = own_ref[...]

    def one(step, carry):
        for part in range(parts):
            export = step * parts + part
            block = slot_ref[EXP_BLK + export]
            sum_refs[part][block] += back_ref[slot_ref[export]]
        return carry

    lax.fori_loop(0, EXP_BLK // parts, one, 0)
    for block in range(BLK_DEV):
        total = sum_refs[0][block]
        for part in range(1, parts):
            total = total + sum_refs[part][block]
        out_ref[:, block * ROWS : (block + 1) * ROWS] = total[0:3]


def add_returned(slots, own, back):
    return pl.pallas_call(
        add_kernel,
        out_shape=jax.ShapeDtypeStruct((3, BLK_DEV * ROWS), f32),
        in_specs=[SMEM, VMEM, VMEM],
        out_specs=VMEM,
        scratch_shapes=[pltpu.VMEM((BLK_DEV, 4, ROWS), f32)] * 4,
        compiler_params=params(16),
        name="add_returned",
    )(slots, own, back)


def swap(values):
    return lax.all_to_all(values, AXES, split_axis=0, concat_axis=0, tiled=True)


def per_device(
    positions,
    masses,
    node_mass,
    node_centre,
    node_quad,
    local_leaves,
    node_lists,
    export_block,
    export_dest,
    export_leaves,
):
    groups = lax.axis_size("wide")
    members = lax.axis_size("narrow")
    devices = groups * members

    def same_core(value):
        flips = [[(i, i ^ flip) for i in range(members)] for flip in (1, 4, 5)]
        return [value] + [lax.ppermute(value, "narrow", flip) for flip in flips]

    def other_core(values):
        return values + [lax.ppermute(value, "wide", [(i, i ^ 1) for i in range(groups)]) for value in values]

    outgoing, slots, pm, rows, parts = send_blocks(
        devices,
        export_block,
        export_dest[:, 0],
        export_leaves.T,
        positions,
        masses[None],
        node_mass[None],
        node_centre,
        node_quad,
        node_lists,
    )
    arrived = swap(outgoing)
    pms = same_core(pm)
    local = local_pull(local_leaves.T, pm)
    arrived, local, pms = lax.optimization_barrier((arrived, local, pms))
    pms = other_core(pms)

    shares = same_core(arrived[:, CAP])
    visitors = arrived.reshape(devices * (CAP + 1), 4, ROWS)
    pulls = remote_pull(visitors, pms)
    pulls, local, shares = lax.optimization_barrier((pulls, local, shares))
    back = swap(pulls)
    shares = other_core(shares)
    own = node_pull(rows, parts, pm, local, shares)
    return add_returned(slots, own, back.reshape(devices * CAP, 4, ROWS))


def solution(mesh):
    both = P(AXES)
    lanes = P(None, AXES)
    rows = P(AXES, None)
    return jax.shard_map(
        per_device,
        mesh=mesh,
        in_specs=(lanes, both, both, lanes, lanes, rows, rows, both, rows, rows),
        out_specs=lanes,
        check_vma=False,
    )
```

```python
import functools

import jax
import jax.numpy as jnp
from jax import lax
from jax.experimental import pallas as pl
from jax.experimental.pallas import tpu as pltpu
from jax.sharding import PartitionSpec as P

ROWS = 128
LEAF_N = 8
LIST_N = 64
CAP = 2
BLK_DEV = 64
EXP_BLK = 128
AXES = ("wide", "narrow")
GROUP = 8
STEP = 16
TAIL = 8
NODE_FIELDS = 10
SOFTEN = 0.01

f32 = jnp.float32
bf16 = jnp.bfloat16
VMEM = pl.BlockSpec(memory_space=pltpu.VMEM)
SMEM = pl.BlockSpec(memory_space=pltpu.SMEM)
HBM = pl.BlockSpec(memory_space=pltpu.HBM)


def params(mib):
    return pltpu.CompilerParams(vmem_limit_bytes=mib * 2**20)


def split3(value):
    high = value.astype(bf16)
    rest = value - high.astype(f32)
    middle = rest.astype(bf16)
    low = (rest - middle.astype(f32)).astype(bf16)
    return high, middle, low


def dot(left, right):
    return jnp.dot(left, right, preferred_element_type=f32)


def fetch(sources, targets, sems):
    copies = [
        pltpu.make_async_copy(source, target, sems.at[number])
        for number, (source, target) in enumerate(zip(sources, targets))
    ]
    for copy in copies:
        copy.start()
    return copies


def node_rows(mass, centre, quad, nodes, devices):
    count = mass.shape[1]
    rows = count // 8
    fields = jnp.concatenate([mass, centre, quad, jnp.zeros((16 - NODE_FIELDS, count), f32)], axis=0)
    parts = [fields[:, part * rows : (part + 1) * rows] for part in range(8)]
    half = BLK_DEV // 2
    nodes = jnp.concatenate([nodes[0:half], nodes[half:]], axis=1)
    bits = rows.bit_length() - 1
    each = rows // GROUP
    share = (nodes & (rows - 1)) // each
    row = (share * devices + (nodes >> (bits + 3))) * each + (nodes & (each - 1))
    return jnp.concatenate(parts, axis=0).T, row, (nodes >> bits) & 7


def send_kernel(
    block_in, dest_in, leaf_in, pos_in, mass_in, node_mass_in, node_centre_in, node_quad_in, list_in,
    out_ref, slot_ref, pm_ref, row_ref, part_ref,
    block_ref, dest_ref, leaf_ref, pos_ref, mass_ref, node_mass_ref, node_centre_ref, node_quad_ref, list_ref,
    count_ref, ids_ref, sems,
):
    copies = fetch(
        (block_in, dest_in, leaf_in, pos_in, mass_in, node_mass_in, node_centre_in, node_quad_in, list_in),
        (
            block_ref, dest_ref, leaf_ref, pos_ref, mass_ref,
            node_mass_ref, node_centre_ref, node_quad_ref, list_ref,
        ),
        sems,
    )
    devices = out_ref.shape[0]
    shift = lax.axis_size("narrow").bit_length() - 1
    turn = lax.axis_index("narrow")
    out_ref[:, 0:CAP, 3:4, :] = jnp.full((devices, CAP, 1, ROWS), -1.0, f32)

    def clear(index, carry):
        for part in range(8):
            count_ref[index * 8 + part] = 0
        return carry

    lax.fori_loop(0, devices // 8, clear, 0)
    for copy in copies:
        copy.wait()
    table, row_ref[...], part_ref[...] = node_rows(
        node_mass_ref[...], node_centre_ref[...], node_quad_ref[...], list_ref[...], devices
    )
    each = table.shape[0] // GROUP
    for device in range(devices):
        member = (device & 1) + ((device >> 2) & 1) * 2 + ((device >> shift) & 1) * 4
        out_ref[device, CAP] = table[member * each : (member + 1) * each]
    size = pos_ref.shape[1]
    centre = jnp.sum(pos_ref[...], axis=1, keepdims=True) * (1.0 / size)
    moved = pos_ref[...] - centre
    square = jnp.sum(moved * moved, axis=0, keepdims=True)
    mass = mass_ref[...]
    pm_ref[:, 0:size] = jnp.concatenate([-2.0 * moved, square, mass * moved, mass], axis=0)
    pm_ref[:, size : size + ROWS] = jnp.broadcast_to(
        jnp.concatenate([centre, jnp.zeros((5, 1), f32)], axis=0), (8, ROWS)
    )
    ids_ref[...] = jnp.concatenate([leaf_ref[...].astype(f32)] * (ROWS // LEAF_N), axis=0).T

    def one(step, carry):
        for part in range(8):
            export = step * 8 + part
            dest = dest_ref[export]
            side, up, core = dest & 1, (dest >> 2) & 1, (dest >> shift) & 1
            base = dest - side - up * 4 - (core << shift)
            seen = count_ref[base]
            count_ref[base] = seen + 1
            member = (seen + turn) & (GROUP - 1)
            slot = seen >> 3
            target = base + (member & 1) + (member & 2) * 2 + ((member >> 2) << shift)
            distance = (side + up * 2 + core * 4) ^ member
            slot_ref[export] = target * CAP + slot
            slot_ref[EXP_BLK + export] = block_ref[export]
            start = pl.multiple_of(block_ref[export] * ROWS, ROWS)
            out_ref[target, slot, 0:3, :] = pos_ref[:, pl.ds(start, ROWS)]
            ids = ids_ref[pl.ds(export, 1), 0:LEAF_N]
            out_ref[target, slot, 3:4, 0:LEAF_N] = ids + (distance * BLK_DEV).astype(f32)
        return carry

    lax.fori_loop(0, EXP_BLK // 8, one, 0)


def send_blocks(devices, *arguments):
    lists = arguments[-1]
    half = (lists.shape[0] // 2, lists.shape[1] * 2)
    return pl.pallas_call(
        send_kernel,
        out_shape=(
            jax.ShapeDtypeStruct((devices, CAP + 1, 4, ROWS), f32),
            jax.ShapeDtypeStruct((2 * EXP_BLK,), jnp.int32),
            jax.ShapeDtypeStruct((8, BLK_DEV * ROWS + ROWS), f32),
            jax.ShapeDtypeStruct(half, jnp.int32),
            jax.ShapeDtypeStruct(half, jnp.int32),
        ),
        in_specs=[HBM] * len(arguments),
        out_specs=(VMEM, SMEM, VMEM, VMEM, VMEM),
        scratch_shapes=[
            pltpu.SMEM((EXP_BLK,), jnp.int32),
            pltpu.SMEM((EXP_BLK,), jnp.int32),
        ]
        + [pltpu.VMEM(value.shape, value.dtype) for value in arguments[2:]]
        + [
            pltpu.SMEM((devices,), jnp.int32),
            pltpu.VMEM((EXP_BLK, 128), f32),
            pltpu.SemaphoreType.DMA((len(arguments),)),
        ],
        compiler_params=params(56),
        name="send_blocks",
    )(*arguments)


def fill_tables(source_refs, table_ref, weight_ref):
    chunk = 32 if len(source_refs) == 1 else 8
    row = lax.broadcasted_iota(jnp.int32, (16, ROWS), 0)
    ones = jnp.where(row < 3, 1.0, 0.0).astype(bf16)

    def step(index, carry):
        start = pl.multiple_of(index * (chunk * ROWS), chunk * ROWS)
        for group, source_ref in enumerate(source_refs):
            rows = source_ref[:, pl.ds(start, chunk * ROWS)]
            for part in range(chunk):
                leaf = group * BLK_DEV + index * chunk + part
                high, middle, low = split3(rows[:, part * ROWS : (part + 1) * ROWS])
                half = [high, high, middle, middle, high, low, ones]
                table_ref[leaf] = jnp.concatenate(half + half, axis=0).T
                weight_ref[leaf] = jnp.concatenate([high, middle], axis=0)
        return carry

    lax.fori_loop(0, BLK_DEV // chunk, step, 0)


def pull_block(moved, leaves, table_ref, weight_ref, left):
    square = jnp.sum(moved * moved, axis=0, keepdims=True) + SOFTEN
    one = jnp.ones_like(square)
    none = jnp.zeros((4, ROWS), f32)
    high, middle, low = split3(jnp.concatenate([moved, one, none], axis=0))
    pieces = [piece.astype(f32) for piece in split3(square)]
    ends = jnp.concatenate(pieces + [none, none, none, one - one], axis=0).astype(bf16)
    half = jnp.concatenate([high, middle, high, middle, low, high, ends], axis=0)
    none = jnp.zeros_like(half)
    right = jnp.concatenate(
        [jnp.concatenate([half, none], axis=1), jnp.concatenate([none, half], axis=1)], axis=0
    )
    total = jnp.zeros((16, ROWS), f32)
    for pair in range(LEAF_N // 2):
        first, second = leaves[2 * pair], leaves[2 * pair + 1]
        spread = dot(jnp.where(left, table_ref[first], table_ref[second]), right)
        root = lax.rsqrt(spread)
        cubed = root * root * root
        high = cubed.astype(bf16)
        low = (cubed - high.astype(f32)).astype(bf16)
        for place, leaf in enumerate((first, second)):
            lanes = slice(place * ROWS, (place + 1) * ROWS)
            weight = weight_ref[leaf]
            total += dot(
                jnp.concatenate([weight, weight], axis=1),
                jnp.concatenate([high[:, lanes], low[:, lanes]], axis=0),
            )
    total = total[4:8] + total[12:16]
    return total[0:3] - moved * total[3:4]


def left_lanes():
    return lax.broadcasted_iota(jnp.int32, (ROWS, 128), 1) < 64


def remote_kernel(pos_ref, *refs):
    pm_refs = refs[:GROUP]
    out_ref, list_ref, leaf_ref, centre_ref, table_ref, weight_ref, sem = refs[GROUP:]
    devices = pos_ref.shape[0] // (CAP + 1)
    copy = pltpu.make_async_copy(pos_ref.at[:, 3], leaf_ref, sem)
    copy.start()
    size = BLK_DEV * ROWS
    for group, pm_ref in enumerate(pm_refs):
        centre_ref[group] = pm_ref[:, size : size + ROWS]
    fill_tables(pm_refs, table_ref, weight_ref)
    copy.wait()

    def note(index, found):
        for part in range(8):
            for slot in range(CAP):
                slot = (index * 8 + part) * (CAP + 1) + slot
                list_ref[found] = slot
                found = found + jnp.where(leaf_ref[slot, 0] >= 0.0, 1, 0)
        return found

    found = lax.fori_loop(0, devices // 8, note, 0)
    last = list_ref[jnp.maximum(found - 1, 0)]
    for place in range(TAIL):
        list_ref[found + place] = last
    left = left_lanes()

    def visits(start, count):
        results = []
        for place in range(count):
            slot = list_ref[start + place]
            leaves = [leaf_ref[slot, k].astype(jnp.int32) for k in range(LEAF_N)]
            moved = pos_ref[slot][0:3] - centre_ref[leaves[0] // BLK_DEV][0:3]
            results.append((slot, pull_block(moved, leaves, table_ref, weight_ref, left)))
        for slot, result in results:
            out_ref[slot // (CAP + 1), slot % (CAP + 1), 0:3] = result

    def step(index, carry):
        visits(index * STEP, STEP)
        return carry

    def tail(index, carry):
        visits(whole * STEP + index * TAIL, TAIL)
        return carry

    whole = found // STEP
    lax.fori_loop(0, whole, step, 0)
    lax.fori_loop(0, (found - whole * STEP + TAIL - 1) // TAIL, tail, 0)


def remote_pull(visitors, pms):
    devices = visitors.shape[0] // (CAP + 1)
    return pl.pallas_call(
        remote_kernel,
        out_shape=jax.ShapeDtypeStruct((devices, CAP, 4, ROWS), f32),
        in_specs=[VMEM] * (1 + GROUP),
        out_specs=VMEM,
        scratch_shapes=[
            pltpu.SMEM((devices * CAP + TAIL,), jnp.int32),
            pltpu.SMEM((visitors.shape[0], ROWS), f32),
            pltpu.VMEM((GROUP, 8, ROWS), f32),
            pltpu.VMEM((GROUP * BLK_DEV, ROWS, 128), bf16),
            pltpu.VMEM((GROUP * BLK_DEV, 16, ROWS), bf16),
            pltpu.SemaphoreType.DMA,
        ],
        compiler_params=params(28),
        cost_estimate=pl.CostEstimate(flops=32 * 10**9, bytes_accessed=10**7, transcendentals=16 * 10**6),
        name="remote_pull",
    )(visitors, *pms)


def node_sum(place, fields):
    mass, cx, cy, cz, qxx, qyy, qzz, qxy, qxz, qyz = fields
    x, y, z = place[0] - cx, place[1] - cy, place[2] - cz
    spread = x * x + y * y + (z * z + SOFTEN)
    quad_x = qxx * x + qxy * y + qxz * z
    quad_y = qxy * x + qyy * y + qyz * z
    quad_z = qxz * x + qyz * y + qzz * z
    root = lax.rsqrt(spread)
    inverse = root * root
    cubed = inverse * root
    fifth = cubed * inverse
    scalar = x * quad_x + y * quad_y + z * quad_z
    radial = mass * cubed + scalar * (fifth * (-2.5 * inverse))
    return radial * x + quad_x * fifth, radial * y + quad_y * fifth, radial * z + quad_z * fifth


NODE_PART = 16


def node_kernel(
    row_ref, part_ref, pm_ref, local_ref, *refs,
):
    half = BLK_DEV // 2
    share_refs, (out_ref, table_ref, weight_ref, spread_ref, gather_ref, nodes_ref) = refs[:GROUP], refs[GROUP : GROUP + 6]
    refs = refs[GROUP + 6 :]
    picked_refs, field_refs, place_refs, pull_refs = refs[0:2], refs[2:4], refs[4:6], refs[6:8]
    narrow = lax.axis_index("narrow")
    here = (narrow & 1) + ((narrow >> 2) & 1) * 2 + (lax.axis_index("wide") & 1) * 4
    devices, each = share_refs[0].shape[0], share_refs[0].shape[1]
    for distance, share_ref in enumerate(share_refs):
        first = pl.multiple_of((here ^ distance) * (devices * each), devices * each)
        for device in range(0, devices, 2):
            nodes_ref[pl.ds(first + device * each, 2 * each), :] = jnp.concatenate(
                [share_ref[device], share_ref[device + 1]], axis=0
            )
    fill_tables((pm_ref,), table_ref, weight_ref)
    left = left_lanes()

    row = lax.broadcasted_iota(jnp.int32, (ROWS, 128), 0)
    lane = lax.broadcasted_iota(jnp.int32, (ROWS, 128), 1)
    for along in range(3):
        inner = row & 63
        hit = (inner == along) | (inner == 16 + along) | (inner == 40 + along)
        hit = hit & ((row >> 6) == (lane >> 6))
        spread_ref[:, 128 * along : 128 * along + 128] = jnp.where(hit, -0.5, 0.0).astype(bf16)
        row16 = lax.broadcasted_iota(jnp.int32, (16, 256), 0)
        lane16 = lax.broadcasted_iota(jnp.int32, (16, 256), 1) & 127
        mine = row16 == along + 4 * (lane16 >> 6)
        gather_ref[along] = jnp.where(mine, 1.0, 0.0).astype(bf16)

    def pick(block, target, first, last):
        for node in range(first, last):
            target[pl.ds(node, 1), :] = nodes_ref[pl.ds(row_ref[block, node], 1), :]

    def lay_out(block, side):
        turned = picked_refs[side][...].T
        part = part_ref[pl.ds(block, 1), :]
        fields = turned[0:16]
        for number in range(1, 8):
            fields = jnp.where(part == number, turned[16 * number : 16 * number + 16], fields)
        centre = pm_ref[:, BLK_DEV * ROWS : BLK_DEV * ROWS + ROWS]
        rows = [-fields[0:1]] + [fields[k + 1 : k + 2] - centre[k : k + 1] for k in range(3)]
        rows += [fields[k : k + 1] for k in range(4, NODE_FIELDS)]
        for number, value in enumerate(rows):
            field_refs[side][number] = jnp.broadcast_to(value, (8, 128))
        both = jnp.where(left, table_ref[block], table_ref[block + half])
        place_refs[side][...] = dot(both, spread_ref[...])

    def compute(side, start):
        rows = [field_refs[side][number] for number in range(NODE_FIELDS)]
        halves = [
            node_sum([place_refs[side][at : at + 8, 128 * k : 128 * k + 128] for k in range(3)], rows)
            for at in range(start, start + NODE_PART, 8)
        ]
        for number in range(3):
            pull = jnp.concatenate([half_[number] for half_ in halves], axis=0)
            high = pull.astype(bf16)
            pull_refs[side][number, start : start + NODE_PART, 0:128] = high
            pull_refs[side][number, start : start + NODE_PART, 128:256] = (pull - high.astype(f32)).astype(bf16)

    def add_up(block, side):
        total = jnp.zeros((16, ROWS), f32)
        for number in range(3):
            total += lax.dot_general(
                gather_ref[number],
                pull_refs[side][number],
                (((1,), (1,)), ((), ())),
                preferred_element_type=f32,
            )
        out_ref[block, 0:3] = local_ref[block, 0:3] + total[0:3]
        out_ref[block + half, 0:3] = local_ref[block + half, 0:3] + total[4:7]

    pick(0, picked_refs[0], 0, 2 * LIST_N)
    pick(1, picked_refs[1], 0, 2 * LIST_N)
    lay_out(0, 0)

    def step(index, carry):
        for side in range(2):
            block = index * 2 + side
            other = 1 - side
            lay_out(jnp.minimum(block + 1, half - 1), other)
            add_up(jnp.maximum(block - 1, 0), other)
            ahead = jnp.minimum(block + 2, half - 1)
            for start in range(0, ROWS, NODE_PART):
                compute(side, start)
                pick(ahead, picked_refs[side], start, start + NODE_PART)
        return carry

    lax.fori_loop(0, half // 2, step, 0)
    add_up(half - 1, 1)


def node_pull(rows, parts, pm, local, shares):
    devices, each = shares[0].shape[0:2]
    return pl.pallas_call(
        node_kernel,
        out_shape=jax.ShapeDtypeStruct((BLK_DEV, 4, ROWS), f32),
        in_specs=[SMEM] + [VMEM] * (3 + GROUP),
        out_specs=VMEM,
        scratch_shapes=[
            pltpu.VMEM((BLK_DEV, ROWS, 128), bf16),
            pltpu.VMEM((BLK_DEV, 16, ROWS), bf16),
            pltpu.VMEM((ROWS, 3 * 128), bf16),
            pltpu.VMEM((3, 16, 256), bf16),
            pltpu.VMEM((GROUP * devices * each, 128), f32),
        ]
        + [pltpu.VMEM((2 * LIST_N, 128), f32)] * 2
        + [pltpu.VMEM((NODE_FIELDS, 8, 128), f32)] * 2
        + [pltpu.VMEM((ROWS, 3 * 128), f32)] * 2
        + [pltpu.VMEM((3, ROWS, 256), bf16)] * 2,
        compiler_params=params(14),
        cost_estimate=pl.CostEstimate(flops=12 * 10**9, bytes_accessed=4 * 10**6, transcendentals=10**6),
        name="node_pull",
    )(rows, parts, pm, local, *shares)


def local_kernel(leaf_ref, pm_ref, out_ref, table_ref, weight_ref):
    fill_tables((pm_ref,), table_ref, weight_ref)
    left = left_lanes()

    def step(index, carry):
        results = []
        for place in range(STEP):
            block = index * STEP + place
            start = pl.multiple_of(block * ROWS, ROWS)
            leaves = [leaf_ref[k, block] for k in range(LEAF_N)]
            moved = pm_ref[0:3, pl.ds(start, ROWS)] * -0.5
            results.append(pull_block(moved, leaves, table_ref, weight_ref, left))
        for place in range(STEP):
            out_ref[index * STEP + place, 0:3] = results[place]
        return carry

    lax.fori_loop(0, BLK_DEV // STEP, step, 0)


def local_pull(local_leaves, pm):
    return pl.pallas_call(
        local_kernel,
        out_shape=jax.ShapeDtypeStruct((BLK_DEV, 4, ROWS), f32),
        in_specs=[SMEM, VMEM],
        out_specs=VMEM,
        scratch_shapes=[
            pltpu.VMEM((BLK_DEV, ROWS, 128), bf16),
            pltpu.VMEM((BLK_DEV, 16, ROWS), bf16),
        ],
        compiler_params=params(10),
        cost_estimate=pl.CostEstimate(flops=16 * 10**9, bytes_accessed=10**6, transcendentals=8 * 10**6),
        name="local_pull",
    )(local_leaves, pm)


def add_kernel(slot_ref, own_ref, back_ref, out_ref, *sum_refs):
    parts = len(sum_refs)
    for part in range(1, parts):
        sum_refs[part][...] = jnp.zeros_like(sum_refs[part])
    sum_refs[0][...] = own_ref[...]

    def one(step, carry):
        for part in range(parts):
            export = step * parts + part
            block = slot_ref[EXP_BLK + export]
            sum_refs[part][block] += back_ref[slot_ref[export]]
        return carry

    lax.fori_loop(0, EXP_BLK // parts, one, 0)
    for block in range(BLK_DEV):
        total = sum_refs[0][block]
        for part in range(1, parts):
            total = total + sum_refs[part][block]
        out_ref[:, block * ROWS : (block + 1) * ROWS] = total[0:3]


def add_returned(slots, own, back):
    return pl.pallas_call(
        add_kernel,
        out_shape=jax.ShapeDtypeStruct((3, BLK_DEV * ROWS), f32),
        in_specs=[SMEM, VMEM, VMEM],
        out_specs=VMEM,
        scratch_shapes=[pltpu.VMEM((BLK_DEV, 4, ROWS), f32)] * 4,
        compiler_params=params(16),
        name="add_returned",
    )(slots, own, back)


def swap(values):
    return lax.all_to_all(values, AXES, split_axis=0, concat_axis=0, tiled=True)


def per_device(
    positions,
    masses,
    node_mass,
    node_centre,
    node_quad,
    local_leaves,
    node_lists,
    export_block,
    export_dest,
    export_leaves,
):
    groups = lax.axis_size("wide")
    members = lax.axis_size("narrow")
    devices = groups * members

    def same_core(value):
        flips = [[(i, i ^ flip) for i in range(members)] for flip in (1, 4, 5)]
        return [value] + [lax.ppermute(value, "narrow", flip) for flip in flips]

    def other_core(values):
        return values + [lax.ppermute(value, "wide", [(i, i ^ 1) for i in range(groups)]) for value in values]

    outgoing, slots, pm, rows, parts = send_blocks(
        devices,
        export_block,
        export_dest[:, 0],
        export_leaves.T,
        positions,
        masses[None],
        node_mass[None],
        node_centre,
        node_quad,
        node_lists,
    )
    arrived = swap(outgoing)
    pms = same_core(pm)
    local = local_pull(local_leaves.T, pm)
    arrived, local, pms = lax.optimization_barrier((arrived, local, pms))
    pms = other_core(pms)

    shares = same_core(arrived[:, CAP])
    visitors = arrived.reshape(devices * (CAP + 1), 4, ROWS)
    pulls = remote_pull(visitors, pms)
    pulls, local, shares = lax.optimization_barrier((pulls, local, shares))
    back = swap(pulls)
    shares = other_core(shares)
    own = node_pull(rows, parts, pm, local, shares)
    return add_returned(slots, own, back.reshape(devices * CAP, 4, ROWS))


def solution(mesh):
    both = P(AXES)
    lanes = P(None, AXES)
    rows = P(AXES, None)
    return jax.shard_map(
        per_device,
        mesh=mesh,
        in_specs=(lanes, both, both, lanes, lanes, rows, rows, both, rows, rows),
        out_specs=lanes,
        check_vma=False,
    )
```

```python
import functools

import jax
import jax.numpy as jnp
from jax import lax
from jax.experimental import pallas as pl
from jax.experimental.pallas import tpu as pltpu
from jax.sharding import PartitionSpec as P

ROWS = 128
LEAF_N = 8
LIST_N = 64
CAP = 2
BLK_DEV = 64
EXP_BLK = 128
AXES = ("wide", "narrow")
GROUP = 8
STEP = 16
TAIL = 8
REMOTE_STEPS = (32, 16, 8)
NODE_FIELDS = 10
SOFTEN = 0.01

f32 = jnp.float32
bf16 = jnp.bfloat16
VMEM = pl.BlockSpec(memory_space=pltpu.VMEM)
SMEM = pl.BlockSpec(memory_space=pltpu.SMEM)
HBM = pl.BlockSpec(memory_space=pltpu.HBM)


def params(mib):
    return pltpu.CompilerParams(vmem_limit_bytes=mib * 2**20)


def split3(value):
    high = value.astype(bf16)
    rest = value - high.astype(f32)
    middle = rest.astype(bf16)
    low = (rest - middle.astype(f32)).astype(bf16)
    return high, middle, low


def dot(left, right):
    return jnp.dot(left, right, preferred_element_type=f32)


def fetch(sources, targets, sems):
    copies = [
        pltpu.make_async_copy(source, target, sems.at[number])
        for number, (source, target) in enumerate(zip(sources, targets))
    ]
    for copy in copies:
        copy.start()
    return copies


def node_rows(mass, centre, quad, nodes, devices):
    count = mass.shape[1]
    rows = count // 8
    fields = jnp.concatenate([mass, centre, quad, jnp.zeros((16 - NODE_FIELDS, count), f32)], axis=0)
    parts = [fields[:, part * rows : (part + 1) * rows] for part in range(8)]
    half = BLK_DEV // 2
    nodes = jnp.concatenate([nodes[0:half], nodes[half:]], axis=1)
    bits = rows.bit_length() - 1
    each = rows // GROUP
    share = (nodes & (rows - 1)) // each
    row = (share * devices + (nodes >> (bits + 3))) * each + (nodes & (each - 1))
    return jnp.concatenate(parts, axis=0).T, row, (nodes >> bits) & 7


def send_kernel(
    block_in, dest_in, leaf_in, pos_in, mass_in, node_mass_in, node_centre_in, node_quad_in, list_in,
    out_ref, slot_ref, pm_ref, row_ref, part_ref,
    block_ref, dest_ref, leaf_ref, pos_ref, mass_ref, node_mass_ref, node_centre_ref, node_quad_ref, list_ref,
    count_ref, ids_ref, sems,
):
    copies = fetch(
        (block_in, dest_in, leaf_in, pos_in, mass_in, node_mass_in, node_centre_in, node_quad_in, list_in),
        (
            block_ref, dest_ref, leaf_ref, pos_ref, mass_ref,
            node_mass_ref, node_centre_ref, node_quad_ref, list_ref,
        ),
        sems,
    )
    devices = out_ref.shape[0]
    shift = lax.axis_size("narrow").bit_length() - 1
    turn = lax.axis_index("narrow")
    out_ref[:, 0:CAP, 3:4, :] = jnp.full((devices, CAP, 1, ROWS), -1.0, f32)

    def clear(index, carry):
        for part in range(8):
            count_ref[index * 8 + part] = 0
        return carry

    lax.fori_loop(0, devices // 8, clear, 0)
    for copy in copies:
        copy.wait()
    table, row_ref[...], part_ref[...] = node_rows(
        node_mass_ref[...], node_centre_ref[...], node_quad_ref[...], list_ref[...], devices
    )
    each = table.shape[0] // GROUP
    for device in range(devices):
        member = (device & 1) + ((device >> 2) & 1) * 2 + ((device >> shift) & 1) * 4
        out_ref[device, CAP] = table[member * each : (member + 1) * each]
    size = pos_ref.shape[1]
    centre = jnp.sum(pos_ref[...], axis=1, keepdims=True) * (1.0 / size)
    moved = pos_ref[...] - centre
    square = jnp.sum(moved * moved, axis=0, keepdims=True)
    mass = mass_ref[...]
    pm_ref[:, 0:size] = jnp.concatenate([-2.0 * moved, square, mass * moved, mass], axis=0)
    pm_ref[:, size : size + ROWS] = jnp.broadcast_to(
        jnp.concatenate([centre, jnp.zeros((5, 1), f32)], axis=0), (8, ROWS)
    )
    ids_ref[...] = jnp.concatenate([leaf_ref[...].astype(f32)] * (ROWS // LEAF_N), axis=0).T

    def one(step, carry):
        for part in range(8):
            export = step * 8 + part
            dest = dest_ref[export]
            side, up, core = dest & 1, (dest >> 2) & 1, (dest >> shift) & 1
            base = dest - side - up * 4 - (core << shift)
            seen = count_ref[base]
            count_ref[base] = seen + 1
            member = (seen + turn) & (GROUP - 1)
            slot = seen >> 3
            target = base + (member & 1) + (member & 2) * 2 + ((member >> 2) << shift)
            distance = (side + up * 2 + core * 4) ^ member
            slot_ref[export] = target * CAP + slot
            slot_ref[EXP_BLK + export] = block_ref[export]
            start = pl.multiple_of(block_ref[export] * ROWS, ROWS)
            out_ref[target, slot, 0:3, :] = pos_ref[:, pl.ds(start, ROWS)]
            ids = ids_ref[pl.ds(export, 1), 0:LEAF_N]
            out_ref[target, slot, 3:4, 0:LEAF_N] = ids + (distance * BLK_DEV).astype(f32)
        return carry

    lax.fori_loop(0, EXP_BLK // 8, one, 0)


def send_blocks(devices, *arguments):
    lists = arguments[-1]
    half = (lists.shape[0] // 2, lists.shape[1] * 2)
    return pl.pallas_call(
        send_kernel,
        out_shape=(
            jax.ShapeDtypeStruct((devices, CAP + 1, 4, ROWS), f32),
            jax.ShapeDtypeStruct((2 * EXP_BLK,), jnp.int32),
            jax.ShapeDtypeStruct((8, BLK_DEV * ROWS + ROWS), f32),
            jax.ShapeDtypeStruct(half, jnp.int32),
            jax.ShapeDtypeStruct(half, jnp.int32),
        ),
        in_specs=[HBM] * len(arguments),
        out_specs=(VMEM, SMEM, VMEM, VMEM, VMEM),
        scratch_shapes=[
            pltpu.SMEM((EXP_BLK,), jnp.int32),
            pltpu.SMEM((EXP_BLK,), jnp.int32),
        ]
        + [pltpu.VMEM(value.shape, value.dtype) for value in arguments[2:]]
        + [
            pltpu.SMEM((devices,), jnp.int32),
            pltpu.VMEM((EXP_BLK, 128), f32),
            pltpu.SemaphoreType.DMA((len(arguments),)),
        ],
        compiler_params=params(56),
        name="send_blocks",
    )(*arguments)


def fill_tables(source_refs, table_ref, weight_ref):
    chunk = 32 if len(source_refs) == 1 else 8
    row = lax.broadcasted_iota(jnp.int32, (16, ROWS), 0)
    ones = jnp.where(row < 3, 1.0, 0.0).astype(bf16)

    def step(index, carry):
        start = pl.multiple_of(index * (chunk * ROWS), chunk * ROWS)
        for group, source_ref in enumerate(source_refs):
            rows = source_ref[:, pl.ds(start, chunk * ROWS)]
            for part in range(chunk):
                leaf = group * BLK_DEV + index * chunk + part
                high, middle, low = split3(rows[:, part * ROWS : (part + 1) * ROWS])
                half = [high, high, middle, middle, high, low, ones]
                table_ref[leaf] = jnp.concatenate(half + half, axis=0).T
                weight_ref[leaf] = jnp.concatenate([high, middle], axis=0)
        return carry

    lax.fori_loop(0, BLK_DEV // chunk, step, 0)


def pull_block(moved, leaves, table_ref, weight_ref, left):
    square = jnp.sum(moved * moved, axis=0, keepdims=True) + SOFTEN
    one = jnp.ones_like(square)
    none = jnp.zeros((4, ROWS), f32)
    high, middle, low = split3(jnp.concatenate([moved, one, none], axis=0))
    pieces = [piece.astype(f32) for piece in split3(square)]
    ends = jnp.concatenate(pieces + [none, none, none, one - one], axis=0).astype(bf16)
    half = jnp.concatenate([high, middle, high, middle, low, high, ends], axis=0)
    none = jnp.zeros_like(half)
    right = jnp.concatenate(
        [jnp.concatenate([half, none], axis=1), jnp.concatenate([none, half], axis=1)], axis=0
    )
    total = jnp.zeros((16, ROWS), f32)
    for pair in range(LEAF_N // 2):
        first, second = leaves[2 * pair], leaves[2 * pair + 1]
        spread = dot(jnp.where(left, table_ref[first], table_ref[second]), right)
        root = lax.rsqrt(spread)
        cubed = root * root * root
        high = cubed.astype(bf16)
        low = (cubed - high.astype(f32)).astype(bf16)
        for place, leaf in enumerate((first, second)):
            lanes = slice(place * ROWS, (place + 1) * ROWS)
            weight = weight_ref[leaf]
            total += dot(
                jnp.concatenate([weight, weight], axis=1),
                jnp.concatenate([high[:, lanes], low[:, lanes]], axis=0),
            )
    total = total[4:8] + total[12:16]
    return total[0:3] - moved * total[3:4]


def left_lanes():
    return lax.broadcasted_iota(jnp.int32, (ROWS, 128), 1) < 64


def remote_kernel(pos_ref, *refs):
    pm_refs = refs[:GROUP]
    out_ref, list_ref, leaf_ref, centre_ref, table_ref, weight_ref, sem = refs[GROUP:]
    devices = pos_ref.shape[0] // (CAP + 1)
    copy = pltpu.make_async_copy(pos_ref.at[:, 3], leaf_ref, sem)
    copy.start()
    size = BLK_DEV * ROWS
    for group, pm_ref in enumerate(pm_refs):
        centre_ref[group] = pm_ref[:, size : size + ROWS]
    fill_tables(pm_refs, table_ref, weight_ref)
    copy.wait()

    def note(index, found):
        for part in range(8):
            for slot in range(CAP):
                slot = (index * 8 + part) * (CAP + 1) + slot
                list_ref[found] = slot
                found = found + jnp.where(leaf_ref[slot, 0] >= 0.0, 1, 0)
        return found

    found = lax.fori_loop(0, devices // 8, note, 0)
    last = list_ref[jnp.maximum(found - 1, 0)]
    for place in range(TAIL):
        list_ref[found + place] = last
    left = left_lanes()

    def visits(start, count):
        results = []
        for place in range(count):
            slot = list_ref[start + place]
            leaves = [leaf_ref[slot, k].astype(jnp.int32) for k in range(LEAF_N)]
            moved = pos_ref[slot][0:3] - centre_ref[leaves[0] // BLK_DEV][0:3]
            results.append((slot, pull_block(moved, leaves, table_ref, weight_ref, left)))
        for slot, result in results:
            out_ref[slot // (CAP + 1), slot % (CAP + 1), 0:3] = result

    done = 0
    for count in REMOTE_STEPS:
        left_over = found - done
        steps = left_over // count if count > TAIL else (left_over + count - 1) // count

        def step(index, carry, start=done, count=count):
            visits(start + index * count, count)
            return carry

        lax.fori_loop(0, steps, step, 0)
        done = done + steps * count


def remote_pull(visitors, pms):
    devices = visitors.shape[0] // (CAP + 1)
    return pl.pallas_call(
        remote_kernel,
        out_shape=jax.ShapeDtypeStruct((devices, CAP, 4, ROWS), f32),
        in_specs=[VMEM] * (1 + GROUP),
        out_specs=VMEM,
        scratch_shapes=[
            pltpu.SMEM((devices * CAP + TAIL,), jnp.int32),
            pltpu.SMEM((visitors.shape[0], ROWS), f32),
            pltpu.VMEM((GROUP, 8, ROWS), f32),
            pltpu.VMEM((GROUP * BLK_DEV, ROWS, 128), bf16),
            pltpu.VMEM((GROUP * BLK_DEV, 16, ROWS), bf16),
            pltpu.SemaphoreType.DMA,
        ],
        compiler_params=params(28),
        cost_estimate=pl.CostEstimate(flops=32 * 10**9, bytes_accessed=10**7, transcendentals=16 * 10**6),
        name="remote_pull",
    )(visitors, *pms)


def node_sum(place, fields):
    mass, cx, cy, cz, qxx, qyy, qzz, qxy, qxz, qyz = fields
    x, y, z = place[0] - cx, place[1] - cy, place[2] - cz
    spread = x * x + y * y + (z * z + SOFTEN)
    quad_x = qxx * x + qxy * y + qxz * z
    quad_y = qxy * x + qyy * y + qyz * z
    quad_z = qxz * x + qyz * y + qzz * z
    root = lax.rsqrt(spread)
    inverse = root * root
    cubed = inverse * root
    fifth = cubed * inverse
    scalar = x * quad_x + y * quad_y + z * quad_z
    radial = mass * cubed + scalar * (fifth * (-2.5 * inverse))
    return radial * x + quad_x * fifth, radial * y + quad_y * fifth, radial * z + quad_z * fifth


NODE_PART = 16


def node_kernel(
    row_ref, part_ref, pm_ref, local_ref, *refs,
):
    half = BLK_DEV // 2
    share_refs, (out_ref, table_ref, weight_ref, spread_ref, gather_ref, nodes_ref) = refs[:GROUP], refs[GROUP : GROUP + 6]
    refs = refs[GROUP + 6 :]
    picked_refs, field_refs, place_refs, pull_refs = refs[0:2], refs[2:4], refs[4:6], refs[6:8]
    narrow = lax.axis_index("narrow")
    here = (narrow & 1) + ((narrow >> 2) & 1) * 2 + (lax.axis_index("wide") & 1) * 4
    devices, each = share_refs[0].shape[0], share_refs[0].shape[1]
    for distance, share_ref in enumerate(share_refs):
        first = pl.multiple_of((here ^ distance) * (devices * each), devices * each)
        for device in range(0, devices, 2):
            nodes_ref[pl.ds(first + device * each, 2 * each), :] = jnp.concatenate(
                [share_ref[device], share_ref[device + 1]], axis=0
            )
    fill_tables((pm_ref,), table_ref, weight_ref)
    left = left_lanes()

    row = lax.broadcasted_iota(jnp.int32, (ROWS, 128), 0)
    lane = lax.broadcasted_iota(jnp.int32, (ROWS, 128), 1)
    for along in range(3):
        inner = row & 63
        hit = (inner == along) | (inner == 16 + along) | (inner == 40 + along)
        hit = hit & ((row >> 6) == (lane >> 6))
        spread_ref[:, 128 * along : 128 * along + 128] = jnp.where(hit, -0.5, 0.0).astype(bf16)
        row16 = lax.broadcasted_iota(jnp.int32, (16, 256), 0)
        lane16 = lax.broadcasted_iota(jnp.int32, (16, 256), 1) & 127
        mine = row16 == along + 4 * (lane16 >> 6)
        gather_ref[along] = jnp.where(mine, 1.0, 0.0).astype(bf16)

    def pick(block, target, first, last):
        for node in range(first, last):
            target[pl.ds(node, 1), :] = nodes_ref[pl.ds(row_ref[block, node], 1), :]

    def lay_out(block, side):
        turned = picked_refs[side][...].T
        part = part_ref[pl.ds(block, 1), :]
        fields = turned[0:16]
        for number in range(1, 8):
            fields = jnp.where(part == number, turned[16 * number : 16 * number + 16], fields)
        centre = pm_ref[:, BLK_DEV * ROWS : BLK_DEV * ROWS + ROWS]
        rows = [-fields[0:1]] + [fields[k + 1 : k + 2] - centre[k : k + 1] for k in range(3)]
        rows += [fields[k : k + 1] for k in range(4, NODE_FIELDS)]
        for number, value in enumerate(rows):
            field_refs[side][number] = jnp.broadcast_to(value, (8, 128))
        both = jnp.where(left, table_ref[block], table_ref[block + half])
        place_refs[side][...] = dot(both, spread_ref[...])

    def compute(side, start):
        rows = [field_refs[side][number] for number in range(NODE_FIELDS)]
        halves = [
            node_sum([place_refs[side][at : at + 8, 128 * k : 128 * k + 128] for k in range(3)], rows)
            for at in range(start, start + NODE_PART, 8)
        ]
        for number in range(3):
            pull = jnp.concatenate([half_[number] for half_ in halves], axis=0)
            high = pull.astype(bf16)
            pull_refs[side][number, start : start + NODE_PART, 0:128] = high
            pull_refs[side][number, start : start + NODE_PART, 128:256] = (pull - high.astype(f32)).astype(bf16)

    def add_up(block, side):
        total = jnp.zeros((16, ROWS), f32)
        for number in range(3):
            total += lax.dot_general(
                gather_ref[number],
                pull_refs[side][number],
                (((1,), (1,)), ((), ())),
                preferred_element_type=f32,
            )
        out_ref[block, 0:3] = local_ref[block, 0:3] + total[0:3]
        out_ref[block + half, 0:3] = local_ref[block + half, 0:3] + total[4:7]

    pick(0, picked_refs[0], 0, 2 * LIST_N)
    pick(1, picked_refs[1], 0, 2 * LIST_N)
    lay_out(0, 0)

    def step(index, carry):
        for side in range(2):
            block = index * 2 + side
            other = 1 - side
            lay_out(jnp.minimum(block + 1, half - 1), other)
            add_up(jnp.maximum(block - 1, 0), other)
            ahead = jnp.minimum(block + 2, half - 1)
            for start in range(0, ROWS, NODE_PART):
                compute(side, start)
                pick(ahead, picked_refs[side], start, start + NODE_PART)
        return carry

    lax.fori_loop(0, half // 2, step, 0)
    add_up(half - 1, 1)


def node_pull(rows, parts, pm, local, shares):
    devices, each = shares[0].shape[0:2]
    return pl.pallas_call(
        node_kernel,
        out_shape=jax.ShapeDtypeStruct((BLK_DEV, 4, ROWS), f32),
        in_specs=[SMEM] + [VMEM] * (3 + GROUP),
        out_specs=VMEM,
        scratch_shapes=[
            pltpu.VMEM((BLK_DEV, ROWS, 128), bf16),
            pltpu.VMEM((BLK_DEV, 16, ROWS), bf16),
            pltpu.VMEM((ROWS, 3 * 128), bf16),
            pltpu.VMEM((3, 16, 256), bf16),
            pltpu.VMEM((GROUP * devices * each, 128), f32),
        ]
        + [pltpu.VMEM((2 * LIST_N, 128), f32)] * 2
        + [pltpu.VMEM((NODE_FIELDS, 8, 128), f32)] * 2
        + [pltpu.VMEM((ROWS, 3 * 128), f32)] * 2
        + [pltpu.VMEM((3, ROWS, 256), bf16)] * 2,
        compiler_params=params(14),
        cost_estimate=pl.CostEstimate(flops=12 * 10**9, bytes_accessed=4 * 10**6, transcendentals=10**6),
        name="node_pull",
    )(rows, parts, pm, local, *shares)


def local_kernel(leaf_ref, pm_ref, out_ref, table_ref, weight_ref):
    fill_tables((pm_ref,), table_ref, weight_ref)
    left = left_lanes()

    def step(index, carry):
        results = []
        for place in range(STEP):
            block = index * STEP + place
            start = pl.multiple_of(block * ROWS, ROWS)
            leaves = [leaf_ref[k, block] for k in range(LEAF_N)]
            moved = pm_ref[0:3, pl.ds(start, ROWS)] * -0.5
            results.append(pull_block(moved, leaves, table_ref, weight_ref, left))
        for place in range(STEP):
            out_ref[index * STEP + place, 0:3] = results[place]
        return carry

    lax.fori_loop(0, BLK_DEV // STEP, step, 0)


def local_pull(local_leaves, pm):
    return pl.pallas_call(
        local_kernel,
        out_shape=jax.ShapeDtypeStruct((BLK_DEV, 4, ROWS), f32),
        in_specs=[SMEM, VMEM],
        out_specs=VMEM,
        scratch_shapes=[
            pltpu.VMEM((BLK_DEV, ROWS, 128), bf16),
            pltpu.VMEM((BLK_DEV, 16, ROWS), bf16),
        ],
        compiler_params=params(10),
        cost_estimate=pl.CostEstimate(flops=16 * 10**9, bytes_accessed=10**6, transcendentals=8 * 10**6),
        name="local_pull",
    )(local_leaves, pm)


def add_kernel(slot_ref, own_ref, back_ref, out_ref, *sum_refs):
    parts = len(sum_refs)
    for part in range(1, parts):
        sum_refs[part][...] = jnp.zeros_like(sum_refs[part])
    sum_refs[0][...] = own_ref[...]

    def one(step, carry):
        for part in range(parts):
            export = step * parts + part
            block = slot_ref[EXP_BLK + export]
            sum_refs[part][block] += back_ref[slot_ref[export]]
        return carry

    lax.fori_loop(0, EXP_BLK // parts, one, 0)
    for block in range(BLK_DEV):
        total = sum_refs[0][block]
        for part in range(1, parts):
            total = total + sum_refs[part][block]
        out_ref[:, block * ROWS : (block + 1) * ROWS] = total[0:3]


def add_returned(slots, own, back):
    return pl.pallas_call(
        add_kernel,
        out_shape=jax.ShapeDtypeStruct((3, BLK_DEV * ROWS), f32),
        in_specs=[SMEM, VMEM, VMEM],
        out_specs=VMEM,
        scratch_shapes=[pltpu.VMEM((BLK_DEV, 4, ROWS), f32)] * 4,
        compiler_params=params(16),
        name="add_returned",
    )(slots, own, back)


def swap(values):
    return lax.all_to_all(values, AXES, split_axis=0, concat_axis=0, tiled=True)


def per_device(
    positions,
    masses,
    node_mass,
    node_centre,
    node_quad,
    local_leaves,
    node_lists,
    export_block,
    export_dest,
    export_leaves,
):
    groups = lax.axis_size("wide")
    members = lax.axis_size("narrow")
    devices = groups * members

    def same_core(value):
        flips = [[(i, i ^ flip) for i in range(members)] for flip in (1, 4, 5)]
        return [value] + [lax.ppermute(value, "narrow", flip) for flip in flips]

    def other_core(values):
        return values + [lax.ppermute(value, "wide", [(i, i ^ 1) for i in range(groups)]) for value in values]

    outgoing, slots, pm, rows, parts = send_blocks(
        devices,
        export_block,
        export_dest[:, 0],
        export_leaves.T,
        positions,
        masses[None],
        node_mass[None],
        node_centre,
        node_quad,
        node_lists,
    )
    arrived = swap(outgoing)
    pms = same_core(pm)
    local = local_pull(local_leaves.T, pm)
    arrived, local, pms = lax.optimization_barrier((arrived, local, pms))
    pms = other_core(pms)

    shares = same_core(arrived[:, CAP])
    visitors = arrived.reshape(devices * (CAP + 1), 4, ROWS)
    pulls = remote_pull(visitors, pms)
    pulls, local, shares = lax.optimization_barrier((pulls, local, shares))
    back = swap(pulls)
    shares = other_core(shares)
    own = node_pull(rows, parts, pm, local, shares)
    return add_returned(slots, own, back.reshape(devices * CAP, 4, ROWS))


def solution(mesh):
    both = P(AXES)
    lanes = P(None, AXES)
    rows = P(AXES, None)
    return jax.shard_map(
        per_device,
        mesh=mesh,
        in_specs=(lanes, both, both, lanes, lanes, rows, rows, both, rows, rows),
        out_specs=lanes,
        check_vma=False,
    )
```
